32 devices in a mesh: seq: 8 (over z, core), dp: 4 (over y, x).
Axes of the slice: x: 2, y: 2, z: 4, core: 2. Of those that a mesh axis runs over, the one named last changes fastest.
Arguments:
- inputs: bfloat16 [4, 1024, 2048], P('dp', 'seq'), may hold values from -6 to 6
- segments: int32 [4, 1024], P('dp'), may hold values from -1 to 2, as said below
- routes: int32 [4, 1024, 6], P('dp', 'seq'), may hold values from 0 to 15, all different within a row; in each aligned block of 128 rows (0 to 127, 128 to 255, ..., all dimensions but the last counted through in order) at most 96 rows name the same one
- cotangent: bfloat16 [4, 1024, 2048], P('dp', 'seq'), may hold values from -6 to 6
- attention_gain: bfloat16 [2048], P('dp'), may hold values from 0.5 to 1.5
- query_weight: bfloat16 [2048, 3072], P('dp'), may hold values from -0.25 to 0.25
- latent_weight: bfloat16 [2048, 576], P('dp'), may hold values from -0.125 to 0.125
- latent_gain: bfloat16 [512], P('dp'), may hold values from 0.5 to 1.5
- expand_weight: bfloat16 [512, 4096], P('dp'), may hold values from -0.25 to 0.25
- output_weight: bfloat16 [2048, 2048], P('dp'), may hold values from -1.5 to 1.5
- feedforward_gain: bfloat16 [2048], P('dp'), may hold values from 0.5 to 1.5
- router_weight: bfloat16 [2048, 16], P('dp'), may hold values from -0.0625 to 0.0625
- shared_gate: bfloat16 [2048, 2816], P('dp'), may hold values from -0.125 to 0.125
- shared_up: bfloat16 [2048, 2816], P('dp'), may hold values from -0.125 to 0.125
- shared_down: bfloat16 [2816, 2048], P('dp'), may hold values from -0.109375 to 0.109375
- expert_gate: bfloat16 [16, 2048, 1408], P('seq', 'dp'), may hold values from -0.125 to 0.125
- expert_up: bfloat16 [16, 2048, 1408], P('seq', 'dp'), may hold values from -0.125 to 0.125
- expert_down: bfloat16 [16, 1408, 2048], P('seq', None, 'dp'), may hold values from -0.625 to 0.625
Outputs:
- layer_out: bfloat16 [4, 1024, 2048], P('dp', 'seq')
- grad_inputs: float32 [4, 1024, 2048], P('dp', 'seq')
- grad_attention_gain: float32 [2048], P('dp')
- grad_query_weight: float32 [2048, 3072], P('dp')
- grad_latent_weight: float32 [2048, 576], P('dp')
- grad_latent_gain: float32 [512], P('dp')
- grad_expand_weight: float32 [512, 4096], P('dp')
- grad_output_weight: float32 [2048, 2048], P('dp')
- grad_feedforward_gain: float32 [2048], P('dp')
- grad_router_weight: float32 [2048, 16], P('dp')
- grad_shared_gate: float32 [2048, 2816], P('dp')
- grad_shared_up: float32 [2048, 2816], P('dp')
- grad_shared_down: float32 [2816, 2048], P('dp')
- grad_expert_gate: float32 [16, 2048, 1408], P('seq', 'dp')
- grad_expert_up: float32 [16, 2048, 1408], P('seq', 'dp')
- grad_expert_down: float32 [16, 1408, 2048], P('seq', None, 'dp')
The draws below stay inside these ranges and needn't reach their ends.
Inputs may be any that keep to these rules, and one draw needn't show every extreme that they name: `segments`: in each group ids never fall except that its last 1 to 32 positions are -1; document 1 begins within the group's first 128 positions and ends within its last 128. `routes`: each row names 6 different experts; in the rows of one device no expert is named by more than 96 rows, a bound that some block reaches.
All inputs are finite; a program needn't handle non-finite values.
Results may differ from the reference program's by a relative error of at most 0.024.
Values may be sent and summed in bfloat16 or wider, within the bound.
A program may use at most 448 MiB of HBM per device.

```python
import math
import jax
import jax.numpy as jnp
import numpy as np
from jax import lax

D = 2048
HEADS = 16
NOPE = 128
ROPE = 64
VDIM = 128
KV_RANK = 512
FFE = 1408
TOP = 6
TOK_DEV = 128
SHARED = 2816
EXPERTS = 16
GROUP = 1024
GROUPS = 4
MOST = 96
CAP = 480


def draw_segments(key, part):
    key = jax.random.fold_in(key, 11)
    first_key, second_key, third_key = jax.random.split(key, 3)
    opening = jax.random.randint(first_key, (GROUPS, 1), 1, TOK_DEV)
    closing = jax.random.randint(second_key, (GROUPS, 1), GROUP - TOK_DEV + 1, GROUP - TOK_DEV // 2)
    padding = jax.random.randint(third_key, (GROUPS, 1), 1, TOK_DEV // 4 + 1)
    positions = jnp.arange(GROUP, dtype=jnp.int32)[None, :]
    doc_ids = (positions >= opening).astype(jnp.int32) + (positions >= closing).astype(jnp.int32)
    return jnp.where(positions >= GROUP - padding, -1, doc_ids).astype(jnp.int32)


def block_scale(rng, dims, pieces, least, largest):
    def one(axis_at, shards_of):
        heights = jax.random.uniform(jax.random.fold_in(jax.random.fold_in(rng, 6), axis_at), (shards_of,), jnp.float32, least / len(pieces), largest / len(pieces))
        return jnp.repeat(jnp.exp(heights), dims[axis_at] // shards_of).reshape((-1,) + (1,) * (len(dims) - axis_at - 1))

    loudness = one(*pieces[0])
    for cut in pieces[1:]:
        loudness = loudness * one(*cut)
    return loudness


def shared_out(key, own, number, rows, count, top, most, slope):
    ranking = jax.random.permutation(key, count)
    heavy_load, usual = portions_of(count, rows * top, most, slope, True), portions_of(count, rows * top, most, slope, False)
    places = jnp.arange(count)

    def named(tallies, offset_by):
        used = int((tallies > 0).sum())
        fixed = max(1, used // 4)
        passed = fixed + (places - fixed + offset_by * (used - fixed)) % max(1, count - fixed)
        return jnp.zeros((count,), jnp.int32).at[ranking[jnp.where(places < fixed, places, passed)]].set(jnp.asarray(tallies, jnp.int32))

    tallies = jnp.where(number % 4 == 0, named(heavy_load, number // 4), named(usual, number - number // 4 - 1))
    mixed = jax.random.permutation(jax.random.fold_in(own, 3), count)
    donor, taker = mixed[0:count // 2 * 2:2], mixed[1:count // 2 * 2:2]
    room = jnp.minimum(tallies[donor] - 1, most - tallies[taker]) // 2
    room = jnp.where((donor == ranking[0]) | (taker == ranking[0]) | (tallies[taker] == 0), 0, jnp.maximum(room, 0))
    passed = jax.random.randint(jax.random.fold_in(own, 4), (count // 2,), 0, 1 << 20) % (room + 1)
    tallies = tallies.at[donor].add(-passed).at[taker].add(passed)
    items = jnp.searchsorted(jnp.cumsum(tallies), jnp.arange(rows * top), side="right").astype(jnp.int32)
    listing = items.reshape(top, rows).T
    listing = listing[jax.random.permutation(jax.random.fold_in(own, 1), rows)]
    offset_by = jax.random.randint(jax.random.fold_in(own, 2), (rows, 1), 0, top)
    return jnp.take_along_axis(listing, (jnp.arange(top)[None, :] + offset_by) % top, axis=1)


def portions_of(count, total, reach, skew, full):
    loads = [(1 << 20) // math.isqrt(rank ** skew) + 1 for rank in range(1, count + 1)]
    largest = reach if full else min(reach, max(-(-total // count), total * loads[0] // sum(loads)))
    least = 1 if total - largest >= count - 1 else 0
    given, rest = [largest] + [least] * (count - 1), total - largest - least * (count - 1)
    while rest > 0:
        candidates = [i for i in range(1, count) if given[i] < largest] or [i for i in range(1, count) if given[i] < reach]
        pool, remaining = sum([loads[i] for i in candidates]), rest
        for i in candidates:
            more = min(reach - given[i], max(1, remaining * loads[i] // pool), rest)
            given[i] = given[i] + more
            rest = rest - more
    return np.array(given)


def centred(own_key, extent, scale, most, shards=(), kind=jnp.bfloat16):
    array = jax.random.normal(own_key, extent, jnp.float32) * scale
    if len(shards) > 0:
        array = block_scale(own_key, extent, shards, -0.22, 0.18) * array
    return jnp.clip(array, min=-most, max=most).astype(kind)


def setup_inputs(seed: int = 0) -> dict:
    splits = jax.random.split(jax.random.key(seed), 19)
    inputs = centred(splits[0], (GROUPS, GROUP, D), 1.0, 6.0, ((0, 4), (1, 8)))
    segments = draw_segments(jax.random.fold_in(splits[18], 71), 0)
    routes_keys = jax.random.split(jax.random.fold_in(splits[2], 1), GROUPS * GROUP // TOK_DEV)
    routes_turns = jax.random.permutation(jax.random.fold_in(splits[2], 3), GROUPS * GROUP // TOK_DEV)
    routes = jax.vmap(lambda own, number: shared_out(jax.random.fold_in(splits[2], 2), own, number, TOK_DEV, EXPERTS, TOP, MOST, 1))(routes_keys, routes_turns).reshape((GROUPS, GROUP, TOP))
    cotangent = centred(splits[3], (GROUPS, GROUP, D), 1.0, 6.0, ((0, 4), (1, 8)))
    attention_gain = jnp.clip(1.0 + 0.1 * jax.random.normal(splits[4], (D,), jnp.float32), 0.5, 1.5).astype(jnp.bfloat16)
    query_weight = centred(splits[5], (D, HEADS * (NOPE + ROPE)), (D // 4) ** -0.5, 0.25, ((0, 4),))
    latent_weight = centred(splits[6], (D, KV_RANK + ROPE), D ** -0.5, 0.125, ((0, 4),))
    latent_gain = jnp.clip(1.0 + 0.1 * jax.random.normal(splits[7], (KV_RANK,), jnp.float32), 0.5, 1.5).astype(jnp.bfloat16)
    expand_weight = centred(splits[8], (KV_RANK, HEADS * (NOPE + VDIM)), KV_RANK ** -0.5, 0.25, ((0, 4),))
    output_weight = centred(splits[9], (HEADS * VDIM, D), HEADS ** -0.5, 1.5, ((0, 4),))
    feedforward_gain = jnp.clip(1.0 + 0.1 * jax.random.normal(splits[10], (D,), jnp.float32), 0.5, 1.5).astype(jnp.bfloat16)
    router_weight = centred(splits[11], (D, EXPERTS), (4 * D) ** -0.5, 0.0625, ((0, 4),))
    shared_gate = centred(splits[12], (D, SHARED), D ** -0.5, 0.125, ((0, 4),))
    shared_up = centred(splits[13], (D, SHARED), D ** -0.5, 0.125, ((0, 4),))
    shared_down = centred(splits[14], (SHARED, D), SHARED ** -0.5, 0.109375, ((0, 4),))
    expert_gate = centred(splits[15], (EXPERTS, D, FFE), D ** -0.5, 0.125, ((0, 8), (1, 4)))
    expert_up = centred(splits[16], (EXPERTS, D, FFE), D ** -0.5, 0.125, ((0, 8), (1, 4)))
    expert_down = centred(splits[17], (EXPERTS, FFE, D), (FFE // 16) ** -0.5, 0.625, ((0, 8), (2, 4)))
    return {"inputs": inputs, "segments": segments, "routes": routes, "cotangent": cotangent, "attention_gain": attention_gain, "query_weight": query_weight, "latent_weight": latent_weight, "latent_gain": latent_gain, "expand_weight": expand_weight, "output_weight": output_weight, "feedforward_gain": feedforward_gain, "router_weight": router_weight, "shared_gate": shared_gate, "shared_up": shared_up, "shared_down": shared_down, "expert_gate": expert_gate, "expert_up": expert_up, "expert_down": expert_down}


@jax.custom_vjp
def low(v):
    return lax.optimization_barrier(v.astype(jnp.bfloat16)).astype(jnp.float32)

@jax.custom_vjp
def low_back(v):
    return v

def low_keep(v):
    return (low(v), None)

def low_pass(kept, grad):
    return (grad,)

def back_keep(v):
    return (v, None)

def back_low(kept, grad):
    return (low(grad),)
low.defvjp(low_keep, low_pass)
low_back.defvjp(back_keep, back_low)
HIGHEST = lax.Precision.HIGHEST
EPSILON = 1e-06
MASKED = -1e+30

def matmul(left, right):
    return jnp.dot(left, right, precision=HIGHEST)

def normalized_rows(values, gain):
    return values * lax.rsqrt(lax.optimization_barrier(jnp.mean(values * values, axis=-1, keepdims=True)) + EPSILON) * gain

def angles(positions):
    frequency = 10000.0 ** (-(2.0 * jnp.arange(ROPE // 2, dtype=jnp.float32)) / ROPE)
    turned = positions.astype(jnp.float32)[:, None] * frequency[None, :]
    return (jnp.cos(turned), jnp.sin(turned))

def rotate(values, cosine, sine):
    half_width = values.shape[-1] // 2
    lower_half = values[..., :half_width]
    upper_half = values[..., half_width:]
    return jnp.concatenate([lower_half * cosine - upper_half * sine, upper_half * cosine + lower_half * sine], axis=-1)

def experts_mix(ffn_in, route_ids, route_gates, expert_gate, expert_up, expert_down):
    pair_count = GROUP * TOP
    flat_route = route_ids.reshape(pair_count)
    pair_hot = (flat_route[:, None] == jnp.arange(EXPERTS, dtype=jnp.int32)[None, :]).astype(jnp.int32)
    pair_slot = lax.optimization_barrier(jnp.sum((jnp.cumsum(pair_hot, axis=0) - 1) * pair_hot, axis=1))
    kept_mask = pair_slot < CAP
    slot_index = jnp.where(kept_mask, flat_route * CAP + pair_slot, EXPERTS * CAP).astype(jnp.int32)
    slot_table = jnp.full((EXPERTS * CAP,), pair_count, jnp.int32).at[slot_index].set(jnp.arange(pair_count, dtype=jnp.int32), mode='drop')
    pair_in = low_back(jnp.repeat(ffn_in, TOP, axis=0))
    padded = jnp.concatenate([pair_in, jnp.zeros((1, D), pair_in.dtype)], axis=0)
    expert_input_rows = padded[slot_table].reshape(EXPERTS, CAP, D)
    hidden_gate = low_back(jnp.einsum('ecd,edf->ecf', expert_input_rows, expert_gate, precision=HIGHEST))
    hidden_up_rows = low_back(jnp.einsum('ecd,edf->ecf', expert_input_rows, expert_up, precision=HIGHEST))
    expert_act = low(jax.nn.silu(hidden_gate) * hidden_up_rows)
    expert_out = low(low_back(jnp.einsum('ecf,efd->ecd', expert_act, expert_down, precision=HIGHEST)))
    flat_out = jnp.concatenate([expert_out.reshape(EXPERTS * CAP, D), jnp.zeros((1, D), expert_out.dtype)], axis=0)
    pair_out = flat_out[slot_index].reshape(GROUP, TOP, D)
    return lax.optimization_barrier(jnp.sum(pair_out * route_gates[:, :, None], axis=1))

def block_layer(params, group_in, group_segments, route_ids):
    attention_gain, query_weight, latent_weight, latent_gain, expand_weight, output_weight, feedforward_gain, router_weight, shared_gate, shared_up, shared_down, expert_gate, expert_up, expert_down = params
    qk_width = NOPE + ROPE
    positions = jnp.arange(GROUP, dtype=jnp.int32)
    cosine, sine = angles(positions)
    attn_in = low(normalized_rows(group_in, attention_gain))
    q_raw = low_back(matmul(attn_in, query_weight)).reshape(GROUP, HEADS, qk_width)
    latent_raw = low_back(matmul(attn_in, latent_weight))
    latent = latent_raw[:, :KV_RANK]
    k_pe = latent_raw[:, KV_RANK:]
    latent_normed = low(normalized_rows(latent, latent_gain))
    key_value = matmul(latent_normed, expand_weight).reshape(GROUP, HEADS, NOPE + VDIM)
    q_full = low(low_back(jnp.concatenate([q_raw[..., :NOPE], rotate(q_raw[..., NOPE:], cosine[:, None, :], sine[:, None, :])], axis=-1)))
    k_rot = rotate(k_pe, cosine, sine)
    k_full = low(low_back(jnp.concatenate([key_value[..., :NOPE], jnp.broadcast_to(k_rot[:, None, :], (GROUP, HEADS, ROPE))], axis=-1)))
    values = low(low_back(key_value[..., NOPE:]))
    block_rows = min(512, GROUP)
    block_count = GROUP // block_rows
    score_scale = 1.0 / math.sqrt(qk_width)

    def attend(block_args):
        query_block, seg_query, pos_query = block_args
        raw_scores = jnp.einsum('qhd,khd->hqk', query_block, k_full, precision=HIGHEST) * score_scale
        scores = low_back(raw_scores)
        visible = (seg_query[:, None] == group_segments[None, :]) & (seg_query[:, None] >= 0) & (positions[None, :] <= pos_query[:, None]) | (positions[None, :] == pos_query[:, None])
        scores = jnp.where(visible[None], scores, MASKED)
        row_peak = lax.optimization_barrier(jnp.max(scores, axis=-1, keepdims=True))
        exponent = jnp.exp(scores - row_peak)
        probs = low(exponent / lax.optimization_barrier(jnp.sum(exponent, axis=-1, keepdims=True)))
        return jnp.einsum('hqk,khd->qhd', probs, values, precision=HIGHEST)
    attended = lax.map(jax.checkpoint(attend), (q_full.reshape(block_count, block_rows, HEADS, qk_width), group_segments.reshape(block_count, block_rows), positions.reshape(block_count, block_rows)))
    head_out = low(low_back(attended.reshape(GROUP, HEADS * VDIM)))
    attn_out = low_back(matmul(head_out, output_weight))
    residual = group_in + attn_out
    ffn_in = low(normalized_rows(residual, feedforward_gain))
    router_probs = jax.nn.softmax(matmul(ffn_in, router_weight), axis=-1)
    route_hot = (route_ids[:, :, None] == jnp.arange(EXPERTS, dtype=jnp.int32)[None, None, :]).astype(jnp.float32)
    chosen = jnp.einsum('tje,te->tj', route_hot, router_probs, precision=HIGHEST)
    route_gates = chosen / lax.optimization_barrier(jnp.sum(chosen, axis=-1, keepdims=True))
    mixture_experts_output = experts_mix(ffn_in, route_ids, route_gates, expert_gate, expert_up, expert_down)
    side_gate = low_back(matmul(ffn_in, shared_gate))
    side_up = low_back(matmul(ffn_in, shared_up))
    side_act = low(jax.nn.silu(side_gate) * side_up)
    side_out = low_back(matmul(side_act, shared_down))
    return residual + side_out + mixture_experts_output

def reference(inputs, segments, routes, cotangent, attention_gain, query_weight, latent_weight, latent_gain, expand_weight, output_weight, feedforward_gain, router_weight, shared_gate, shared_up, shared_down, expert_gate, expert_up, expert_down):
    weights = tuple((weight.astype(jnp.float32) for weight in (attention_gain, query_weight, latent_weight, latent_gain, expand_weight, output_weight, feedforward_gain, router_weight, shared_gate, shared_up, shared_down, expert_gate, expert_up, expert_down)))

    def forward(whole_input, *params):

        def one_group(group_args):
            return block_layer(params, group_args[0], group_args[1], group_args[2])
        return lax.map(jax.checkpoint(one_group), (whole_input, segments, routes))
    layer_out, pullback = jax.vjp(forward, inputs.astype(jnp.float32), *weights)
    grads = pullback(cotangent.astype(jnp.float32))
    return (layer_out.astype(jnp.bfloat16), grads[0], grads[1], grads[2], grads[3], grads[4], grads[5], grads[6], grads[7], grads[8], grads[9], grads[10], grads[11], grads[12], grads[13], grads[14])
```

```python
import math

import jax
import jax.numpy as jnp
from jax import lax
from jax.sharding import PartitionSpec as P

HEADS = 16
NOPE = 128
ROPE = 64
VDIM = 128
KV_RANK = 512
TOP = 6
EXP_DEV = 2
CAP = 480

EPSILON = 1e-06
MASKED = -1e30
HIGHEST = lax.Precision.HIGHEST
F32 = jnp.float32
BF16 = jnp.bfloat16
QK = NOPE + ROPE


def normalized_rows(values, gain):
    return values * lax.rsqrt(jnp.mean(values * values, axis=-1, keepdims=True) + EPSILON) * gain


def norm_backward(values, gain, upstream):
    scale = lax.rsqrt(jnp.mean(values * values, axis=-1, keepdims=True) + EPSILON)
    normed = values * scale
    weighted = upstream * gain
    d_values = scale * (weighted - normed * jnp.mean(weighted * normed, axis=-1, keepdims=True))
    return d_values, jnp.sum(upstream * normed, axis=0)


def angles(positions, width):
    frequency = 10000.0 ** (-(2.0 * jnp.arange(width // 2, dtype=F32)) / width)
    turned = positions.astype(F32)[:, None] * frequency[None, :]
    return (jnp.cos(turned), jnp.sin(turned))


def rotate(values, cosine, sine):
    half_width = values.shape[-1] // 2
    lower_half = values[..., :half_width]
    upper_half = values[..., half_width:]
    return jnp.concatenate(
        [lower_half * cosine - upper_half * sine, upper_half * cosine + lower_half * sine], axis=-1
    )


def swiglu(gate_portion, up_part):
    return jax.nn.silu(gate_portion) * up_part


def dot(left, right):
    return jnp.dot(left, right, preferred_element_type=F32)


def dot_t(left, right):
    return lax.dot_general(left, right, (((1,), (1,)), ((), ())), preferred_element_type=F32)


def t_dot(left, right):
    return lax.dot_general(left, right, (((0,), (0,)), ((), ())), preferred_element_type=F32)


def swap(value, axis, mask):
    count = lax.axis_size(axis)
    return lax.ppermute(value, axis, [(i, i ^ mask) for i in range(count)])


def flip_blocks(value, index, bit, axis):
    shape = value.shape
    count = shape[axis]
    step = 1 << bit
    split = value.reshape(shape[:axis] + (count // (2 * step), 2, step) + shape[axis + 1 :])
    flipped = jnp.flip(split, axis + 1).reshape(shape)
    return jnp.where(((index >> bit) & 1) == 1, flipped, value)


def xor_order(value, index, axis):
    for bit in range(value.shape[axis].bit_length() - 1):
        value = flip_blocks(value, index, bit, axis)
    return value


def to_own_order(value, me):
    count = value.shape[0]
    pairs = xor_order(value, me, 0).reshape((count // 2, 2) + value.shape[1:])
    return jnp.swapaxes(pairs, 0, 1).reshape(value.shape)


def from_own_order(value, me):
    count = value.shape[0]
    pairs = jnp.swapaxes(value.reshape((2, count // 2) + value.shape[1:]), 0, 1)
    return xor_order(pairs.reshape(value.shape), me, 0)


def own_masks():
    chips = lax.axis_size("seq") // 2
    return [2 * k + c for c in range(2) for k in range(chips)]


def gather_seq(block):
    chips = lax.axis_size("seq") // 2
    half = jnp.concatenate([block] + [swap(block, "seq", 2 * k) for k in range(1, chips)], axis=0)
    return jnp.concatenate([half, swap(half, "seq", 1)], axis=0)


def scatter_seq(partial):
    chips = lax.axis_size("seq") // 2
    half = partial.shape[0] // 2
    tokens = half // chips
    mine = partial.astype(BF16)
    peer = swap(mine[half:], "seq", 1)
    total = mine[:half].astype(F32) + peer.astype(F32)
    sent = total.astype(BF16)
    result = total[:tokens]
    for k in range(1, chips):
        result = result + swap(sent[k * tokens : (k + 1) * tokens], "seq", 2 * k).astype(F32)
    return result


def exchange_seq(blocks):
    return jnp.stack(
        [blocks[r] if m == 0 else swap(blocks[r], "seq", m) for r, m in enumerate(own_masks())]
    )


def gather_dp(value, axis):
    return lax.all_gather(value, "dp", axis=axis, tiled=True)


def reduce_dp(value, axis):
    return lax.psum_scatter(value.astype(BF16), "dp", scatter_dimension=axis, tiled=True)


def token_gradient(rows_in, upstream, d_rank):
    parts = lax.axis_size("dp")
    width = rows_in.shape[1] // parts
    lefts, rights = [], []
    for p in range(parts):
        piece = lax.dynamic_slice_in_dim(rows_in, (d_rank ^ p) * width, width, 1)
        lefts.append(piece if p == 0 else swap(piece, "dp", p))
        rights.append(upstream if p == 0 else swap(upstream, "dp", p))
    partial = t_dot(jnp.concatenate(lefts, axis=0), jnp.concatenate(rights, axis=0))
    return lax.psum(partial.astype(BF16), "seq").astype(F32)


def local(
    inputs,
    segments,
    routes,
    cotangent,
    attention_gain,
    query_weight,
    latent_weight,
    latent_gain,
    expand_weight,
    output_weight,
    feedforward_gain,
    router_weight,
    shared_gate,
    shared_up,
    shared_down,
    expert_gate,
    expert_up,
    expert_down,
):
    seq_count = lax.axis_size("seq")
    dp_count = lax.axis_size("dp")
    me = lax.axis_index("seq")
    d_rank = lax.axis_index("dp")
    tokens = inputs.shape[1]
    width = inputs.shape[2]
    group = tokens * seq_count
    experts = EXP_DEV * seq_count
    heads_dev = HEADS // seq_count
    score_scale = 1.0 / math.sqrt(QK)
    shard = width // dp_count

    small = gather_dp(
        jnp.concatenate(
            [attention_gain, feedforward_gain, latent_gain, router_weight.reshape(-1)]
        ).reshape(1, -1),
        0,
    )
    g_attn = small[:, :shard].reshape(width).astype(F32)
    g_ffn = small[:, shard : 2 * shard].reshape(width).astype(F32)
    rank_shard = latent_gain.shape[0]
    g_latent = small[:, 2 * shard : 2 * shard + rank_shard].reshape(KV_RANK).astype(F32)
    w_router = small[:, 2 * shard + rank_shard :].reshape(width, experts)

    hq = heads_dev * QK
    hkv = heads_dev * (NOPE + VDIM)
    x_all = gather_seq(inputs[0])
    w_query = gather_dp(lax.dynamic_slice_in_dim(query_weight, me * hq, hq, 1), 0)
    w_latent = gather_dp(latent_weight, 0)
    w_expand = gather_dp(lax.dynamic_slice_in_dim(expand_weight, me * hkv, hkv, 1), 0)
    core = me & 1
    out_half = output_weight.shape[0] // 2
    out_mine = gather_dp(
        lax.dynamic_slice_in_dim(output_weight, core * out_half, out_half, 0)[None], 0
    )
    out_peer = swap(out_mine, "seq", 1)
    w_output = jnp.where(
        core == 0,
        jnp.stack([out_mine, out_peer], axis=1),
        jnp.stack([out_peer, out_mine], axis=1),
    ).reshape(width, width)

    g_all = gather_seq(cotangent[0])
    w_egate = gather_dp(expert_gate, 1)
    w_eup = gather_dp(expert_up, 1)
    w_edown = gather_dp(expert_down, 2)
    hidden = shared_gate.shape[1]
    unit = hidden // (dp_count * seq_count)

    def columns_of(weight):
        split = weight.reshape(weight.shape[0], dp_count, seq_count, unit)
        mine = lax.dynamic_index_in_dim(split, me, 2, keepdims=False)
        return mine.reshape(weight.shape[0], dp_count * unit)

    w_sgate = gather_dp(columns_of(shared_gate), 0)
    w_sup = gather_dp(columns_of(shared_up), 0)
    w_sdown = gather_dp(
        lax.dynamic_slice_in_dim(shared_down, me * unit, unit, 0)[None], 0
    ).reshape(dp_count * unit, width)

    ranks = me ^ jnp.array(own_masks(), jnp.int32)
    positions = (ranks[:, None] * tokens + jnp.arange(tokens, dtype=jnp.int32)[None, :]).reshape(
        group
    )
    seg_all = to_own_order(segments[0].reshape(seq_count, tokens), me).reshape(group)
    cosine, sine = angles(positions, ROPE)
    routes_abs = lax.all_gather(routes[0], "seq", axis=0, tiled=True)
    my_experts = me * EXP_DEV + jnp.arange(EXP_DEV, dtype=jnp.int32)
    hit_abs = jnp.any(routes_abs[None] == my_experts[:, None, None], axis=-1).astype(jnp.int32)
    slot_abs = jnp.where(hit_abs == 1, jnp.cumsum(hit_abs, axis=1) - hit_abs, CAP)
    slot_own = jnp.swapaxes(
        to_own_order(jnp.swapaxes(slot_abs.reshape(EXP_DEV, seq_count, tokens), 0, 1), me), 0, 1
    ).reshape(EXP_DEV, group)
    routes_own = to_own_order(routes_abs.reshape(seq_count, tokens, TOP), me).reshape(group, TOP)
    expert_ids = jnp.arange(experts, dtype=jnp.int32)
    route_hot = jnp.any(routes_own[:, :, None] == expert_ids[None, None, :], axis=1)
    placed = slot_own[:, None, :] == jnp.arange(CAP, dtype=jnp.int32)[None, :, None]
    dispatch = placed.astype(BF16).reshape(EXP_DEV * CAP, group)

    attn_in = normalized_rows(x_all.astype(F32), g_attn).astype(BF16)
    q_raw = dot(attn_in, w_query).reshape(group, heads_dev, QK)
    latent_raw = dot(attn_in, w_latent)
    latent = latent_raw[:, :KV_RANK]
    latent_normed = normalized_rows(latent, g_latent).astype(BF16)
    key_value = dot(latent_normed, w_expand).reshape(group, heads_dev, NOPE + VDIM)
    q_full = jnp.concatenate(
        [q_raw[..., :NOPE], rotate(q_raw[..., NOPE:], cosine[:, None, :], sine[:, None, :])],
        axis=-1,
    ).astype(BF16)
    k_rot = rotate(latent_raw[:, KV_RANK:], cosine, sine)
    k_full = jnp.concatenate(
        [key_value[..., :NOPE], jnp.broadcast_to(k_rot[:, None, :], (group, heads_dev, ROPE))],
        axis=-1,
    ).astype(BF16)
    values = key_value[..., NOPE:].astype(BF16)
    visible = (seg_all[:, None] == seg_all[None, :]) & (seg_all[:, None] >= 0) & (
        positions[None, :] <= positions[:, None]
    ) | (positions[None, :] == positions[:, None])
    scores = jnp.einsum("qhd,khd->hqk", q_full, k_full, preferred_element_type=F32) * score_scale
    scores = jnp.where(visible[None], scores, MASKED)
    row_peak = jnp.max(scores, axis=-1, keepdims=True)
    exponent = jnp.exp(scores - row_peak)
    soft_float = exponent / jnp.sum(exponent, axis=-1, keepdims=True)
    soft = soft_float.astype(BF16)
    head_out = jnp.einsum("hqk,khd->qhd", soft, values, preferred_element_type=F32)
    head_out = head_out.astype(BF16).reshape(seq_count, tokens, heads_dev * VDIM)
    flat_out = jnp.swapaxes(from_own_order(exchange_seq(head_out), me), 0, 1).reshape(
        tokens, HEADS * VDIM
    )
    x_float = inputs[0].astype(F32)
    residual = x_float + dot(flat_out, w_output)
    ffn_in = normalized_rows(residual, g_ffn).astype(BF16)
    ffn_all = gather_seq(ffn_in)

    router_probs = jax.nn.softmax(dot(ffn_all, w_router), axis=-1)
    chosen = jnp.where(route_hot, router_probs, 0.0)
    chosen_sum = jnp.sum(chosen, axis=-1, keepdims=True)
    gates = chosen / chosen_sum
    my_gates = lax.dynamic_slice_in_dim(gates.T, me * EXP_DEV, EXP_DEV, 0)
    gate_rows = jnp.sum(jnp.where(placed, my_gates[:, None, :], 0.0), axis=-1)

    rows_shape = (EXP_DEV, CAP, width)
    expert_in = dot(dispatch, ffn_all).astype(BF16).reshape(rows_shape)
    grad_rows = dot(dispatch, g_all).reshape(rows_shape)
    expert_grad = (gate_rows[:, :, None] * grad_rows).astype(BF16)
    hidden_gate = jnp.einsum("nmh,nhq->nmq", expert_in, w_egate, preferred_element_type=F32)
    hidden_up = jnp.einsum("nmh,nhq->nmq", expert_in, w_eup, preferred_element_type=F32)
    expert_act = swiglu(hidden_gate, hidden_up).astype(BF16)
    expert_out = jnp.einsum(
        "kcf,kfd->kcd", expert_act, w_edown, preferred_element_type=F32
    ).astype(BF16).astype(F32)
    d_gate_rows = jnp.sum(expert_out * grad_rows, axis=-1)
    moe_rows = (gate_rows[:, :, None] * expert_out).astype(BF16).reshape(EXP_DEV * CAP, width)

    side_gate = dot(ffn_all, w_sgate)
    side_up = dot(ffn_all, w_sup)
    side_act = swiglu(side_gate, side_up).astype(BF16)
    ffn_out = scatter_seq(dot(side_act, w_sdown) + t_dot(dispatch, moe_rows))
    layer_out = (residual + ffn_out).astype(BF16)

    grad_sdown = t_dot(side_act, g_all)
    d_side_act = dot_t(g_all, w_sdown)
    _, side_pull = jax.vjp(swiglu, side_gate, side_up)
    d_side_gate, d_side_up = side_pull(d_side_act)
    d_side_gate = d_side_gate.astype(BF16)
    d_side_up = d_side_up.astype(BF16)
    grad_sgate = t_dot(ffn_all, d_side_gate)
    grad_sup = t_dot(ffn_all, d_side_up)

    d_act = jnp.einsum("kcd,kfd->kcf", expert_grad, w_edown, preferred_element_type=F32)
    _, expert_pull = jax.vjp(swiglu, hidden_gate, hidden_up)
    d_hidden_gate, d_hidden_up = expert_pull(d_act)
    d_hidden_gate = d_hidden_gate.astype(BF16)
    d_hidden_up = d_hidden_up.astype(BF16)
    d_expert_in = (
        jnp.einsum("sta,sra->str", d_hidden_gate, w_egate, preferred_element_type=F32)
        + jnp.einsum("sta,sra->str", d_hidden_up, w_eup, preferred_element_type=F32)
    ).astype(BF16)
    d_ffn_partial = (
        dot_t(d_side_gate, w_sgate)
        + dot_t(d_side_up, w_sup)
        + t_dot(dispatch, d_expert_in.reshape(EXP_DEV * CAP, width))
    )
    d_ffn = scatter_seq(d_ffn_partial)
    grad_edown = jnp.einsum("kcf,kcd->kfd", expert_act, expert_grad, preferred_element_type=F32)
    grad_egate = jnp.einsum("kcd,kcf->kdf", expert_in, d_hidden_gate, preferred_element_type=F32)
    grad_eup = jnp.einsum("kcd,kcf->kdf", expert_in, d_hidden_up, preferred_element_type=F32)

    d_gate_own = jnp.sum(jnp.where(placed, d_gate_rows[:, :, None], 0.0), axis=1)
    d_gate_abs = from_own_order(
        jnp.swapaxes(d_gate_own.reshape(EXP_DEV, seq_count, tokens), 0, 1), me
    )
    d_gate_all = lax.all_gather(d_gate_abs, "seq", axis=0, tiled=False)
    d_gate = lax.dynamic_index_in_dim(d_gate_all, me, 1, keepdims=False).reshape(experts, tokens).T
    own_hot = route_hot[:tokens]
    own_probs = router_probs[:tokens]
    own_gates = gates[:tokens]
    d_chosen = (d_gate - jnp.sum(d_gate * own_gates, axis=-1, keepdims=True)) / chosen_sum[:tokens]
    d_probs = jnp.where(own_hot, d_chosen, 0.0)
    d_logits = own_probs * (d_probs - jnp.sum(own_probs * d_probs, axis=-1, keepdims=True))
    grad_router = jnp.einsum("td,te->de", ffn_in.astype(F32), d_logits, precision=HIGHEST)
    d_ffn = d_ffn + jnp.einsum("te,de->td", d_logits, w_router.astype(F32), precision=HIGHEST)

    grad_out = cotangent[0].astype(F32)
    d_resid_part, grad_ffn_gain = norm_backward(residual, g_ffn, d_ffn)
    d_residual = grad_out + d_resid_part
    d_attn = d_residual.astype(BF16)
    d_head = dot_t(d_attn, w_output).astype(BF16)
    d_head_blocks = jnp.swapaxes(d_head.reshape(tokens, seq_count, heads_dev * VDIM), 0, 1)
    head_grad = exchange_seq(to_own_order(d_head_blocks, me)).reshape(group, heads_dev, VDIM)

    d_values = jnp.einsum("hqk,qhd->khd", soft, head_grad, preferred_element_type=F32).astype(BF16)
    d_prob = jnp.einsum("qhd,khd->hqk", head_grad, values, preferred_element_type=F32)
    d_score = (
        soft_float * (d_prob - jnp.sum(soft_float * d_prob, axis=-1, keepdims=True))
    ).astype(BF16)
    d_query = jnp.einsum("hqk,khd->qhd", d_score, k_full, preferred_element_type=F32)
    d_query = (d_query * score_scale).astype(BF16).astype(F32)
    d_key = jnp.einsum("hqk,qhd->khd", d_score, q_full, preferred_element_type=F32)
    d_key = (d_key * score_scale).astype(BF16)
    d_q_raw = jnp.concatenate(
        [d_query[..., :NOPE], rotate(d_query[..., NOPE:], cosine[:, None, :], -sine[:, None, :])],
        axis=-1,
    )
    d_q_raw = d_q_raw.astype(BF16).reshape(group, hq)
    d_key_value = jnp.concatenate([d_key[..., :NOPE], d_values], axis=-1).reshape(group, hkv)
    dk_rope = jnp.sum(d_key[..., NOPE:].astype(F32), axis=1)
    d_latent_part = jnp.concatenate([dot_t(d_key_value, w_expand), dk_rope], axis=-1)
    d_latent_sum = scatter_seq(d_latent_part)
    d_attn_in = scatter_seq(dot_t(d_q_raw, w_query))
    grad_expand = t_dot(latent_normed, d_key_value)
    grad_query = t_dot(attn_in, d_q_raw)

    d_k_pe = rotate(d_latent_sum[:, KV_RANK:], cosine[:tokens], -sine[:tokens])
    d_latent, grad_latent_gain = norm_backward(
        latent[:tokens], g_latent, d_latent_sum[:, :KV_RANK]
    )
    d_latent_raw = jnp.concatenate([d_latent, d_k_pe], axis=-1).astype(BF16)
    d_attn_in = d_attn_in + dot_t(d_latent_raw, w_latent)
    d_x_part, grad_attn_gain = norm_backward(x_float, g_attn, d_attn_in)
    grad_inputs = d_residual + d_x_part

    shard_edown = reduce_dp(grad_edown, 2).astype(F32)
    shard_egate = reduce_dp(grad_egate, 1).astype(F32)
    shard_eup = reduce_dp(grad_eup, 1).astype(F32)

    def joined(piece):
        return lax.all_gather(piece, "seq", axis=0, tiled=False)

    def shared_columns(gradient):
        all_units = joined(reduce_dp(gradient, 0)).reshape(seq_count, shard, dp_count, unit)
        return all_units.transpose(1, 2, 0, 3).reshape(shard, hidden).astype(F32)

    out_sgate = shared_columns(grad_sgate)
    out_sup = shared_columns(grad_sup)
    out_sdown = joined(reduce_dp(grad_sdown, 0)).reshape(hidden // dp_count, width).astype(F32)
    out_output = token_gradient(flat_out, d_attn, d_rank)
    out_query = (
        joined(reduce_dp(grad_query, 0)).transpose(1, 0, 2).reshape(shard, HEADS * QK).astype(F32)
    )
    out_expand = (
        joined(reduce_dp(grad_expand, 0))
        .transpose(1, 0, 2)
        .reshape(KV_RANK // dp_count, HEADS * (NOPE + VDIM))
        .astype(F32)
    )
    out_latent = token_gradient(attn_in[:tokens], d_latent_raw, d_rank)

    early = lax.psum(
        jnp.concatenate([grad_ffn_gain, grad_router.reshape(-1)]), ("seq", "dp")
    )
    late = lax.psum(jnp.concatenate([grad_attn_gain, grad_latent_gain]), ("seq", "dp"))
    out_ffn_gain = lax.dynamic_slice_in_dim(early, d_rank * shard, shard, 0)
    out_router = lax.dynamic_slice_in_dim(
        early[width:].reshape(width, experts), d_rank * shard, shard, 0
    )
    out_attn_gain = lax.dynamic_slice_in_dim(late, d_rank * shard, shard, 0)
    out_latent_gain = lax.dynamic_slice_in_dim(late, width + d_rank * rank_shard, rank_shard, 0)

    return (
        layer_out[None],
        grad_inputs[None],
        out_attn_gain,
        out_query,
        out_latent,
        out_latent_gain,
        out_expand,
        out_output,
        out_ffn_gain,
        out_router,
        out_sgate,
        out_sup,
        out_sdown,
        shard_egate,
        shard_eup,
        shard_edown,
    )


def solution(mesh):
    placed = (
        P("dp", "seq", None),
        P("dp", None),
        P("dp", "seq", None),
        P("dp", "seq", None),
        P("dp"),
        P("dp", None),
        P("dp", None),
        P("dp"),
        P("dp", None),
        P("dp", None),
        P("dp"),
        P("dp", None),
        P("dp", None),
        P("dp", None),
        P("dp", None),
        P("seq", "dp", None),
        P("seq", "dp", None),
        P("seq", None, "dp"),
    )
    return jax.shard_map(
        local,
        mesh=mesh,
        in_specs=placed,
        out_specs=(
            P("dp", "seq", None),
            P("dp", "seq", None),
            P("dp"),
            P("dp", None),
            P("dp", None),
            P("dp"),
            P("dp", None),
            P("dp", None),
            P("dp"),
            P("dp", None),
            P("dp", None),
            P("dp", None),
            P("dp", None),
            P("seq", "dp", None),
            P("seq", "dp", None),
            P("seq", None, "dp"),
        ),
        check_vma=False,
    )
```

```python
import math

import jax
import jax.numpy as jnp
from jax import lax
from jax.experimental import pallas as pl
from jax.experimental.pallas import tpu as pltpu
from jax.sharding import PartitionSpec as P

HEADS = 16
NOPE = 128
ROPE = 64
VDIM = 128
KV_RANK = 512
TOP = 6
EXP_DEV = 2
CAP = 480

EPSILON = 1e-06
MASKED = -1e30
HIGHEST = lax.Precision.HIGHEST
F32 = jnp.float32
BF16 = jnp.bfloat16
QK = NOPE + ROPE


def normalized_rows(values, gain):
    return values * lax.rsqrt(jnp.mean(values * values, axis=-1, keepdims=True) + EPSILON) * gain


def norm_backward(values, gain, upstream):
    scale = lax.rsqrt(jnp.mean(values * values, axis=-1, keepdims=True) + EPSILON)
    normed = values * scale
    weighted = upstream * gain
    d_values = scale * (weighted - normed * jnp.mean(weighted * normed, axis=-1, keepdims=True))
    return d_values, jnp.sum(upstream * normed, axis=0)


def angles(positions, width):
    frequency = 10000.0 ** (-(2.0 * jnp.arange(width // 2, dtype=F32)) / width)
    turned = positions.astype(F32)[:, None] * frequency[None, :]
    return (jnp.cos(turned), jnp.sin(turned))


def rotate(values, cosine, sine):
    half_width = values.shape[-1] // 2
    lower_half = values[..., :half_width]
    upper_half = values[..., half_width:]
    return jnp.concatenate(
        [lower_half * cosine - upper_half * sine, upper_half * cosine + lower_half * sine], axis=-1
    )


def swiglu(gate_portion, up_part):
    return jax.nn.silu(gate_portion) * up_part


def dot(left, right):
    return jnp.dot(left, right, preferred_element_type=F32)


def dot_t(left, right):
    return lax.dot_general(left, right, (((1,), (1,)), ((), ())), preferred_element_type=F32)


def t_dot(left, right):
    return lax.dot_general(left, right, (((0,), (0,)), ((), ())), preferred_element_type=F32)


def flip_copy(src, dst, send_sem, recv_sem, target):
    copy = pltpu.make_async_remote_copy(
        src_ref=src,
        dst_ref=dst,
        send_sem=send_sem,
        recv_sem=recv_sem,
        device_id=target,
        device_id_type=pl.DeviceIdType.MESH,
    )
    copy.start()
    return copy


def waiting(block, send_sem, recv_sem, target):
    return pltpu.make_async_remote_copy(
        src_ref=block,
        dst_ref=block,
        send_sem=send_sem,
        recv_sem=recv_sem,
        device_id=target,
        device_id_type=pl.DeviceIdType.MESH,
    )


def spread_seq(block, out, sems, place, chips):
    sends, recvs, near_send, near_recv, own_sem = sems
    chip, core, group = place
    beside = {"seq": 2 * chip + 1 - core}
    local_copy = pltpu.make_async_copy(block, out.at[chip, core], own_sem.at[0])
    local_copy.start()
    more = [chip + 1 < chips, chip > 0]
    onward = [{"seq": 2 * (chip + 1) + core}, {"seq": 2 * (chip - 1) + core}]
    for way in range(2):

        @pl.when(more[way])
        def _(way=way):
            flip_copy(
                block, out.at[chip, core], sends.at[way, 0], recvs.at[way, 0], onward[way]
            )

    flip_copy(block, out.at[chip, core], near_send.at[0, 0], near_recv.at[0, 0], beside)
    yield
    for step in range(1, chips):
        for way in range(2):
            source = chip - step if way == 0 else chip + step
            there = source >= 0 if way == 0 else source < chips

            @pl.when(there)
            def _(way=way, step=step, source=source):
                arrived = out.at[source, core]
                waiting(
                    arrived, sends.at[way, step - 1], recvs.at[way, step - 1], beside
                ).wait_recv()
                if step < chips - 1:

                    @pl.when(more[way])
                    def _():
                        flip_copy(
                            arrived,
                            arrived,
                            sends.at[way, step],
                            recvs.at[way, step],
                            onward[way],
                        )

                flip_copy(
                    arrived, arrived, near_send.at[way, step], near_recv.at[way, step], beside
                )

        yield
    own = out.at[chip, core]
    waiting(own, near_send.at[0, 0], near_recv.at[0, 0], beside).wait()
    for step in range(chips):
        for way in range(2):
            source = chip - step if way == 0 else chip + step
            there = source >= 0 if way == 0 else source < chips
            if step:

                @pl.when(there)
                def _(way=way, step=step):
                    waiting(
                        own, near_send.at[way, step], near_recv.at[way, step], beside
                    ).wait()

            if step < chips - 1:

                @pl.when(there & more[way])
                def _(way=way, step=step):
                    waiting(
                        own, sends.at[way, step], recvs.at[way, step], onward[way]
                    ).wait_send()

    local_copy.wait()


def spread_sems(chips):
    return [pltpu.SemaphoreType.DMA((2, chips)) for _ in range(4)] + [
        pltpu.SemaphoreType.DMA((1,))
    ]


class Part:
    axes = ("near", "far")

    def __init__(self, value):
        self.value = value
        self.chips = lax.axis_size("seq") // 2
        self.groups = lax.axis_size("dp")


class GatherSeq(Part):
    def result(self):
        shape = (self.chips, 2) + self.value.shape
        return jax.ShapeDtypeStruct(shape, self.value.dtype), pl.ANY

    def scratch(self):
        return spread_sems(self.chips)

    def steps(self, block, out, scratch, place):
        chip, core, group = place
        yield from spread_seq(block, out, scratch, place, self.chips)

    def finish(self, out):
        return out.reshape((2 * self.chips,) + self.value.shape)


class ExchangeSeq(Part):
    axes = ("near", "all")

    def result(self):
        return jax.ShapeDtypeStruct(self.value.shape, self.value.dtype), pl.ANY

    def scratch(self):
        count = 2 * self.chips
        return [pltpu.SemaphoreType.DMA((count,)), pltpu.SemaphoreType.DMA((count,))]

    def steps(self, block, out, scratch, place):
        chip, core, group = place
        send, recv = scratch
        me = 2 * chip + core
        local_copy = pltpu.make_async_copy(block.at[me], out.at[me], send.at[0])
        local_copy.start()
        copies = [
            flip_copy(block.at[me ^ m], out.at[me], send.at[m], recv.at[m], {"seq": me ^ m})
            for m in range(1, 2 * self.chips)
        ]
        yield
        for copy in copies:
            copy.wait()
        local_copy.wait()

    def finish(self, out):
        return out


class GatherDp(Part):
    axes = ("dp",)
    cores = False

    def result(self):
        lead = (self.groups, 2) if self.cores else (self.groups,)
        return jax.ShapeDtypeStruct(lead + self.value.shape, self.value.dtype), pl.ANY

    def scratch(self):
        return [pltpu.SemaphoreType.DMA((2, self.groups + 1)) for _ in range(2)] + [
            pltpu.SemaphoreType.DMA((2, 1)) for _ in range(2)
        ]

    def steps(self, block, out, scratch, place):
        chip, core, group = place
        send, recv, relay_send, relay_recv = scratch
        count = self.groups
        beside = {"seq": 2 * chip + 1 - core}
        relayed = count == 4

        def at(rank):
            return out.at[rank, core] if self.cores else out.at[rank]

        def near(p):
            return flip_copy(
                at(group ^ p), at(group ^ p), send.at[1, p], recv.at[1, p], beside
            )

        local_copy = pltpu.make_async_copy(block, at(group), send.at[0, count])
        local_copy.start()
        copies = {
            p: flip_copy(block, at(group), send.at[0, p], recv.at[0, p], {"dp": group ^ p})
            for p in range(1, count)
            if not (relayed and p == 3)
        }
        cores = []
        if self.cores:
            cores.append(
                flip_copy(block, at(group), send.at[1, 0], recv.at[1, 0], beside)
            )
        yield
        relays = []
        for p, copy in copies.items():
            copy.wait_recv()
            if relayed:
                first = self.value.shape[0] // 32 * 16
                rows = pl.ds(0, first) if p == 1 else pl.ds(first, self.value.shape[0] - first)
                half = at(group ^ p).at[rows]
                relays.append(
                    flip_copy(
                        half,
                        half,
                        relay_send.at[p - 1, 0],
                        relay_recv.at[p - 1, 0],
                        {"dp": group ^ (3 - p)},
                    )
                )
            if self.cores:
                cores.append(near(p))
        yield
        for copy in relays:
            copy.wait()
        if self.cores and relayed:
            cores.append(near(3))
        for copy in copies.values():
            copy.wait_send()
        yield
        for copy in cores:
            copy.wait()
        local_copy.wait()

    def finish(self, out):
        return out


class GatherDpCores(GatherDp):
    axes = ("dp", "near")
    cores = True


class PairCores(Part):
    axes = ("near",)

    def result(self):
        shape = (self.value.shape[0], 2) + self.value.shape[1:]
        return jax.ShapeDtypeStruct(shape, self.value.dtype), pl.ANY

    def scratch(self):
        return [pltpu.SemaphoreType.DMA((3,))]

    def steps(self, block, out, scratch, place):
        chip, core, group = place
        (sems,) = scratch
        local_copy = pltpu.make_async_copy(block, out.at[:, core], sems.at[0])
        local_copy.start()
        copy = flip_copy(
            block, out.at[:, core], sems.at[1], sems.at[2], {"seq": 2 * chip + 1 - core}
        )
        yield
        copy.wait()
        local_copy.wait()

    def finish(self, out):
        return out


class Pass(Part):
    axes = ()

    def result(self):
        return jax.ShapeDtypeStruct(self.value.shape, self.value.dtype), pl.ANY

    def scratch(self):
        return [pltpu.SemaphoreType.DMA((1,))]

    def steps(self, block, out, scratch, place):
        local_copy = pltpu.make_async_copy(block, out, scratch[0].at[0])
        local_copy.start()
        yield
        local_copy.wait()

    def finish(self, out):
        return out


class ExchangeDp(Part):
    axes = ("dp",)

    def result(self):
        return jax.ShapeDtypeStruct(self.value.shape, self.value.dtype), pl.ANY

    def scratch(self):
        return [pltpu.SemaphoreType.DMA((self.groups,)) for _ in range(2)]

    def steps(self, block, out, scratch, place):
        chip, core, group = place
        send, recv = scratch
        local_copy = pltpu.make_async_copy(block.at[group], out.at[group], send.at[0])
        local_copy.start()
        copies = [
            flip_copy(block.at[group ^ p], out.at[group], send.at[p], recv.at[p], {"dp": group ^ p})
            for p in range(1, self.groups)
        ]
        yield
        for copy in copies:
            copy.wait()
        local_copy.wait()

    def finish(self, out):
        return out


def add_rows(target, sources):
    rows = target.shape[0]

    @pl.loop(0, rows // 16)
    def _(i):
        at = pl.ds(pl.multiple_of(i * 16, 16), 16)
        total = sources[0][at, :].astype(F32)
        for source in sources[1:]:
            total = total + source[at, :].astype(F32)
        target[at, :] = total.astype(target.dtype)


class ScatterSeq(Part):
    axes = ("near", "far")

    def result(self):
        return jax.ShapeDtypeStruct(self.value.shape[1:], F32), pltpu.VMEM

    def prepare(self):
        shape = self.value.shape
        return self.value.reshape((self.chips, 2) + shape[1:])

    def scratch(self):
        block = self.value.shape[1:]
        return [
            pltpu.VMEM((self.chips,) + block, BF16),
            pltpu.VMEM((self.chips,) + block, BF16),
            pltpu.VMEM((2, self.chips) + block, BF16),
            pltpu.SemaphoreType.DMA((2, self.chips)),
            pltpu.SemaphoreType.DMA((2, self.chips)),
            pltpu.SemaphoreType.DMA((2,)),
            pltpu.SemaphoreType.DMA((1,)),
        ]

    def reduce(self, partial, out, scratch, place):
        chip, core, group = place
        chips = self.chips
        mine, peer, arrived, send, recv, near, own_sem = scratch
        local_copy = pltpu.make_async_copy(partial.at[:, core], mine, own_sem.at[0])
        local_copy.start()
        beside = flip_copy(
            partial.at[:, 1 - core], peer, near.at[0], near.at[1], {"seq": 2 * chip + 1 - core}
        )
        yield
        local_copy.wait()
        beside.wait()
        for k in range(chips):
            add_rows(mine.at[k], [mine.at[k], peer.at[k]])
        more = [chip + 1 < chips, chip > 0]
        onward = [{"seq": 2 * (chip + 1) + core}, {"seq": 2 * (chip - 1) + core}]
        for step in range(chips - 1):
            for way in range(2):
                to = chips - 1 - step if way == 0 else step
                ahead = chip < to if way == 0 else chip > to

                @pl.when(ahead)
                def _(way=way, to=to):
                    @pl.when(more[1 - way])
                    def _():
                        waiting(
                            arrived.at[way, to], send.at[way, to], recv.at[way, to], onward[way]
                        ).wait_recv()
                        add_rows(mine.at[to], [mine.at[to], arrived.at[way, to]])

                    flip_copy(
                        mine.at[to],
                        arrived.at[way, to],
                        send.at[way, to],
                        recv.at[way, to],
                        onward[way],
                    )

            yield
        for way in range(2):

            @pl.when(more[1 - way])
            def _(way=way):
                waiting(
                    arrived.at[way, chip], send.at[way, chip], recv.at[way, chip], onward[way]
                ).wait_recv()

        @pl.when(more[0] & more[1])
        def _():
            add_rows(out, [mine.at[chip], arrived.at[0, chip], arrived.at[1, chip]])

        for way in range(2):

            @pl.when(more[1 - way] & jnp.logical_not(more[way]))
            def _(way=way):
                add_rows(out, [mine.at[chip], arrived.at[way, chip]])

            for to in range(chips):
                ahead = chip < to if way == 0 else chip > to

                @pl.when(ahead)
                def _(way=way, to=to):
                    waiting(
                        mine.at[to], send.at[way, to], recv.at[way, to], onward[way]
                    ).wait_send()

    def steps(self, partial, out, scratch, place):
        yield from self.reduce(partial, out, scratch, place)

    def finish(self, out):
        return out


class SumSeq(ScatterSeq):
    def result(self):
        return jax.ShapeDtypeStruct((self.chips, 2) + self.value.shape[1:], BF16), pl.ANY

    def scratch(self):
        return (
            ScatterSeq.scratch(self)
            + [pltpu.VMEM(self.value.shape[1:], BF16)]
            + spread_sems(self.chips)
        )

    def steps(self, partial, out, scratch, place):
        chip, core, group = place
        total = scratch[7]
        yield from self.reduce(partial, total, scratch[:7], place)
        yield from spread_seq(total, out, scratch[8:], place, self.chips)

    def finish(self, out):
        return out.reshape(self.value.shape)


class ReduceDp(Part):
    axes = ("dp",)

    def result(self):
        return jax.ShapeDtypeStruct(self.value.shape[1:], self.value.dtype), pltpu.VMEM

    def scratch(self):
        return [
            pltpu.VMEM(self.value.shape, self.value.dtype),
            pltpu.SemaphoreType.DMA((self.groups,)),
            pltpu.SemaphoreType.DMA((self.groups,)),
        ]

    def reduce(self, value, out, scratch, place):
        chip, core, group = place
        arrived, send, recv = scratch
        local_copy = pltpu.make_async_copy(value.at[group], arrived.at[0], send.at[0])
        local_copy.start()
        copies = [
            flip_copy(value.at[group ^ p], arrived.at[p], send.at[p], recv.at[p], {"dp": group ^ p})
            for p in range(1, self.groups)
        ]
        yield
        local_copy.wait()
        for copy in copies:
            copy.wait()
        add_rows(out, [arrived.at[p] for p in range(self.groups)])

    def steps(self, value, out, scratch, place):
        yield from self.reduce(value, out, scratch, place)

    def finish(self, out):
        return out


class ReduceDpGatherSeq(ReduceDp):
    axes = ("dp", "near", "far")

    def result(self):
        shape = (self.chips, 2) + self.value.shape[1:]
        return jax.ShapeDtypeStruct(shape, self.value.dtype), pl.ANY

    def scratch(self):
        return (
            ReduceDp.scratch(self)
            + [pltpu.VMEM(self.value.shape[1:], self.value.dtype)]
            + spread_sems(self.chips)
        )

    def steps(self, value, out, scratch, place):
        chip, core, group = place
        total = scratch[3]
        yield from self.reduce(value, total, scratch[:3], place)
        yield from spread_seq(total, out, scratch[4:], place, self.chips)

    def finish(self, out):
        return out.reshape((2 * self.chips,) + self.value.shape[1:])


def communicate(number, parts):
    values = [part.prepare() if isinstance(part, ScatterSeq) else part.value for part in parts]
    results = [part.result() for part in parts]
    scratches = [part.scratch() for part in parts]
    chips, groups = parts[0].chips, parts[0].groups
    axes = set()
    for part in parts:
        axes.update(part.axes)

    def kernel(*refs):
        ins, outs = refs[: len(parts)], refs[len(parts) : 2 * len(parts)]
        rest = list(refs[2 * len(parts) :])
        me, group = lax.axis_index("seq"), lax.axis_index("dp")
        chip, core = me // 2, lax.rem(me, 2)
        targets = []
        for m in range(1, 2 * chips):
            if "all" in axes or (m == 1 and "near" in axes) or (m % 2 == 0 and "far" in axes):
                targets.append({"seq": me ^ m})
        if "dp" in axes:
            targets += [{"dp": group ^ p} for p in range(1, groups)]
        barrier = pltpu.get_barrier_semaphore()
        for target in targets:
            pl.semaphore_signal(
                barrier, inc=1, device_id=target, device_id_type=pl.DeviceIdType.MESH
            )
        pl.semaphore_wait(barrier, len(targets))
        running = []
        for part, value, out, scratch in zip(parts, ins, outs, scratches):
            own, rest = rest[: len(scratch)], rest[len(scratch) :]
            running.append(part.steps(value, out, own, (chip, core, group)))
        while running:
            running = [steps for steps in running if next(steps, "end") != "end"]

    outs = pl.pallas_call(
        kernel,
        out_shape=[shape for shape, _ in results],
        in_specs=[pl.BlockSpec(memory_space=pl.ANY)] * len(parts),
        out_specs=[pl.BlockSpec(memory_space=space) for _, space in results],
        scratch_shapes=[item for scratch in scratches for item in scratch],
        compiler_params=pltpu.CompilerParams(
            collective_id=number, has_side_effects=True, vmem_limit_bytes=48 * 1024 * 1024
        ),
    )(*values)
    return [part.finish(out) for part, out in zip(parts, outs)]


def padded_rows(value):
    rows = value.shape[-2]
    more = -rows % 16
    return jnp.pad(value, [(0, 0)] * (value.ndim - 2) + [(0, more), (0, 0)])


def local(
    inputs,
    segments,
    routes,
    cotangent,
    attention_gain,
    query_weight,
    latent_weight,
    latent_gain,
    expand_weight,
    output_weight,
    feedforward_gain,
    router_weight,
    shared_gate,
    shared_up,
    shared_down,
    expert_gate,
    expert_up,
    expert_down,
):
    seq_count = lax.axis_size("seq")
    dp_count = lax.axis_size("dp")
    me = lax.axis_index("seq")
    d_rank = lax.axis_index("dp")
    tokens = inputs.shape[1]
    width = inputs.shape[2]
    group = tokens * seq_count
    experts = EXP_DEV * seq_count
    heads_dev = HEADS // seq_count
    score_scale = 1.0 / math.sqrt(QK)
    shard = width // dp_count

    hq = heads_dev * QK
    hkv = heads_dev * (NOPE + VDIM)
    rank_shard = latent_gain.shape[0]
    latent_width = latent_weight.shape[1]
    small = jnp.concatenate(
        [attention_gain, feedforward_gain, latent_gain, router_weight.reshape(-1)]
    )
    fold = shard // rank_shard
    expand_part = lax.dynamic_slice_in_dim(expand_weight, me * hkv, hkv, 1)
    expand_part = (
        expand_part.reshape(rank_shard, fold, hkv // fold).transpose(1, 0, 2).reshape(shard, -1)
    )
    pack = jnp.concatenate(
        [lax.dynamic_slice_in_dim(query_weight, me * hq, hq, 1), expand_part], axis=1
    )
    pack_width = pack.shape[1]
    small_rows = -(-small.shape[0] // (16 * pack_width)) * 16
    small_pack = jnp.pad(small, (0, small_rows * pack_width - small.shape[0]))
    pack = jnp.concatenate([pack, small_pack.reshape(small_rows, pack_width)], axis=0)
    routes_pad = jnp.pad(routes[0], ((0, 0), (0, 128 - TOP))).astype(BF16)

    core = lax.rem(me, 2)

    def half_of(weight):
        rows = weight.shape[0] // 2
        return lax.dynamic_slice_in_dim(weight, core * rows, rows, 0)

    hidden = shared_gate.shape[1]
    unit = hidden // (dp_count * seq_count)
    side = dp_count * unit

    def columns_of(weight):
        split = weight.reshape(weight.shape[0], dp_count, seq_count, unit)
        mine = lax.dynamic_index_in_dim(split, me, 2, keepdims=False)
        return mine.reshape(weight.shape[0], side)

    w_output = lax.all_gather(half_of(output_weight), "dp", axis=0, tiled=False)
    w_sin = lax.all_gather(
        jnp.concatenate([columns_of(shared_gate), columns_of(shared_up)], axis=1),
        "dp",
        axis=0,
        tiled=True,
    )
    w_sdown = lax.all_gather(
        lax.dynamic_slice_in_dim(shared_down, me * unit, unit, 0), "dp", axis=0, tiled=True
    )
    w_egate = lax.all_gather(expert_gate, "dp", axis=1, tiled=True)
    w_eup = lax.all_gather(expert_up, "dp", axis=1, tiled=True)
    w_edown = lax.all_gather(expert_down, "dp", axis=2, tiled=True)

    x_all, routes_all, pack, w_latent = communicate(
        1,
        [
            GatherSeq(inputs[0]),
            GatherSeq(routes_pad),
            GatherDp(pack),
            GatherDpCores(half_of(latent_weight)),
        ],
    )
    x_all = x_all.reshape(group, width)
    w_query = pack[:, :shard, :hq].reshape(width, hq)
    w_latent = w_latent.reshape(width, latent_width)
    w_expand = (
        pack[:, :shard, hq:]
        .reshape(dp_count, fold, rank_shard, hkv // fold)
        .transpose(0, 2, 1, 3)
        .reshape(KV_RANK, hkv)
    )
    small = pack[:, shard:].reshape(dp_count, small_rows * pack_width)
    g_attn = small[:, :shard].reshape(width).astype(F32)
    g_ffn = small[:, shard : 2 * shard].reshape(width).astype(F32)
    g_latent = small[:, 2 * shard : 2 * shard + rank_shard].reshape(KV_RANK).astype(F32)
    w_router = small[:, 2 * shard + rank_shard :][:, : shard * experts].reshape(width, experts)

    routes_all = routes_all.reshape(group, 128)[:, :TOP].astype(jnp.int32)
    positions = jnp.arange(group, dtype=jnp.int32)
    seg_all = segments[0]
    cosine, sine = angles(positions, ROPE)
    my_experts = me * EXP_DEV + jnp.arange(EXP_DEV, dtype=jnp.int32)
    expert_ids = jnp.arange(experts, dtype=jnp.int32)
    hit = jnp.any(routes_all[None] == my_experts[:, None, None], axis=-1).astype(jnp.int32)
    slot = jnp.where(hit == 1, jnp.cumsum(hit, axis=1) - hit, CAP)
    route_hot = jnp.any(routes_all[:, :, None] == expert_ids[None, None, :], axis=1)
    placed = slot[:, None, :] == jnp.arange(CAP, dtype=jnp.int32)[None, :, None]
    dispatch = placed.astype(BF16).reshape(EXP_DEV * CAP, group)

    def own(value):
        return lax.dynamic_slice_in_dim(value, me * tokens, tokens, 0)

    attn_in = normalized_rows(x_all.astype(F32), g_attn).astype(BF16)
    q_raw = dot(attn_in, w_query).reshape(group, heads_dev, QK)
    latent_raw = dot(attn_in, w_latent)
    latent = latent_raw[:, :KV_RANK]
    latent_normed = normalized_rows(latent, g_latent).astype(BF16)
    key_value = dot(latent_normed, w_expand).reshape(group, heads_dev, NOPE + VDIM)
    q_full = jnp.concatenate(
        [q_raw[..., :NOPE], rotate(q_raw[..., NOPE:], cosine[:, None, :], sine[:, None, :])],
        axis=-1,
    ).astype(BF16)
    k_rot = rotate(latent_raw[:, KV_RANK:], cosine, sine)
    k_full = jnp.concatenate(
        [key_value[..., :NOPE], jnp.broadcast_to(k_rot[:, None, :], (group, heads_dev, ROPE))],
        axis=-1,
    ).astype(BF16)
    values = key_value[..., NOPE:].astype(BF16)
    visible = (seg_all[:, None] == seg_all[None, :]) & (seg_all[:, None] >= 0) & (
        positions[None, :] <= positions[:, None]
    ) | (positions[None, :] == positions[:, None])
    scores = jnp.einsum("qhd,khd->hqk", q_full, k_full, preferred_element_type=F32) * score_scale
    scores = jnp.where(visible[None], scores, MASKED)
    row_peak = jnp.max(scores, axis=-1, keepdims=True)
    exponent = jnp.exp(scores - row_peak)
    soft_float = exponent / jnp.sum(exponent, axis=-1, keepdims=True)
    soft = soft_float.astype(BF16)
    head_out = jnp.einsum("hqk,khd->qhd", soft, values, preferred_element_type=F32)
    head_out = head_out.astype(BF16).reshape(seq_count, tokens, heads_dev * VDIM)

    head_out, w_output = communicate(2, [ExchangeSeq(head_out), PairCores(w_output)])
    w_output = w_output.reshape(width, width)
    flat_out = jnp.swapaxes(head_out, 0, 1).reshape(tokens, HEADS * VDIM)
    x_float = inputs[0].astype(F32)
    residual = x_float + dot(flat_out, w_output)
    ffn_in = normalized_rows(residual, g_ffn).astype(BF16)

    (ffn_all,) = communicate(3, [GatherSeq(ffn_in)])
    ffn_all = ffn_all.reshape(group, width)

    router_probs = jax.nn.softmax(dot(ffn_all, w_router), axis=-1)
    chosen = jnp.where(route_hot, router_probs, 0.0)
    chosen_sum = jnp.sum(chosen, axis=-1, keepdims=True)
    gates = chosen / chosen_sum
    my_gates = lax.dynamic_slice_in_dim(gates.T, me * EXP_DEV, EXP_DEV, 0)
    gate_rows = jnp.sum(jnp.where(placed, my_gates[:, None, :], 0.0), axis=-1)

    g_own = lax.optimization_barrier((cotangent[0], ffn_all))[0]
    (g_all,) = communicate(4, [GatherSeq(g_own)])
    g_all = g_all.reshape(group, width)

    side_in = dot(ffn_all, w_sin)
    side_gate, side_up = side_in[:, :side], side_in[:, side:]
    side_act = swiglu(side_gate, side_up).astype(BF16)
    grad_sdown = t_dot(side_act, g_all)
    d_side_act = dot_t(g_all, w_sdown)
    _, side_pull = jax.vjp(swiglu, side_gate, side_up)
    d_side_gate, d_side_up = side_pull(d_side_act)
    d_side = jnp.concatenate([d_side_gate, d_side_up], axis=1).astype(BF16)
    grad_sin = t_dot(ffn_all, d_side)
    rows_shape = (EXP_DEV, CAP, width)
    expert_in = dot(dispatch, ffn_all).astype(BF16).reshape(rows_shape)
    hidden_gate = jnp.einsum("nmh,nhq->nmq", expert_in, w_egate, preferred_element_type=F32)
    expert_in, all_sin, all_sdown = communicate(
        5,
        [
            Pass(expert_in),
            ReduceDpGatherSeq(grad_sin.astype(BF16).reshape(dp_count, shard, 2 * side)),
            ReduceDpGatherSeq(padded_rows(grad_sdown.astype(BF16).reshape(dp_count, unit, width))),
        ],
    )
    all_side = all_sin.reshape(seq_count, shard, 2, dp_count, unit)
    all_side = all_side.transpose(2, 1, 3, 0, 4).reshape(2, shard, hidden).astype(F32)
    out_sgate, out_sup = all_side[0], all_side[1]
    out_sdown = all_sdown[:, :unit].reshape(hidden // dp_count, width).astype(F32)

    grad_rows = dot(dispatch, g_all).reshape(rows_shape)
    expert_grad = (gate_rows[:, :, None] * grad_rows).astype(BF16)
    hidden_up = jnp.einsum("nmh,nhq->nmq", expert_in, w_eup, preferred_element_type=F32)
    expert_act = swiglu(hidden_gate, hidden_up).astype(BF16)
    grad_edown = jnp.einsum("kcf,kcd->kfd", expert_act, expert_grad, preferred_element_type=F32)
    expert_out = jnp.einsum(
        "kcf,kfd->kcd", expert_act, w_edown, preferred_element_type=F32
    ).astype(BF16).astype(F32)
    d_gate_rows = jnp.sum(expert_out * grad_rows, axis=-1)
    moe_rows = (gate_rows[:, :, None] * expert_out).astype(BF16).reshape(EXP_DEV * CAP, width)
    ffn_out = (dot(side_act, w_sdown) + t_dot(dispatch, moe_rows)).astype(BF16)

    d_act = jnp.einsum("kcd,kfd->kcf", expert_grad, w_edown, preferred_element_type=F32)
    _, expert_pull = jax.vjp(swiglu, hidden_gate, hidden_up)
    d_hidden_gate, d_hidden_up = expert_pull(d_act)
    d_hidden_gate = d_hidden_gate.astype(BF16)
    d_hidden_up = d_hidden_up.astype(BF16)
    grad_egate = jnp.einsum("kcd,kcf->kdf", expert_in, d_hidden_gate, preferred_element_type=F32)
    grad_eup = jnp.einsum("kcd,kcf->kdf", expert_in, d_hidden_up, preferred_element_type=F32)
    shard_edown = lax.psum_scatter(
        grad_edown.astype(BF16), "dp", scatter_dimension=2, tiled=True
    ).astype(F32)
    shard_egate = lax.psum_scatter(
        grad_egate.astype(BF16), "dp", scatter_dimension=1, tiled=True
    ).astype(F32)
    shard_eup = lax.psum_scatter(
        grad_eup.astype(BF16), "dp", scatter_dimension=1, tiled=True
    ).astype(F32)
    d_expert_in = (
        jnp.einsum("sta,sra->str", d_hidden_gate, w_egate, preferred_element_type=F32)
        + jnp.einsum("sta,sra->str", d_hidden_up, w_eup, preferred_element_type=F32)
    ).astype(BF16)
    d_ffn_partial = dot_t(d_side, w_sin) + t_dot(
        dispatch, d_expert_in.reshape(EXP_DEV * CAP, width)
    )
    d_gate_own = jnp.sum(jnp.where(placed, d_gate_rows[:, :, None], 0.0), axis=1)
    mine_hot = (my_experts[:, None] == expert_ids[None, :]).astype(F32)
    d_gate_wide = jnp.sum(d_gate_own[:, :, None] * mine_hot[:, None, :], axis=0)
    d_gate_high = d_gate_wide.astype(BF16)
    d_gate_low = (d_gate_wide - d_gate_high.astype(F32)).astype(BF16)
    d_gate_pack = jnp.concatenate(
        [d_gate_high, d_gate_low, jnp.zeros((group, 128 - 2 * experts), BF16)], axis=1
    )
    d_ffn, d_gate = communicate(
        6,
        [
            ScatterSeq(d_ffn_partial.astype(BF16).reshape(seq_count, tokens, width)),
            ScatterSeq(d_gate_pack.reshape(seq_count, tokens, 128)),
        ],
    )
    d_gate = d_gate[:, :experts] + d_gate[:, experts : 2 * experts]

    own_hot = own(route_hot)
    own_probs = own(router_probs)
    own_gates = own(gates)
    d_chosen = (d_gate - jnp.sum(d_gate * own_gates, axis=-1, keepdims=True)) / own(chosen_sum)
    d_probs = jnp.where(own_hot, d_chosen, 0.0)
    d_logits = own_probs * (d_probs - jnp.sum(own_probs * d_probs, axis=-1, keepdims=True))
    grad_router = jnp.einsum("td,te->de", ffn_in.astype(F32), d_logits, precision=HIGHEST)
    d_ffn = d_ffn + jnp.einsum("te,de->td", d_logits, w_router.astype(F32), precision=HIGHEST)

    grad_out = cotangent[0].astype(F32)
    d_resid_part, grad_ffn_gain = norm_backward(residual, g_ffn, d_ffn)
    d_residual = grad_out + d_resid_part
    d_attn = d_residual.astype(BF16)
    d_head = dot_t(d_attn, w_output).astype(BF16)
    d_head = jnp.swapaxes(d_head.reshape(tokens, seq_count, heads_dev * VDIM), 0, 1)
    (head_grad,) = communicate(7, [ExchangeSeq(d_head)])
    head_grad = head_grad.reshape(group, heads_dev, VDIM)

    d_values = jnp.einsum("hqk,qhd->khd", soft, head_grad, preferred_element_type=F32).astype(BF16)
    d_prob = jnp.einsum("qhd,khd->hqk", head_grad, values, preferred_element_type=F32)
    d_score = (
        soft_float * (d_prob - jnp.sum(soft_float * d_prob, axis=-1, keepdims=True))
    ).astype(BF16)
    d_query = jnp.einsum("hqk,khd->qhd", d_score, k_full, preferred_element_type=F32)
    d_query = (d_query * score_scale).astype(BF16).astype(F32)
    d_key = jnp.einsum("hqk,qhd->khd", d_score, q_full, preferred_element_type=F32)
    d_key = (d_key * score_scale).astype(BF16)
    d_q_raw = jnp.concatenate(
        [d_query[..., :NOPE], rotate(d_query[..., NOPE:], cosine[:, None, :], -sine[:, None, :])],
        axis=-1,
    )
    d_q_raw = d_q_raw.astype(BF16).reshape(group, hq)
    d_key_value = jnp.concatenate([d_key[..., :NOPE], d_values], axis=-1).reshape(group, hkv)
    dk_rope = jnp.sum(d_key[..., NOPE:].astype(F32), axis=1)
    latent_pad = -latent_width % 128
    d_latent_part = jnp.concatenate(
        [dot_t(d_key_value, w_expand), dk_rope, jnp.zeros((group, latent_pad), F32)], axis=-1
    ).astype(BF16)
    d_attn_part = dot_t(d_q_raw, w_query).astype(BF16)
    grad_expand = t_dot(latent_normed, d_key_value).astype(BF16)
    grad_query = t_dot(attn_in, d_q_raw).astype(BF16)

    def by_group(rows):
        return jnp.swapaxes(rows.reshape(tokens, dp_count, -1), 0, 1)

    own_attn_in = own(attn_in)
    d_latent_sum, d_attn_in, sum_query, sum_expand, left_out, right_out, left_latent = communicate(
        8,
        [
            ScatterSeq(d_latent_part.reshape(seq_count, tokens, latent_width + latent_pad)),
            ScatterSeq(d_attn_part.reshape(seq_count, tokens, width)),
            ReduceDp(grad_query.reshape(dp_count, shard, hq)),
            ReduceDp(grad_expand.reshape(dp_count, rank_shard, hkv)),
            ExchangeDp(by_group(flat_out)),
            GatherDp(d_attn),
            ExchangeDp(by_group(own_attn_in)),
        ],
    )
    d_k_pe = rotate(d_latent_sum[:, KV_RANK:latent_width], own(cosine), -own(sine))
    d_latent, grad_latent_gain = norm_backward(
        own(latent), g_latent, d_latent_sum[:, :KV_RANK]
    )
    d_latent_raw = jnp.concatenate([d_latent, d_k_pe], axis=-1).astype(BF16)
    d_attn_in = d_attn_in + dot_t(d_latent_raw, w_latent)
    d_x_part, grad_attn_gain = norm_backward(x_float, g_attn, d_attn_in)
    grad_inputs = d_residual + d_x_part

    all_tokens = dp_count * tokens
    grad_output = t_dot(left_out.reshape(all_tokens, shard), right_out.reshape(all_tokens, width))
    grad_output = grad_output.astype(BF16).reshape(seq_count, shard // seq_count, width)
    latent_rows = jnp.pad(d_latent_raw, ((0, 0), (0, latent_pad)))

    gains = jnp.concatenate(
        [
            grad_attn_gain.reshape(dp_count, -1),
            grad_ffn_gain.reshape(dp_count, -1),
            grad_latent_gain.reshape(dp_count, -1),
            grad_router.reshape(dp_count, -1),
        ],
        axis=1,
    )
    gain_width = gains.shape[1]
    gain_rows = -(-gain_width // (16 * 128)) * 16
    gains = jnp.pad(gains, ((0, 0), (0, gain_rows * 128 - gain_width)))

    moe, all_query, all_expand, out_output, right_latent, all_gains = communicate(
        9,
        [
            ScatterSeq(ffn_out.reshape(seq_count, tokens, width)),
            GatherSeq(sum_query),
            GatherSeq(sum_expand),
            SumSeq(grad_output),
            GatherDp(latent_rows),
            ReduceDpGatherSeq(gains.reshape(dp_count, gain_rows, 128)),
        ],
    )
    layer_out = (residual + moe).astype(BF16)
    out_query = jnp.swapaxes(all_query, 0, 1).reshape(shard, HEADS * QK).astype(F32)
    out_expand = (
        jnp.swapaxes(all_expand, 0, 1).reshape(rank_shard, HEADS * (NOPE + VDIM)).astype(F32)
    )
    out_output = out_output.reshape(shard, width).astype(F32)
    grad_latent = t_dot(
        left_latent.reshape(all_tokens, shard),
        right_latent.reshape(all_tokens, -1)[:, :latent_width],
    ).astype(BF16)
    latent_blocks = jnp.pad(
        grad_latent.reshape(seq_count, shard // seq_count, latent_width),
        ((0, 0), (0, 0), (0, latent_pad)),
    )
    (out_latent,) = communicate(10, [SumSeq(latent_blocks)])
    out_latent = out_latent.reshape(shard, -1)[:, :latent_width].astype(F32)

    sums = jnp.sum(all_gains, axis=0).reshape(-1)
    out_attn_gain = sums[:shard]
    out_ffn_gain = sums[shard : 2 * shard]
    out_latent_gain = sums[2 * shard : 2 * shard + rank_shard]
    out_router = sums[2 * shard + rank_shard : gain_width].reshape(shard, experts)

    return (
        layer_out[None],
        grad_inputs[None],
        out_attn_gain,
        out_query,
        out_latent,
        out_latent_gain,
        out_expand,
        out_output,
        out_ffn_gain,
        out_router,
        out_sgate,
        out_sup,
        out_sdown,
        shard_egate,
        shard_eup,
        shard_edown,
    )


def solution(mesh):
    placed = (
        P("dp", "seq", None),
        P("dp", None),
        P("dp", "seq", None),
        P("dp", "seq", None),
        P("dp"),
        P("dp", None),
        P("dp", None),
        P("dp"),
        P("dp", None),
        P("dp", None),
        P("dp"),
        P("dp", None),
        P("dp", None),
        P("dp", None),
        P("dp", None),
        P("seq", "dp", None),
        P("seq", "dp", None),
        P("seq", None, "dp"),
    )
    return jax.shard_map(
        local,
        mesh=mesh,
        in_specs=placed,
        out_specs=(
            P("dp", "seq", None),
            P("dp", "seq", None),
            P("dp"),
            P("dp", None),
            P("dp", None),
            P("dp"),
            P("dp", None),
            P("dp", None),
            P("dp"),
            P("dp", None),
            P("dp", None),
            P("dp", None),
            P("dp", None),
            P("seq", "dp", None),
            P("seq", "dp", None),
            P("seq", None, "dp"),
        ),
        check_vma=False,
    )
```

```python
import math

import jax
import jax.numpy as jnp
from jax import lax
from jax.experimental import pallas as pl
from jax.experimental.pallas import tpu as pltpu
from jax.sharding import PartitionSpec as P

HEADS = 16
NOPE = 128
ROPE = 64
VDIM = 128
KV_RANK = 512
TOP = 6
EXP_DEV = 2
CAP = 480

EPSILON = 1e-06
MASKED = -1e30
HIGHEST = lax.Precision.HIGHEST
F32 = jnp.float32
BF16 = jnp.bfloat16
QK = NOPE + ROPE


def normalized_rows(values, gain):
    return values * lax.rsqrt(jnp.mean(values * values, axis=-1, keepdims=True) + EPSILON) * gain


def norm_backward(values, gain, upstream):
    scale = lax.rsqrt(jnp.mean(values * values, axis=-1, keepdims=True) + EPSILON)
    normed = values * scale
    weighted = upstream * gain
    d_values = scale * (weighted - normed * jnp.mean(weighted * normed, axis=-1, keepdims=True))
    return d_values, jnp.sum(upstream * normed, axis=0)


def angles(positions, width):
    frequency = 10000.0 ** (-(2.0 * jnp.arange(width // 2, dtype=F32)) / width)
    turned = positions.astype(F32)[:, None] * frequency[None, :]
    return (jnp.cos(turned), jnp.sin(turned))


def rotate(values, cosine, sine):
    half_width = values.shape[-1] // 2
    lower_half = values[..., :half_width]
    upper_half = values[..., half_width:]
    return jnp.concatenate(
        [lower_half * cosine - upper_half * sine, upper_half * cosine + lower_half * sine], axis=-1
    )


def swiglu(gate_portion, up_part):
    return jax.nn.silu(gate_portion) * up_part


def dot(left, right):
    return jnp.dot(left, right, preferred_element_type=F32)


def dot_t(left, right):
    return lax.dot_general(left, right, (((1,), (1,)), ((), ())), preferred_element_type=F32)


def t_dot(left, right):
    return lax.dot_general(left, right, (((0,), (0,)), ((), ())), preferred_element_type=F32)


def flip_copy(src, dst, send_sem, recv_sem, target):
    copy = pltpu.make_async_remote_copy(
        src_ref=src,
        dst_ref=dst,
        send_sem=send_sem,
        recv_sem=recv_sem,
        device_id=target,
        device_id_type=pl.DeviceIdType.MESH,
    )
    copy.start()
    return copy


def waiting(block, send_sem, recv_sem, target):
    return pltpu.make_async_remote_copy(
        src_ref=block,
        dst_ref=block,
        send_sem=send_sem,
        recv_sem=recv_sem,
        device_id=target,
        device_id_type=pl.DeviceIdType.MESH,
    )


def spread_seq(block, out, sems, place, chips):
    sends, recvs, near_send, near_recv, own_sem = sems
    chip, core, group = place
    beside = {"seq": 2 * chip + 1 - core}
    local_copy = pltpu.make_async_copy(block, out.at[chip, core], own_sem.at[0])
    local_copy.start()
    more = [chip + 1 < chips, chip > 0]
    onward = [{"seq": 2 * (chip + 1) + core}, {"seq": 2 * (chip - 1) + core}]
    for way in range(2):

        @pl.when(more[way])
        def _(way=way):
            flip_copy(
                block, out.at[chip, core], sends.at[way, 0], recvs.at[way, 0], onward[way]
            )

    flip_copy(block, out.at[chip, core], near_send.at[0, 0], near_recv.at[0, 0], beside)
    yield
    for step in range(1, chips):
        for way in range(2):
            source = chip - step if way == 0 else chip + step
            there = source >= 0 if way == 0 else source < chips

            @pl.when(there)
            def _(way=way, step=step, source=source):
                arrived = out.at[source, core]
                waiting(
                    arrived, sends.at[way, step - 1], recvs.at[way, step - 1], beside
                ).wait_recv()
                if step < chips - 1:

                    @pl.when(more[way])
                    def _():
                        flip_copy(
                            arrived,
                            arrived,
                            sends.at[way, step],
                            recvs.at[way, step],
                            onward[way],
                        )

                flip_copy(
                    arrived, arrived, near_send.at[way, step], near_recv.at[way, step], beside
                )

        yield
    own = out.at[chip, core]
    waiting(own, near_send.at[0, 0], near_recv.at[0, 0], beside).wait()
    for step in range(chips):
        for way in range(2):
            source = chip - step if way == 0 else chip + step
            there = source >= 0 if way == 0 else source < chips
            if step:

                @pl.when(there)
                def _(way=way, step=step):
                    waiting(
                        own, near_send.at[way, step], near_recv.at[way, step], beside
                    ).wait()

            if step < chips - 1:

                @pl.when(there & more[way])
                def _(way=way, step=step):
                    waiting(
                        own, sends.at[way, step], recvs.at[way, step], onward[way]
                    ).wait_send()

    local_copy.wait()


def spread_sems(chips):
    return [pltpu.SemaphoreType.DMA((2, chips)) for _ in range(4)] + [
        pltpu.SemaphoreType.DMA((1,))
    ]


class Part:
    axes = ("near", "far")
    alias = False

    def __init__(self, value):
        self.value = value
        self.chips = lax.axis_size("seq") // 2
        self.groups = lax.axis_size("dp")


class GatherSeq(Part):
    def result(self):
        shape = (self.chips, 2) + self.value.shape
        return jax.ShapeDtypeStruct(shape, self.value.dtype), pl.ANY

    def scratch(self):
        return spread_sems(self.chips)

    def steps(self, block, out, scratch, place):
        chip, core, group = place
        yield from spread_seq(block, out, scratch, place, self.chips)

    def finish(self, out):
        return out.reshape((2 * self.chips,) + self.value.shape)


class ExchangeSeq(Part):
    axes = ("near", "all")

    def result(self):
        return jax.ShapeDtypeStruct(self.value.shape, self.value.dtype), pl.ANY

    def scratch(self):
        count = 2 * self.chips
        return [pltpu.SemaphoreType.DMA((count,)), pltpu.SemaphoreType.DMA((count,))]

    def steps(self, block, out, scratch, place):
        chip, core, group = place
        send, recv = scratch
        me = 2 * chip + core
        local_copy = pltpu.make_async_copy(block.at[me], out.at[me], send.at[0])
        local_copy.start()
        copies = [
            flip_copy(block.at[me ^ m], out.at[me], send.at[m], recv.at[m], {"seq": me ^ m})
            for m in range(1, 2 * self.chips)
        ]
        yield
        for copy in copies:
            copy.wait()
        local_copy.wait()

    def finish(self, out):
        return out


class GatherDp(Part):
    axes = ("dp",)
    cores = False

    def result(self):
        lead = (self.groups, 2) if self.cores else (self.groups,)
        return jax.ShapeDtypeStruct(lead + self.value.shape, self.value.dtype), pl.ANY

    def scratch(self):
        return [pltpu.SemaphoreType.DMA((2, self.groups + 1)) for _ in range(2)] + [
            pltpu.SemaphoreType.DMA((2, 1)) for _ in range(2)
        ]

    def steps(self, block, out, scratch, place):
        chip, core, group = place
        send, recv, relay_send, relay_recv = scratch
        count = self.groups
        beside = {"seq": 2 * chip + 1 - core}
        relayed = count == 4

        def at(rank):
            return out.at[rank, core] if self.cores else out.at[rank]

        def near(p):
            return flip_copy(
                at(group ^ p), at(group ^ p), send.at[1, p], recv.at[1, p], beside
            )

        local_copy = pltpu.make_async_copy(block, at(group), send.at[0, count])
        local_copy.start()
        copies = {
            p: flip_copy(block, at(group), send.at[0, p], recv.at[0, p], {"dp": group ^ p})
            for p in range(1, count)
            if not (relayed and p == 3)
        }
        cores = []
        if self.cores:
            cores.append(
                flip_copy(block, at(group), send.at[1, 0], recv.at[1, 0], beside)
            )
        yield
        relays = []
        for p, copy in copies.items():
            copy.wait_recv()
            if relayed:
                first = self.value.shape[0] // 32 * 16
                rows = pl.ds(0, first) if p == 1 else pl.ds(first, self.value.shape[0] - first)
                half = at(group ^ p).at[rows]
                relays.append(
                    flip_copy(
                        half,
                        half,
                        relay_send.at[p - 1, 0],
                        relay_recv.at[p - 1, 0],
                        {"dp": group ^ (3 - p)},
                    )
                )
            if self.cores:
                cores.append(near(p))
        yield
        for copy in relays:
            copy.wait()
        if self.cores and relayed:
            cores.append(near(3))
        for copy in copies.values():
            copy.wait_send()
        yield
        for copy in cores:
            copy.wait()
        local_copy.wait()

    def finish(self, out):
        return out


class GatherDpCores(GatherDp):
    axes = ("dp", "near")
    cores = True


class Pass(Part):
    axes = ()
    alias = True

    def result(self):
        return jax.ShapeDtypeStruct(self.value.shape, self.value.dtype), pl.ANY

    def scratch(self):
        return []

    def steps(self, block, out, scratch, place):
        yield

    def finish(self, out):
        return out


def add_rows(target, sources):
    rows = target.shape[0]

    @pl.loop(0, rows // 16)
    def _(i):
        at = pl.ds(pl.multiple_of(i * 16, 16), 16)
        total = sources[0][at, :].astype(F32)
        for source in sources[1:]:
            total = total + source[at, :].astype(F32)
        target[at, :] = total.astype(target.dtype)


class ScatterSeq(Part):
    axes = ("near", "far")

    def result(self):
        return jax.ShapeDtypeStruct(self.value.shape[1:], F32), pltpu.VMEM

    def prepare(self):
        shape = self.value.shape
        return self.value.reshape((self.chips, 2) + shape[1:])

    def scratch(self):
        block = self.value.shape[1:]
        return [
            pltpu.VMEM((self.chips,) + block, BF16),
            pltpu.VMEM((self.chips,) + block, BF16),
            pltpu.VMEM((2, self.chips) + block, BF16),
            pltpu.SemaphoreType.DMA((2, self.chips)),
            pltpu.SemaphoreType.DMA((2, self.chips)),
            pltpu.SemaphoreType.DMA((2, self.chips)),
            pltpu.SemaphoreType.DMA((1,)),
        ]

    def reduce(self, partial, out, scratch, place):
        chip, core, group = place
        chips = self.chips
        mine, peer, arrived, send, recv, near, own_sem = scratch
        local_copy = pltpu.make_async_copy(partial.at[:, core], mine, own_sem.at[0])
        local_copy.start()
        order = [k for i in range(chips // 2) for k in (chips - 1 - i, i)]
        beside = {
            k: flip_copy(
                partial.at[k, 1 - core],
                peer.at[k],
                near.at[0, k],
                near.at[1, k],
                {"seq": 2 * chip + 1 - core},
            )
            for k in order
        }
        yield
        local_copy.wait()

        def pair(k):
            beside[k].wait()
            add_rows(mine.at[k], [mine.at[k], peer.at[k]])

        more = [chip + 1 < chips, chip > 0]
        onward = [{"seq": 2 * (chip + 1) + core}, {"seq": 2 * (chip - 1) + core}]
        for step in range(chips - 1):
            for way in range(2):
                to = chips - 1 - step if way == 0 else step
                ahead = chip < to if way == 0 else chip > to
                if 2 * step < chips:
                    pair(to)

                @pl.when(ahead)
                def _(way=way, to=to):
                    @pl.when(more[1 - way])
                    def _():
                        waiting(
                            arrived.at[way, to], send.at[way, to], recv.at[way, to], onward[way]
                        ).wait_recv()
                        add_rows(mine.at[to], [mine.at[to], arrived.at[way, to]])

                    flip_copy(
                        mine.at[to],
                        arrived.at[way, to],
                        send.at[way, to],
                        recv.at[way, to],
                        onward[way],
                    )

            yield
        for way in range(2):

            @pl.when(more[1 - way])
            def _(way=way):
                waiting(
                    arrived.at[way, chip], send.at[way, chip], recv.at[way, chip], onward[way]
                ).wait_recv()

        @pl.when(more[0] & more[1])
        def _():
            add_rows(out, [mine.at[chip], arrived.at[0, chip], arrived.at[1, chip]])

        for way in range(2):

            @pl.when(more[1 - way] & jnp.logical_not(more[way]))
            def _(way=way):
                add_rows(out, [mine.at[chip], arrived.at[way, chip]])

            for to in range(chips):
                ahead = chip < to if way == 0 else chip > to

                @pl.when(ahead)
                def _(way=way, to=to):
                    waiting(
                        mine.at[to], send.at[way, to], recv.at[way, to], onward[way]
                    ).wait_send()

    def steps(self, partial, out, scratch, place):
        yield from self.reduce(partial, out, scratch, place)

    def finish(self, out):
        return out


class SumSeq(ScatterSeq):
    def result(self):
        return jax.ShapeDtypeStruct((self.chips, 2) + self.value.shape[1:], BF16), pl.ANY

    def scratch(self):
        return (
            ScatterSeq.scratch(self)
            + [pltpu.VMEM(self.value.shape[1:], BF16)]
            + spread_sems(self.chips)
        )

    def steps(self, partial, out, scratch, place):
        chip, core, group = place
        total = scratch[7]
        yield from self.reduce(partial, total, scratch[:7], place)
        yield from spread_seq(total, out, scratch[8:], place, self.chips)

    def finish(self, out):
        return out.reshape(self.value.shape)


class ReduceDp(Part):
    axes = ("dp",)

    def result(self):
        return jax.ShapeDtypeStruct(self.value.shape[1:], self.value.dtype), pltpu.VMEM

    def scratch(self):
        return [
            pltpu.VMEM(self.value.shape, self.value.dtype),
            pltpu.SemaphoreType.DMA((self.groups,)),
            pltpu.SemaphoreType.DMA((self.groups,)),
        ]

    def reduce(self, value, out, scratch, place):
        chip, core, group = place
        arrived, send, recv = scratch
        local_copy = pltpu.make_async_copy(value.at[group], arrived.at[0], send.at[0])
        local_copy.start()
        copies = [
            flip_copy(value.at[group ^ p], arrived.at[p], send.at[p], recv.at[p], {"dp": group ^ p})
            for p in range(1, self.groups)
        ]
        yield
        local_copy.wait()
        for copy in copies:
            copy.wait()
        add_rows(out, [arrived.at[p] for p in range(self.groups)])

    def steps(self, value, out, scratch, place):
        yield from self.reduce(value, out, scratch, place)

    def finish(self, out):
        return out


class ReduceDpGatherSeq(ReduceDp):
    axes = ("dp", "near", "far")

    def result(self):
        shape = (self.chips, 2) + self.value.shape[1:]
        return jax.ShapeDtypeStruct(shape, self.value.dtype), pl.ANY

    def scratch(self):
        return (
            ReduceDp.scratch(self)
            + [pltpu.VMEM(self.value.shape[1:], self.value.dtype)]
            + spread_sems(self.chips)
        )

    def steps(self, value, out, scratch, place):
        chip, core, group = place
        total = scratch[3]
        yield from self.reduce(value, total, scratch[:3], place)
        yield from spread_seq(total, out, scratch[4:], place, self.chips)

    def finish(self, out):
        return out.reshape((2 * self.chips,) + self.value.shape[1:])


def communicate(number, parts, micros=50):
    values = [part.prepare() if isinstance(part, ScatterSeq) else part.value for part in parts]
    results = [part.result() for part in parts]
    scratches = [part.scratch() for part in parts]
    chips, groups = parts[0].chips, parts[0].groups
    axes = set()
    for part in parts:
        axes.update(part.axes)

    def kernel(*refs):
        ins, outs = refs[: len(parts)], refs[len(parts) : 2 * len(parts)]
        rest = list(refs[2 * len(parts) :])
        me, group = lax.axis_index("seq"), lax.axis_index("dp")
        chip, core = me // 2, lax.rem(me, 2)
        targets = []
        for m in range(1, 2 * chips):
            if "all" in axes or (m == 1 and "near" in axes) or (m % 2 == 0 and "far" in axes):
                targets.append({"seq": me ^ m})
        if "dp" in axes:
            targets += [{"dp": group ^ p} for p in range(1, groups)]
        barrier = pltpu.get_barrier_semaphore()
        for target in targets:
            pl.semaphore_signal(
                barrier, inc=1, device_id=target, device_id_type=pl.DeviceIdType.MESH
            )
        pl.semaphore_wait(barrier, len(targets))
        running = []
        for part, value, out, scratch in zip(parts, ins, outs, scratches):
            own, rest = rest[: len(scratch)], rest[len(scratch) :]
            running.append(part.steps(value, out, own, (chip, core, group)))
        while running:
            running = [steps for steps in running if next(steps, "end") != "end"]

    outs = pl.pallas_call(
        kernel,
        out_shape=[shape for shape, _ in results],
        in_specs=[pl.BlockSpec(memory_space=pl.ANY)] * len(parts),
        out_specs=[pl.BlockSpec(memory_space=space) for _, space in results],
        scratch_shapes=[item for scratch in scratches for item in scratch],
        input_output_aliases={i: i for i, part in enumerate(parts) if part.alias},
        cost_estimate=pl.CostEstimate(
            flops=0, bytes_accessed=micros * 3_000_000, transcendentals=0
        ),
        compiler_params=pltpu.CompilerParams(
            collective_id=number, has_side_effects=True, vmem_limit_bytes=48 * 1024 * 1024
        ),
    )(*values)
    return [part.finish(out) for part, out in zip(parts, outs)]


def swap_dp(value, mask):
    return lax.ppermute(value, "dp", [(i, i ^ mask) for i in range(lax.axis_size("dp"))])


def background_reduce(value):
    me = lax.axis_index("dp")
    total = lax.dynamic_index_in_dim(value, me, 0, keepdims=False).astype(F32)
    for p in range(1, lax.axis_size("dp")):
        piece = lax.dynamic_index_in_dim(value, me ^ p, 0, keepdims=False)
        total = total + swap_dp(piece, p).astype(F32)
    return total.astype(BF16)


def background_gather(value):
    return jnp.stack([value] + [swap_dp(value, p) for p in range(1, lax.axis_size("dp"))])


def background_exchange(value):
    me = lax.axis_index("dp")
    pieces = [
        lax.dynamic_index_in_dim(value, me ^ p, 0, keepdims=False)
        for p in range(lax.axis_size("dp"))
    ]
    return jnp.stack([pieces[0]] + [swap_dp(pieces[p], p) for p in range(1, len(pieces))])


def after(values, others):
    def kernel(*refs):
        del refs

    count = len(values)
    return pl.pallas_call(
        kernel,
        out_shape=[jax.ShapeDtypeStruct(v.shape, v.dtype) for v in values],
        in_specs=[pl.BlockSpec(memory_space=pl.ANY)] * (count + len(others)),
        out_specs=[pl.BlockSpec(memory_space=pl.ANY)] * count,
        input_output_aliases={i: i for i in range(count)},
        compiler_params=pltpu.CompilerParams(has_side_effects=True),
    )(*values, *others)


def joined_columns(pieces, groups, unit):
    count, rows, columns = pieces.shape
    half = columns // 2
    block = 64

    def kernel(pieces_ref, *out_refs):
        parts = [pieces_ref[rank].astype(F32) for rank in range(count)]
        for side, out_ref in enumerate(out_refs):
            out_ref[...] = jnp.concatenate(
                [
                    parts[rank][:, side * half + p * unit : side * half + (p + 1) * unit]
                    for p in range(groups)
                    for rank in range(count)
                ],
                axis=1,
            )

    shape = jax.ShapeDtypeStruct((rows, count * half), F32)
    return pl.pallas_call(
        kernel,
        grid=(rows // block,),
        out_shape=[shape, shape],
        in_specs=[pl.BlockSpec((count, block, columns), lambda i: (0, i, 0))],
        out_specs=[pl.BlockSpec((block, count * half), lambda i: (i, 0))] * 2,
        compiler_params=pltpu.CompilerParams(vmem_limit_bytes=48 * 1024 * 1024),
    )(pieces)


def padded_rows(value):
    rows = value.shape[-2]
    more = -rows % 16
    return jnp.pad(value, [(0, 0)] * (value.ndim - 2) + [(0, more), (0, 0)])


def local(
    inputs,
    segments,
    routes,
    cotangent,
    attention_gain,
    query_weight,
    latent_weight,
    latent_gain,
    expand_weight,
    output_weight,
    feedforward_gain,
    router_weight,
    shared_gate,
    shared_up,
    shared_down,
    expert_gate,
    expert_up,
    expert_down,
):
    seq_count = lax.axis_size("seq")
    dp_count = lax.axis_size("dp")
    me = lax.axis_index("seq")
    d_rank = lax.axis_index("dp")
    tokens = inputs.shape[1]
    width = inputs.shape[2]
    group = tokens * seq_count
    experts = EXP_DEV * seq_count
    heads_dev = HEADS // seq_count
    score_scale = 1.0 / math.sqrt(QK)
    shard = width // dp_count

    hq = heads_dev * QK
    hkv = heads_dev * (NOPE + VDIM)
    rank_shard = latent_gain.shape[0]
    latent_width = latent_weight.shape[1]
    small = jnp.concatenate(
        [attention_gain, feedforward_gain, latent_gain, router_weight.reshape(-1)]
    )
    fold = shard // rank_shard
    expand_part = lax.dynamic_slice_in_dim(expand_weight, me * hkv, hkv, 1)
    expand_part = (
        expand_part.reshape(rank_shard, fold, hkv // fold).transpose(1, 0, 2).reshape(shard, -1)
    )
    pack = jnp.concatenate(
        [lax.dynamic_slice_in_dim(query_weight, me * hq, hq, 1), expand_part], axis=1
    )
    pack_width = pack.shape[1]
    small_rows = -(-small.shape[0] // (16 * pack_width)) * 16
    small_pack = jnp.pad(small, (0, small_rows * pack_width - small.shape[0]))
    pack = jnp.concatenate([pack, small_pack.reshape(small_rows, pack_width)], axis=0)
    routes_pad = jnp.pad(routes[0], ((0, 0), (0, 128 - TOP))).astype(BF16)

    core = lax.rem(me, 2)

    def half_of(weight):
        rows = weight.shape[0] // 2
        return lax.dynamic_slice_in_dim(weight, core * rows, rows, 0)

    hidden = shared_gate.shape[1]
    unit = hidden // (dp_count * seq_count)
    side = dp_count * unit

    def columns_of(weight):
        return [
            lax.dynamic_slice_in_dim(weight, (p * seq_count + me) * unit, unit, 1)
            for p in range(dp_count)
        ]

    x_all, routes_all, pack, w_latent, w_output, w_sin, w_sdown, g_all = communicate(
        1,
        [
            GatherSeq(inputs[0]),
            GatherSeq(routes_pad),
            GatherDp(pack),
            GatherDpCores(half_of(latent_weight)),
            GatherDpCores(half_of(output_weight)),
            GatherDp(jnp.concatenate(columns_of(shared_gate) + columns_of(shared_up), axis=1)),
            GatherDp(padded_rows(lax.dynamic_slice_in_dim(shared_down, me * unit, unit, 0))),
            GatherSeq(cotangent[0]),
        ],
    )
    expert_gate, expert_up, expert_down = after([expert_gate, expert_up, expert_down], [x_all])
    w_egate = lax.all_gather(expert_gate, "dp", axis=1, tiled=True)
    w_eup = lax.all_gather(expert_up, "dp", axis=1, tiled=True)
    w_edown = lax.all_gather(expert_down, "dp", axis=2, tiled=True)
    w_sin = w_sin.reshape(width, 2 * side)
    w_sdown = w_sdown[:, :unit].reshape(side, width)
    g_all = g_all.reshape(group, width)
    x_all = x_all.reshape(group, width)
    w_query = pack[:, :shard, :hq].reshape(width, hq)
    w_latent = w_latent.reshape(width, latent_width)
    w_expand = (
        pack[:, :shard, hq:]
        .reshape(dp_count, fold, rank_shard, hkv // fold)
        .transpose(0, 2, 1, 3)
        .reshape(KV_RANK, hkv)
    )
    small = pack[:, shard:].reshape(dp_count, small_rows * pack_width)
    g_attn = small[:, :shard].reshape(width).astype(F32)
    g_ffn = small[:, shard : 2 * shard].reshape(width).astype(F32)
    g_latent = small[:, 2 * shard : 2 * shard + rank_shard].reshape(KV_RANK).astype(F32)
    w_router = small[:, 2 * shard + rank_shard :][:, : shard * experts].reshape(width, experts)

    routes_all = routes_all.reshape(group, 128)[:, :TOP].astype(jnp.int32)
    positions = jnp.arange(group, dtype=jnp.int32)
    seg_all = segments[0]
    cosine, sine = angles(positions, ROPE)
    my_experts = me * EXP_DEV + jnp.arange(EXP_DEV, dtype=jnp.int32)
    expert_ids = jnp.arange(experts, dtype=jnp.int32)
    hit = jnp.any(routes_all[None] == my_experts[:, None, None], axis=-1).astype(jnp.int32)
    slot = jnp.where(hit == 1, jnp.cumsum(hit, axis=1) - hit, CAP)
    route_hot = jnp.any(routes_all[:, :, None] == expert_ids[None, None, :], axis=1)
    placed = slot[:, None, :] == jnp.arange(CAP, dtype=jnp.int32)[None, :, None]
    dispatch = placed.astype(BF16).reshape(EXP_DEV * CAP, group)

    def own(value):
        return lax.dynamic_slice_in_dim(value, me * tokens, tokens, 0)

    attn_in = normalized_rows(x_all.astype(F32), g_attn).astype(BF16)
    q_raw = dot(attn_in, w_query).reshape(group, heads_dev, QK)
    latent_raw = dot(attn_in, w_latent)
    latent = latent_raw[:, :KV_RANK]
    latent_normed = normalized_rows(latent, g_latent).astype(BF16)
    key_value = dot(latent_normed, w_expand).reshape(group, heads_dev, NOPE + VDIM)
    q_full = jnp.concatenate(
        [q_raw[..., :NOPE], rotate(q_raw[..., NOPE:], cosine[:, None, :], sine[:, None, :])],
        axis=-1,
    ).astype(BF16)
    k_rot = rotate(latent_raw[:, KV_RANK:], cosine, sine)
    k_full = jnp.concatenate(
        [key_value[..., :NOPE], jnp.broadcast_to(k_rot[:, None, :], (group, heads_dev, ROPE))],
        axis=-1,
    ).astype(BF16)
    values = key_value[..., NOPE:].astype(BF16)
    visible = (seg_all[:, None] == seg_all[None, :]) & (seg_all[:, None] >= 0) & (
        positions[None, :] <= positions[:, None]
    ) | (positions[None, :] == positions[:, None])
    scores = jnp.einsum("qhd,khd->hqk", q_full, k_full, preferred_element_type=F32) * score_scale
    scores = jnp.where(visible[None], scores, MASKED)
    row_peak = jnp.max(scores, axis=-1, keepdims=True)
    exponent = jnp.exp(scores - row_peak)
    soft_float = exponent / jnp.sum(exponent, axis=-1, keepdims=True)
    soft = soft_float.astype(BF16)
    head_out = jnp.einsum("hqk,khd->qhd", soft, values, preferred_element_type=F32)
    head_out = head_out.astype(BF16).reshape(seq_count, tokens, heads_dev * VDIM)

    (head_out,) = communicate(2, [ExchangeSeq(head_out)])
    w_output = w_output.reshape(width, width)
    flat_out = jnp.swapaxes(head_out, 0, 1).reshape(tokens, HEADS * VDIM)
    x_float = inputs[0].astype(F32)
    residual = x_float + dot(flat_out, w_output)
    ffn_in = normalized_rows(residual, g_ffn).astype(BF16)

    (ffn_all,) = communicate(3, [GatherSeq(ffn_in)])
    ffn_all = ffn_all.reshape(group, width)

    router_probs = jax.nn.softmax(dot(ffn_all, w_router), axis=-1)
    chosen = jnp.where(route_hot, router_probs, 0.0)
    chosen_sum = jnp.sum(chosen, axis=-1, keepdims=True)
    gates = chosen / chosen_sum
    my_gates = lax.dynamic_slice_in_dim(gates.T, me * EXP_DEV, EXP_DEV, 0)
    gate_rows = jnp.sum(jnp.where(placed, my_gates[:, None, :], 0.0), axis=-1)

    side_in = dot(ffn_all, w_sin)
    side_gate, side_up = side_in[:, :side], side_in[:, side:]
    side_act = swiglu(side_gate, side_up).astype(BF16)
    grad_sdown = t_dot(side_act, g_all)
    d_side_act = dot_t(g_all, w_sdown)
    _, side_pull = jax.vjp(swiglu, side_gate, side_up)
    d_side_gate, d_side_up = side_pull(d_side_act)
    d_side = jnp.concatenate([d_side_gate, d_side_up], axis=1).astype(BF16)
    grad_sin = t_dot(ffn_all, d_side)
    dispatch, all_sin, all_sdown = communicate(
        5,
        [
            Pass(dispatch),
            ReduceDpGatherSeq(grad_sin.astype(BF16).reshape(dp_count, shard, 2 * side)),
            ReduceDpGatherSeq(padded_rows(grad_sdown.astype(BF16).reshape(dp_count, unit, width))),
        ],
    )

    out_sgate, out_sup = joined_columns(all_sin, dp_count, unit)
    out_sdown = all_sdown[:, :unit].reshape(hidden // dp_count, width).astype(F32)

    rows_shape = (EXP_DEV, CAP, width)
    expert_in = dot(dispatch, ffn_all).astype(BF16).reshape(rows_shape)
    hidden_gate = jnp.einsum("nmh,nhq->nmq", expert_in, w_egate, preferred_element_type=F32)
    g_rows = dot(dispatch, g_all).astype(BF16).reshape(rows_shape)
    expert_grad = (gate_rows[:, :, None] * g_rows.astype(F32)).astype(BF16)
    hidden_up = jnp.einsum("nmh,nhq->nmq", expert_in, w_eup, preferred_element_type=F32)
    expert_act = swiglu(hidden_gate, hidden_up).astype(BF16)
    grad_edown = jnp.einsum("kcf,kcd->kfd", expert_act, expert_grad, preferred_element_type=F32)
    grad_edown = grad_edown.astype(BF16)
    (g_rows,) = after([g_rows], [grad_edown, out_sgate, out_sup, out_sdown])

    d_act_plain = jnp.einsum("kcd,kfd->kcf", g_rows, w_edown, preferred_element_type=F32)
    d_gate_rows = jnp.sum(expert_act.astype(F32) * d_act_plain, axis=-1)
    _, expert_pull = jax.vjp(swiglu, hidden_gate, hidden_up)
    d_hidden_gate, d_hidden_up = expert_pull(gate_rows[:, :, None] * d_act_plain)
    d_hidden_gate = d_hidden_gate.astype(BF16)
    d_hidden_up = d_hidden_up.astype(BF16)
    grad_egate = jnp.einsum("kcd,kcf->kdf", expert_in, d_hidden_gate, preferred_element_type=F32)
    grad_eup = jnp.einsum("kcd,kcf->kdf", expert_in, d_hidden_up, preferred_element_type=F32)
    grad_egate, grad_eup = grad_egate.astype(BF16), grad_eup.astype(BF16)
    shard_edown = lax.psum_scatter(grad_edown, "dp", scatter_dimension=2, tiled=True).astype(F32)
    shard_egate = lax.psum_scatter(grad_egate, "dp", scatter_dimension=1, tiled=True).astype(F32)
    shard_eup = lax.psum_scatter(grad_eup, "dp", scatter_dimension=1, tiled=True).astype(F32)
    d_hidden_gate, d_hidden_up = after([d_hidden_gate, d_hidden_up], [grad_egate, grad_eup])
    d_expert_in = (
        jnp.einsum("sta,sra->str", d_hidden_gate, w_egate, preferred_element_type=F32)
        + jnp.einsum("sta,sra->str", d_hidden_up, w_eup, preferred_element_type=F32)
    ).astype(BF16)
    d_ffn_partial = dot_t(d_side, w_sin) + t_dot(
        dispatch, d_expert_in.reshape(EXP_DEV * CAP, width)
    )
    d_gate_own = jnp.sum(jnp.where(placed, d_gate_rows[:, :, None], 0.0), axis=1)
    mine_hot = (my_experts[:, None] == expert_ids[None, :]).astype(F32)
    d_gate_wide = jnp.sum(d_gate_own[:, :, None] * mine_hot[:, None, :], axis=0)
    d_gate_high = d_gate_wide.astype(BF16)
    d_gate_low = (d_gate_wide - d_gate_high.astype(F32)).astype(BF16)
    d_gate_pack = jnp.concatenate(
        [d_gate_high, d_gate_low, jnp.zeros((group, 128 - 2 * experts), BF16)], axis=1
    )
    d_ffn, d_gate = communicate(
        6,
        [
            ScatterSeq(d_ffn_partial.astype(BF16).reshape(seq_count, tokens, width)),
            ScatterSeq(d_gate_pack.reshape(seq_count, tokens, 128)),
        ],
    )
    d_gate = d_gate[:, :experts] + d_gate[:, experts : 2 * experts]

    (expert_act,) = after([expert_act], [d_ffn])
    expert_out = jnp.einsum("kcf,kfd->kcd", expert_act, w_edown, preferred_element_type=F32)
    expert_out = expert_out.astype(BF16).astype(F32)
    moe_rows = (gate_rows[:, :, None] * expert_out).astype(BF16).reshape(EXP_DEV * CAP, width)
    ffn_out = (dot(side_act, w_sdown) + t_dot(dispatch, moe_rows)).astype(BF16)

    own_hot = own(route_hot)
    own_probs = own(router_probs)
    own_gates = own(gates)
    d_chosen = (d_gate - jnp.sum(d_gate * own_gates, axis=-1, keepdims=True)) / own(chosen_sum)
    d_probs = jnp.where(own_hot, d_chosen, 0.0)
    d_logits = own_probs * (d_probs - jnp.sum(own_probs * d_probs, axis=-1, keepdims=True))
    grad_router = jnp.einsum("td,te->de", ffn_in.astype(F32), d_logits, precision=HIGHEST)
    d_ffn = d_ffn + jnp.einsum("te,de->td", d_logits, w_router.astype(F32), precision=HIGHEST)

    grad_out = cotangent[0].astype(F32)
    d_resid_part, grad_ffn_gain = norm_backward(residual, g_ffn, d_ffn)
    d_residual = grad_out + d_resid_part
    d_attn = d_residual.astype(BF16)
    d_head = dot_t(d_attn, w_output).astype(BF16)
    d_head = jnp.swapaxes(d_head.reshape(tokens, seq_count, heads_dev * VDIM), 0, 1)
    (head_grad,) = communicate(7, [ExchangeSeq(d_head)])
    head_grad = head_grad.reshape(group, heads_dev, VDIM)

    d_values = jnp.einsum("hqk,qhd->khd", soft, head_grad, preferred_element_type=F32).astype(BF16)
    d_prob = jnp.einsum("qhd,khd->hqk", head_grad, values, preferred_element_type=F32)
    d_score = (
        soft_float * (d_prob - jnp.sum(soft_float * d_prob, axis=-1, keepdims=True))
    ).astype(BF16)
    d_query = jnp.einsum("hqk,khd->qhd", d_score, k_full, preferred_element_type=F32)
    d_query = (d_query * score_scale).astype(BF16).astype(F32)
    d_key = jnp.einsum("hqk,qhd->khd", d_score, q_full, preferred_element_type=F32)
    d_key = (d_key * score_scale).astype(BF16)
    d_q_raw = jnp.concatenate(
        [d_query[..., :NOPE], rotate(d_query[..., NOPE:], cosine[:, None, :], -sine[:, None, :])],
        axis=-1,
    )
    d_q_raw = d_q_raw.astype(BF16).reshape(group, hq)
    d_key_value = jnp.concatenate([d_key[..., :NOPE], d_values], axis=-1).reshape(group, hkv)
    dk_rope = jnp.sum(d_key[..., NOPE:].astype(F32), axis=1)
    latent_pad = -latent_width % 128
    d_latent_part = jnp.concatenate(
        [dot_t(d_key_value, w_expand), dk_rope, jnp.zeros((group, latent_pad), F32)], axis=-1
    ).astype(BF16)
    d_attn_part = dot_t(d_q_raw, w_query).astype(BF16)
    grad_expand = t_dot(latent_normed, d_key_value).astype(BF16)
    grad_query = t_dot(attn_in, d_q_raw).astype(BF16)

    def by_group(rows):
        return jnp.swapaxes(rows.reshape(tokens, dp_count, -1), 0, 1)

    left_out = background_exchange(by_group(flat_out))
    right_out = background_gather(d_attn)
    (right_out,) = after([right_out], [d_attn_part])
    left_latent = background_exchange(by_group(own(attn_in)))
    sum_query = background_reduce(grad_query.reshape(dp_count, shard, hq))
    sum_expand = background_reduce(grad_expand.reshape(dp_count, rank_shard, hkv))
    d_latent_sum, d_attn_in, moe = communicate(
        8,
        [
            ScatterSeq(d_latent_part.reshape(seq_count, tokens, latent_width + latent_pad)),
            ScatterSeq(d_attn_part.reshape(seq_count, tokens, width)),
            ScatterSeq(ffn_out.reshape(seq_count, tokens, width)),
        ],
        micros=90,
    )
    d_k_pe = rotate(d_latent_sum[:, KV_RANK:latent_width], own(cosine), -own(sine))
    d_latent, grad_latent_gain = norm_backward(
        own(latent), g_latent, d_latent_sum[:, :KV_RANK]
    )
    d_latent_raw = jnp.concatenate([d_latent, d_k_pe], axis=-1).astype(BF16)
    d_attn_in = d_attn_in + dot_t(d_latent_raw, w_latent)
    d_x_part, grad_attn_gain = norm_backward(x_float, g_attn, d_attn_in)
    grad_inputs = d_residual + d_x_part

    all_tokens = dp_count * tokens
    grad_output = t_dot(left_out.reshape(all_tokens, shard), right_out.reshape(all_tokens, width))
    grad_output = grad_output.astype(BF16).reshape(seq_count, shard // seq_count, width)
    latent_rows = jnp.pad(d_latent_raw, ((0, 0), (0, latent_pad)))

    gains = jnp.concatenate(
        [
            grad_attn_gain.reshape(dp_count, -1),
            grad_ffn_gain.reshape(dp_count, -1),
            grad_latent_gain.reshape(dp_count, -1),
            grad_router.reshape(dp_count, -1),
        ],
        axis=1,
    )
    gain_width = gains.shape[1]
    gain_rows = -(-gain_width // (16 * 128)) * 16
    gains = jnp.pad(gains, ((0, 0), (0, gain_rows * 128 - gain_width)))

    right_latent = background_gather(latent_rows)
    grad_latent = t_dot(
        left_latent.reshape(all_tokens, shard),
        right_latent.reshape(all_tokens, -1)[:, :latent_width],
    ).astype(BF16)
    latent_blocks = jnp.pad(
        grad_latent.reshape(seq_count, shard // seq_count, latent_width),
        ((0, 0), (0, 0), (0, latent_pad)),
    )
    out_output, all_query, all_expand, out_latent, all_gains = communicate(
        9,
        [
            SumSeq(grad_output),
            GatherSeq(sum_query),
            GatherSeq(sum_expand),
            SumSeq(latent_blocks),
            ReduceDpGatherSeq(gains.reshape(dp_count, gain_rows, 128)),
        ],
    )
    layer_out = (residual + moe).astype(BF16)
    out_query = jnp.swapaxes(all_query, 0, 1).reshape(shard, HEADS * QK).astype(F32)
    out_expand = (
        jnp.swapaxes(all_expand, 0, 1).reshape(rank_shard, HEADS * (NOPE + VDIM)).astype(F32)
    )
    out_output = out_output.reshape(shard, width).astype(F32)
    out_latent = out_latent.reshape(shard, -1)[:, :latent_width].astype(F32)

    sums = jnp.sum(all_gains, axis=0).reshape(-1)
    out_attn_gain = sums[:shard]
    out_ffn_gain = sums[shard : 2 * shard]
    out_latent_gain = sums[2 * shard : 2 * shard + rank_shard]
    out_router = sums[2 * shard + rank_shard : gain_width].reshape(shard, experts)

    return (
        layer_out[None],
        grad_inputs[None],
        out_attn_gain,
        out_query,
        out_latent,
        out_latent_gain,
        out_expand,
        out_output,
        out_ffn_gain,
        out_router,
        out_sgate,
        out_sup,
        out_sdown,
        shard_egate,
        shard_eup,
        shard_edown,
    )


def solution(mesh):
    placed = (
        P("dp", "seq", None),
        P("dp", None),
        P("dp", "seq", None),
        P("dp", "seq", None),
        P("dp"),
        P("dp", None),
        P("dp", None),
        P("dp"),
        P("dp", None),
        P("dp", None),
        P("dp"),
        P("dp", None),
        P("dp", None),
        P("dp", None),
        P("dp", None),
        P("seq", "dp", None),
        P("seq", "dp", None),
        P("seq", None, "dp"),
    )
    return jax.shard_map(
        local,
        mesh=mesh,
        in_specs=placed,
        out_specs=(
            P("dp", "seq", None),
            P("dp", "seq", None),
            P("dp"),
            P("dp", None),
            P("dp", None),
            P("dp"),
            P("dp", None),
            P("dp", None),
            P("dp"),
            P("dp", None),
            P("dp", None),
            P("dp", None),
            P("dp", None),
            P("seq", "dp", None),
            P("seq", "dp", None),
            P("seq", None, "dp"),
        ),
        check_vma=False,
    )
```

```python
import math

import jax
import jax.numpy as jnp
from jax import lax
from jax.experimental import pallas as pl
from jax.experimental.pallas import tpu as pltpu
from jax.sharding import PartitionSpec as P

HEADS = 16
NOPE = 128
ROPE = 64
VDIM = 128
KV_RANK = 512
TOP = 6
EXP_DEV = 2
CAP = 480

EPSILON = 1e-06
MASKED = -1e30
HIGHEST = lax.Precision.HIGHEST
F32 = jnp.float32
BF16 = jnp.bfloat16
QK = NOPE + ROPE


def normalized_rows(values, gain):
    return values * lax.rsqrt(jnp.mean(values * values, axis=-1, keepdims=True) + EPSILON) * gain


def norm_backward(values, gain, upstream):
    scale = lax.rsqrt(jnp.mean(values * values, axis=-1, keepdims=True) + EPSILON)
    normed = values * scale
    weighted = upstream * gain
    d_values = scale * (weighted - normed * jnp.mean(weighted * normed, axis=-1, keepdims=True))
    return d_values, jnp.sum(upstream * normed, axis=0)


def angles(positions, width):
    frequency = 10000.0 ** (-(2.0 * jnp.arange(width // 2, dtype=F32)) / width)
    turned = positions.astype(F32)[:, None] * frequency[None, :]
    return (jnp.cos(turned), jnp.sin(turned))


def rotate(values, cosine, sine):
    half_width = values.shape[-1] // 2
    lower_half = values[..., :half_width]
    upper_half = values[..., half_width:]
    return jnp.concatenate(
        [lower_half * cosine - upper_half * sine, upper_half * cosine + lower_half * sine], axis=-1
    )


def swiglu(gate_portion, up_part):
    return jax.nn.silu(gate_portion) * up_part


def dot(left, right):
    return jnp.dot(left, right, preferred_element_type=F32)


def dot_t(left, right):
    return lax.dot_general(left, right, (((1,), (1,)), ((), ())), preferred_element_type=F32)


def t_dot(left, right):
    return lax.dot_general(left, right, (((0,), (0,)), ((), ())), preferred_element_type=F32)


def flip_copy(src, dst, send_sem, recv_sem, target):
    copy = pltpu.make_async_remote_copy(
        src_ref=src,
        dst_ref=dst,
        send_sem=send_sem,
        recv_sem=recv_sem,
        device_id=target,
        device_id_type=pl.DeviceIdType.MESH,
    )
    copy.start()
    return copy


def waiting(block, send_sem, recv_sem, target):
    return pltpu.make_async_remote_copy(
        src_ref=block,
        dst_ref=block,
        send_sem=send_sem,
        recv_sem=recv_sem,
        device_id=target,
        device_id_type=pl.DeviceIdType.MESH,
    )


def spread_seq(block, out, sems, place, chips):
    sends, recvs, near_send, near_recv, own_sem = sems
    chip, core, group = place
    beside = {"seq": 2 * chip + 1 - core}
    local_copy = pltpu.make_async_copy(block, out.at[chip, core], own_sem.at[0])
    local_copy.start()
    more = [chip + 1 < chips, chip > 0]
    onward = [{"seq": 2 * (chip + 1) + core}, {"seq": 2 * (chip - 1) + core}]
    for way in range(2):

        @pl.when(more[way])
        def _(way=way):
            flip_copy(
                block, out.at[chip, core], sends.at[way, 0], recvs.at[way, 0], onward[way]
            )

    flip_copy(block, out.at[chip, core], near_send.at[0, 0], near_recv.at[0, 0], beside)
    yield
    for step in range(1, chips):
        for way in range(2):
            source = chip - step if way == 0 else chip + step
            there = source >= 0 if way == 0 else source < chips

            @pl.when(there)
            def _(way=way, step=step, source=source):
                arrived = out.at[source, core]
                waiting(
                    arrived, sends.at[way, step - 1], recvs.at[way, step - 1], beside
                ).wait_recv()
                if step < chips - 1:

                    @pl.when(more[way])
                    def _():
                        flip_copy(
                            arrived,
                            arrived,
                            sends.at[way, step],
                            recvs.at[way, step],
                            onward[way],
                        )

                flip_copy(
                    arrived, arrived, near_send.at[way, step], near_recv.at[way, step], beside
                )

        yield
    own = out.at[chip, core]
    waiting(own, near_send.at[0, 0], near_recv.at[0, 0], beside).wait()
    for step in range(chips):
        for way in range(2):
            source = chip - step if way == 0 else chip + step
            there = source >= 0 if way == 0 else source < chips
            if step:

                @pl.when(there)
                def _(way=way, step=step):
                    waiting(
                        own, near_send.at[way, step], near_recv.at[way, step], beside
                    ).wait()

            if step < chips - 1:

                @pl.when(there & more[way])
                def _(way=way, step=step):
                    waiting(
                        own, sends.at[way, step], recvs.at[way, step], onward[way]
                    ).wait_send()

    local_copy.wait()


def spread_sems(chips):
    return [pltpu.SemaphoreType.DMA((2, chips)) for _ in range(4)] + [
        pltpu.SemaphoreType.DMA((1,))
    ]


class Part:
    axes = ("near", "far")
    alias = False

    def __init__(self, value):
        self.value = value
        self.chips = lax.axis_size("seq") // 2
        self.groups = lax.axis_size("dp")


class GatherSeq(Part):
    def result(self):
        shape = (self.chips, 2) + self.value.shape
        return jax.ShapeDtypeStruct(shape, self.value.dtype), pl.ANY

    def scratch(self):
        return spread_sems(self.chips)

    def steps(self, block, out, scratch, place):
        chip, core, group = place
        yield from spread_seq(block, out, scratch, place, self.chips)

    def finish(self, out):
        return out.reshape((2 * self.chips,) + self.value.shape)


class ExchangeSeq(Part):
    axes = ("near", "all")

    def result(self):
        return jax.ShapeDtypeStruct(self.value.shape, self.value.dtype), pl.ANY

    def scratch(self):
        count = 2 * self.chips
        return [pltpu.SemaphoreType.DMA((count,)), pltpu.SemaphoreType.DMA((count,))]

    def steps(self, block, out, scratch, place):
        chip, core, group = place
        send, recv = scratch
        me = 2 * chip + core
        local_copy = pltpu.make_async_copy(block.at[me], out.at[me], send.at[0])
        local_copy.start()
        copies = [
            flip_copy(block.at[me ^ m], out.at[me], send.at[m], recv.at[m], {"seq": me ^ m})
            for m in range(1, 2 * self.chips)
        ]
        yield
        for copy in copies:
            copy.wait()
        local_copy.wait()

    def finish(self, out):
        return out


class GatherDp(Part):
    axes = ("dp",)
    cores = False

    def result(self):
        lead = (self.groups, 2) if self.cores else (self.groups,)
        return jax.ShapeDtypeStruct(lead + self.value.shape, self.value.dtype), pl.ANY

    def scratch(self):
        return [pltpu.SemaphoreType.DMA((2, self.groups + 1)) for _ in range(2)] + [
            pltpu.SemaphoreType.DMA((2, 1)) for _ in range(2)
        ]

    def steps(self, block, out, scratch, place):
        chip, core, group = place
        send, recv, relay_send, relay_recv = scratch
        count = self.groups
        beside = {"seq": 2 * chip + 1 - core}
        relayed = count == 4

        def at(rank):
            return out.at[rank, core] if self.cores else out.at[rank]

        def near(p):
            return flip_copy(
                at(group ^ p), at(group ^ p), send.at[1, p], recv.at[1, p], beside
            )

        local_copy = pltpu.make_async_copy(block, at(group), send.at[0, count])
        local_copy.start()
        copies = {
            p: flip_copy(block, at(group), send.at[0, p], recv.at[0, p], {"dp": group ^ p})
            for p in range(1, count)
            if not (relayed and p == 3)
        }
        cores = []
        if self.cores:
            cores.append(
                flip_copy(block, at(group), send.at[1, 0], recv.at[1, 0], beside)
            )
        yield
        relays = []
        for p, copy in copies.items():
            copy.wait_recv()
            if relayed:
                first = self.value.shape[0] // 32 * 16
                rows = pl.ds(0, first) if p == 1 else pl.ds(first, self.value.shape[0] - first)
                half = at(group ^ p).at[rows]
                relays.append(
                    flip_copy(
                        half,
                        half,
                        relay_send.at[p - 1, 0],
                        relay_recv.at[p - 1, 0],
                        {"dp": group ^ (3 - p)},
                    )
                )
            if self.cores:
                cores.append(near(p))
        yield
        for copy in relays:
            copy.wait()
        if self.cores and relayed:
            cores.append(near(3))
        for copy in copies.values():
            copy.wait_send()
        yield
        for copy in cores:
            copy.wait()
        local_copy.wait()

    def finish(self, out):
        return out


class GatherDpCores(GatherDp):
    axes = ("dp", "near")
    cores = True


class Pass(Part):
    axes = ()
    alias = True

    def result(self):
        return jax.ShapeDtypeStruct(self.value.shape, self.value.dtype), pl.ANY

    def scratch(self):
        return []

    def steps(self, block, out, scratch, place):
        yield

    def finish(self, out):
        return out


def add_rows(target, sources):
    rows = target.shape[0]

    @pl.loop(0, rows // 16)
    def _(i):
        at = pl.ds(pl.multiple_of(i * 16, 16), 16)
        total = sources[0][at, :].astype(F32)
        for source in sources[1:]:
            total = total + source[at, :].astype(F32)
        target[at, :] = total.astype(target.dtype)


class ScatterSeq(Part):
    axes = ("near", "far")

    def result(self):
        return jax.ShapeDtypeStruct(self.value.shape[1:], F32), pltpu.VMEM

    def prepare(self):
        shape = self.value.shape
        return self.value.reshape((self.chips, 2) + shape[1:])

    def scratch(self):
        block = self.value.shape[1:]
        return [
            pltpu.VMEM((self.chips,) + block, BF16),
            pltpu.VMEM((self.chips,) + block, BF16),
            pltpu.VMEM((2, self.chips) + block, BF16),
            pltpu.SemaphoreType.DMA((2, self.chips)),
            pltpu.SemaphoreType.DMA((2, self.chips)),
            pltpu.SemaphoreType.DMA((2, self.chips)),
            pltpu.SemaphoreType.DMA((1,)),
        ]

    def reduce(self, partial, out, scratch, place):
        chip, core, group = place
        chips = self.chips
        mine, peer, arrived, send, recv, near, own_sem = scratch
        local_copy = pltpu.make_async_copy(partial.at[:, core], mine, own_sem.at[0])
        local_copy.start()
        order = [k for i in range(chips // 2) for k in (chips - 1 - i, i)]
        beside = {
            k: flip_copy(
                partial.at[k, 1 - core],
                peer.at[k],
                near.at[0, k],
                near.at[1, k],
                {"seq": 2 * chip + 1 - core},
            )
            for k in order
        }
        yield
        local_copy.wait()

        def pair(k):
            beside[k].wait()
            add_rows(mine.at[k], [mine.at[k], peer.at[k]])

        more = [chip + 1 < chips, chip > 0]
        onward = [{"seq": 2 * (chip + 1) + core}, {"seq": 2 * (chip - 1) + core}]
        for step in range(chips - 1):
            for way in range(2):
                to = chips - 1 - step if way == 0 else step
                ahead = chip < to if way == 0 else chip > to
                if 2 * step < chips:
                    pair(to)

                @pl.when(ahead)
                def _(way=way, to=to):
                    @pl.when(more[1 - way])
                    def _():
                        waiting(
                            arrived.at[way, to], send.at[way, to], recv.at[way, to], onward[way]
                        ).wait_recv()
                        add_rows(mine.at[to], [mine.at[to], arrived.at[way, to]])

                    flip_copy(
                        mine.at[to],
                        arrived.at[way, to],
                        send.at[way, to],
                        recv.at[way, to],
                        onward[way],
                    )

            yield
        for way in range(2):

            @pl.when(more[1 - way])
            def _(way=way):
                waiting(
                    arrived.at[way, chip], send.at[way, chip], recv.at[way, chip], onward[way]
                ).wait_recv()

        @pl.when(more[0] & more[1])
        def _():
            add_rows(out, [mine.at[chip], arrived.at[0, chip], arrived.at[1, chip]])

        for way in range(2):

            @pl.when(more[1 - way] & jnp.logical_not(more[way]))
            def _(way=way):
                add_rows(out, [mine.at[chip], arrived.at[way, chip]])

            for to in range(chips):
                ahead = chip < to if way == 0 else chip > to

                @pl.when(ahead)
                def _(way=way, to=to):
                    waiting(
                        mine.at[to], send.at[way, to], recv.at[way, to], onward[way]
                    ).wait_send()

    def steps(self, partial, out, scratch, place):
        yield from self.reduce(partial, out, scratch, place)

    def finish(self, out):
        return out


class SumSeq(ScatterSeq):
    def result(self):
        return jax.ShapeDtypeStruct((self.chips, 2) + self.value.shape[1:], BF16), pl.ANY

    def scratch(self):
        return (
            ScatterSeq.scratch(self)
            + [pltpu.VMEM(self.value.shape[1:], BF16)]
            + spread_sems(self.chips)
        )

    def steps(self, partial, out, scratch, place):
        chip, core, group = place
        total = scratch[7]
        yield from self.reduce(partial, total, scratch[:7], place)
        yield from spread_seq(total, out, scratch[8:], place, self.chips)

    def finish(self, out):
        return out.reshape(self.value.shape)


class ReduceDp(Part):
    axes = ("dp",)

    def result(self):
        return jax.ShapeDtypeStruct(self.value.shape[1:], self.value.dtype), pltpu.VMEM

    def scratch(self):
        return [
            pltpu.VMEM(self.value.shape, self.value.dtype),
            pltpu.SemaphoreType.DMA((self.groups,)),
            pltpu.SemaphoreType.DMA((self.groups,)),
        ]

    def reduce(self, value, out, scratch, place):
        chip, core, group = place
        arrived, send, recv = scratch
        local_copy = pltpu.make_async_copy(value.at[group], arrived.at[0], send.at[0])
        local_copy.start()
        copies = [
            flip_copy(value.at[group ^ p], arrived.at[p], send.at[p], recv.at[p], {"dp": group ^ p})
            for p in range(1, self.groups)
        ]
        yield
        local_copy.wait()
        for copy in copies:
            copy.wait()
        add_rows(out, [arrived.at[p] for p in range(self.groups)])

    def steps(self, value, out, scratch, place):
        yield from self.reduce(value, out, scratch, place)

    def finish(self, out):
        return out


class ReduceDpGatherSeq(ReduceDp):
    axes = ("dp", "near", "far")

    def result(self):
        shape = (self.chips, 2) + self.value.shape[1:]
        return jax.ShapeDtypeStruct(shape, self.value.dtype), pl.ANY

    def scratch(self):
        return (
            ReduceDp.scratch(self)
            + [pltpu.VMEM(self.value.shape[1:], self.value.dtype)]
            + spread_sems(self.chips)
        )

    def steps(self, value, out, scratch, place):
        chip, core, group = place
        total = scratch[3]
        yield from self.reduce(value, total, scratch[:3], place)
        yield from spread_seq(total, out, scratch[4:], place, self.chips)

    def finish(self, out):
        return out.reshape((2 * self.chips,) + self.value.shape[1:])


def communicate(number, parts, micros=50):
    values = [part.prepare() if isinstance(part, ScatterSeq) else part.value for part in parts]
    results = [part.result() for part in parts]
    scratches = [part.scratch() for part in parts]
    chips, groups = parts[0].chips, parts[0].groups
    axes = set()
    for part in parts:
        axes.update(part.axes)

    def kernel(*refs):
        ins, outs = refs[: len(parts)], refs[len(parts) : 2 * len(parts)]
        rest = list(refs[2 * len(parts) :])
        me, group = lax.axis_index("seq"), lax.axis_index("dp")
        chip, core = me // 2, lax.rem(me, 2)
        targets = []
        for m in range(1, 2 * chips):
            if "all" in axes or (m == 1 and "near" in axes) or (m % 2 == 0 and "far" in axes):
                targets.append({"seq": me ^ m})
        if "dp" in axes:
            targets += [{"dp": group ^ p} for p in range(1, groups)]
        barrier = pltpu.get_barrier_semaphore()
        for target in targets:
            pl.semaphore_signal(
                barrier, inc=1, device_id=target, device_id_type=pl.DeviceIdType.MESH
            )
        pl.semaphore_wait(barrier, len(targets))
        running = []
        for part, value, out, scratch in zip(parts, ins, outs, scratches):
            own, rest = rest[: len(scratch)], rest[len(scratch) :]
            running.append(part.steps(value, out, own, (chip, core, group)))
        while running:
            running = [steps for steps in running if next(steps, "end") != "end"]

    outs = pl.pallas_call(
        kernel,
        out_shape=[shape for shape, _ in results],
        in_specs=[pl.BlockSpec(memory_space=pl.ANY)] * len(parts),
        out_specs=[pl.BlockSpec(memory_space=space) for _, space in results],
        scratch_shapes=[item for scratch in scratches for item in scratch],
        input_output_aliases={i: i for i, part in enumerate(parts) if part.alias},
        cost_estimate=pl.CostEstimate(
            flops=0, bytes_accessed=micros * 3_000_000, transcendentals=0
        ),
        compiler_params=pltpu.CompilerParams(
            collective_id=number, has_side_effects=True, vmem_limit_bytes=48 * 1024 * 1024
        ),
    )(*values)
    return [part.finish(out) for part, out in zip(parts, outs)]


def swap_dp(value, mask):
    return lax.ppermute(value, "dp", [(i, i ^ mask) for i in range(lax.axis_size("dp"))])


def background_pieces(value):
    me = lax.axis_index("dp")
    groups = lax.axis_size("dp")
    pieces = [
        lax.dynamic_index_in_dim(value, me ^ p, 0, keepdims=False) for p in range(groups)
    ]
    return [pieces[0]] + [swap_dp(pieces[p], p) for p in range(1, groups)]


def sum_pieces(pieces):
    return sum([piece.astype(F32) for piece in pieces[1:]], pieces[0].astype(F32)).astype(BF16)


def background_gather(value):
    return jnp.stack([value] + [swap_dp(value, p) for p in range(1, lax.axis_size("dp"))])


def background_exchange(value):
    me = lax.axis_index("dp")
    pieces = [
        lax.dynamic_index_in_dim(value, me ^ p, 0, keepdims=False)
        for p in range(lax.axis_size("dp"))
    ]
    return jnp.stack([pieces[0]] + [swap_dp(pieces[p], p) for p in range(1, len(pieces))])


def after(values, others):
    def kernel(*refs):
        del refs

    count = len(values)
    return pl.pallas_call(
        kernel,
        out_shape=[jax.ShapeDtypeStruct(v.shape, v.dtype) for v in values],
        in_specs=[pl.BlockSpec(memory_space=pl.ANY)] * (count + len(others)),
        out_specs=[pl.BlockSpec(memory_space=pl.ANY)] * count,
        input_output_aliases={i: i for i in range(count)},
        compiler_params=pltpu.CompilerParams(has_side_effects=True),
    )(*values, *others)


def joined_columns(pieces, groups, unit):
    count, rows, columns = pieces.shape
    half = columns // 2
    block = 64

    def kernel(pieces_ref, *out_refs):
        parts = [pieces_ref[rank].astype(F32) for rank in range(count)]
        for side, out_ref in enumerate(out_refs):
            out_ref[...] = jnp.concatenate(
                [
                    parts[rank][:, side * half + p * unit : side * half + (p + 1) * unit]
                    for p in range(groups)
                    for rank in range(count)
                ],
                axis=1,
            )

    shape = jax.ShapeDtypeStruct((rows, count * half), F32)
    return pl.pallas_call(
        kernel,
        grid=(rows // block,),
        out_shape=[shape, shape],
        in_specs=[pl.BlockSpec((count, block, columns), lambda i: (0, i, 0))],
        out_specs=[pl.BlockSpec((block, count * half), lambda i: (i, 0))] * 2,
        compiler_params=pltpu.CompilerParams(vmem_limit_bytes=48 * 1024 * 1024),
    )(pieces)


def padded_rows(value):
    rows = value.shape[-2]
    more = -rows % 16
    return jnp.pad(value, [(0, 0)] * (value.ndim - 2) + [(0, more), (0, 0)])


def local(
    inputs,
    segments,
    routes,
    cotangent,
    attention_gain,
    query_weight,
    latent_weight,
    latent_gain,
    expand_weight,
    output_weight,
    feedforward_gain,
    router_weight,
    shared_gate,
    shared_up,
    shared_down,
    expert_gate,
    expert_up,
    expert_down,
):
    seq_count = lax.axis_size("seq")
    dp_count = lax.axis_size("dp")
    me = lax.axis_index("seq")
    d_rank = lax.axis_index("dp")
    tokens = inputs.shape[1]
    width = inputs.shape[2]
    group = tokens * seq_count
    experts = EXP_DEV * seq_count
    heads_dev = HEADS // seq_count
    score_scale = 1.0 / math.sqrt(QK)
    shard = width // dp_count

    hq = heads_dev * QK
    hkv = heads_dev * (NOPE + VDIM)
    rank_shard = latent_gain.shape[0]
    latent_width = latent_weight.shape[1]
    small = jnp.concatenate(
        [attention_gain, feedforward_gain, latent_gain, router_weight.reshape(-1)]
    )
    fold = shard // rank_shard
    expand_part = lax.dynamic_slice_in_dim(expand_weight, me * hkv, hkv, 1)
    expand_part = (
        expand_part.reshape(rank_shard, fold, hkv // fold).transpose(1, 0, 2).reshape(shard, -1)
    )
    pack = jnp.concatenate(
        [lax.dynamic_slice_in_dim(query_weight, me * hq, hq, 1), expand_part], axis=1
    )
    pack_width = pack.shape[1]
    small_rows = -(-small.shape[0] // (16 * pack_width)) * 16
    small_pack = jnp.pad(small, (0, small_rows * pack_width - small.shape[0]))
    pack = jnp.concatenate([pack, small_pack.reshape(small_rows, pack_width)], axis=0)
    routes_pad = jnp.pad(routes[0], ((0, 0), (0, 128 - TOP))).astype(BF16)

    core = lax.rem(me, 2)

    def half_of(weight):
        rows = weight.shape[0] // 2
        return lax.dynamic_slice_in_dim(weight, core * rows, rows, 0)

    hidden = shared_gate.shape[1]
    unit = hidden // (dp_count * seq_count)
    side = dp_count * unit

    def columns_of(weight):
        return [
            lax.dynamic_slice_in_dim(weight, (p * seq_count + me) * unit, unit, 1)
            for p in range(dp_count)
        ]

    x_all, routes_all, pack, w_latent, w_output, g_all = communicate(
        1,
        [
            GatherSeq(inputs[0]),
            GatherSeq(routes_pad),
            GatherDp(pack),
            GatherDpCores(half_of(latent_weight)),
            GatherDpCores(half_of(output_weight)),
            GatherSeq(cotangent[0]),
        ],
    )
    arrived = routes_all[0, 0, 0] >= 0
    expert_gate, expert_up, expert_down = (
        jnp.where(arrived, weight, jnp.zeros_like(weight))
        for weight in (expert_gate, expert_up, expert_down)
    )
    w_egate = lax.all_gather(expert_gate, "dp", axis=1, tiled=True)
    w_eup = lax.all_gather(expert_up, "dp", axis=1, tiled=True)
    w_edown = lax.all_gather(expert_down, "dp", axis=2, tiled=True)
    g_all = g_all.reshape(group, width)
    x_all = x_all.reshape(group, width)
    w_query = pack[:, :shard, :hq].reshape(width, hq)
    w_latent = w_latent.reshape(width, latent_width)
    w_expand = (
        pack[:, :shard, hq:]
        .reshape(dp_count, fold, rank_shard, hkv // fold)
        .transpose(0, 2, 1, 3)
        .reshape(KV_RANK, hkv)
    )
    small = pack[:, shard:].reshape(dp_count, small_rows * pack_width)
    g_attn = small[:, :shard].reshape(width).astype(F32)
    g_ffn = small[:, shard : 2 * shard].reshape(width).astype(F32)
    g_latent = small[:, 2 * shard : 2 * shard + rank_shard].reshape(KV_RANK).astype(F32)
    w_router = small[:, 2 * shard + rank_shard :][:, : shard * experts].reshape(width, experts)

    routes_all = routes_all.reshape(group, 128)[:, :TOP].astype(jnp.int32)
    positions = jnp.arange(group, dtype=jnp.int32)
    seg_all = segments[0]
    cosine, sine = angles(positions, ROPE)
    my_experts = me * EXP_DEV + jnp.arange(EXP_DEV, dtype=jnp.int32)
    expert_ids = jnp.arange(experts, dtype=jnp.int32)
    hit = jnp.any(routes_all[None] == my_experts[:, None, None], axis=-1).astype(jnp.int32)
    slot = jnp.where(hit == 1, jnp.cumsum(hit, axis=1) - hit, CAP)
    route_hot = jnp.any(routes_all[:, :, None] == expert_ids[None, None, :], axis=1)
    placed = slot[:, None, :] == jnp.arange(CAP, dtype=jnp.int32)[None, :, None]
    dispatch = placed.astype(BF16).reshape(EXP_DEV * CAP, group)

    def own(value):
        return lax.dynamic_slice_in_dim(value, me * tokens, tokens, 0)

    attn_in = normalized_rows(x_all.astype(F32), g_attn).astype(BF16)
    q_raw = dot(attn_in, w_query).reshape(group, heads_dev, QK)
    latent_raw = dot(attn_in, w_latent)
    latent = latent_raw[:, :KV_RANK]
    latent_normed = normalized_rows(latent, g_latent).astype(BF16)
    key_value = dot(latent_normed, w_expand).reshape(group, heads_dev, NOPE + VDIM)
    q_full = jnp.concatenate(
        [q_raw[..., :NOPE], rotate(q_raw[..., NOPE:], cosine[:, None, :], sine[:, None, :])],
        axis=-1,
    ).astype(BF16)
    k_rot = rotate(latent_raw[:, KV_RANK:], cosine, sine)
    k_full = jnp.concatenate(
        [key_value[..., :NOPE], jnp.broadcast_to(k_rot[:, None, :], (group, heads_dev, ROPE))],
        axis=-1,
    ).astype(BF16)
    values = key_value[..., NOPE:].astype(BF16)
    visible = (seg_all[:, None] == seg_all[None, :]) & (seg_all[:, None] >= 0) & (
        positions[None, :] <= positions[:, None]
    ) | (positions[None, :] == positions[:, None])
    scores = jnp.einsum("qhd,khd->hqk", q_full, k_full, preferred_element_type=F32) * score_scale
    scores = jnp.where(visible[None], scores, MASKED)
    row_peak = jnp.max(scores, axis=-1, keepdims=True)
    exponent = jnp.exp(scores - row_peak)
    soft_float = exponent / jnp.sum(exponent, axis=-1, keepdims=True)
    soft = soft_float.astype(BF16)
    head_out = jnp.einsum("hqk,khd->qhd", soft, values, preferred_element_type=F32)
    head_out = head_out.astype(BF16).reshape(seq_count, tokens, heads_dev * VDIM)

    (head_out,) = communicate(2, [ExchangeSeq(head_out)])
    w_output = w_output.reshape(width, width)
    flat_out = jnp.swapaxes(head_out, 0, 1).reshape(tokens, HEADS * VDIM)
    x_float = inputs[0].astype(F32)
    residual = x_float + dot(flat_out, w_output)
    ffn_in = normalized_rows(residual, g_ffn).astype(BF16)

    ffn_all, w_sin, w_sdown = communicate(
        3,
        [
            GatherSeq(ffn_in),
            GatherDp(jnp.concatenate(columns_of(shared_gate) + columns_of(shared_up), axis=1)),
            GatherDp(padded_rows(lax.dynamic_slice_in_dim(shared_down, me * unit, unit, 0))),
        ],
    )
    w_sin = w_sin.reshape(width, 2 * side)
    w_sdown = w_sdown[:, :unit].reshape(side, width)
    ffn_all = ffn_all.reshape(group, width)

    router_probs = jax.nn.softmax(dot(ffn_all, w_router), axis=-1)
    chosen = jnp.where(route_hot, router_probs, 0.0)
    chosen_sum = jnp.sum(chosen, axis=-1, keepdims=True)
    gates = chosen / chosen_sum
    my_gates = lax.dynamic_slice_in_dim(gates.T, me * EXP_DEV, EXP_DEV, 0)
    gate_rows = jnp.sum(jnp.where(placed, my_gates[:, None, :], 0.0), axis=-1)

    side_in = dot(ffn_all, w_sin)
    side_gate, side_up = side_in[:, :side], side_in[:, side:]
    side_act = swiglu(side_gate, side_up).astype(BF16)
    grad_sdown = t_dot(side_act, g_all)
    d_side_act = dot_t(g_all, w_sdown)
    _, side_pull = jax.vjp(swiglu, side_gate, side_up)
    d_side_gate, d_side_up = side_pull(d_side_act)
    d_side = jnp.concatenate([d_side_gate, d_side_up], axis=1).astype(BF16)
    grad_sin = t_dot(ffn_all, d_side)
    dispatch, all_sin, all_sdown = communicate(
        5,
        [
            Pass(dispatch),
            ReduceDpGatherSeq(grad_sin.astype(BF16).reshape(dp_count, shard, 2 * side)),
            ReduceDpGatherSeq(padded_rows(grad_sdown.astype(BF16).reshape(dp_count, unit, width))),
        ],
    )

    out_sgate, out_sup = joined_columns(all_sin, dp_count, unit)
    out_sdown = all_sdown[:, :unit].reshape(hidden // dp_count, width).astype(F32)

    rows_shape = (EXP_DEV, CAP, width)
    expert_in = dot(dispatch, ffn_all).astype(BF16).reshape(rows_shape)
    hidden_gate = jnp.einsum("nmh,nhq->nmq", expert_in, w_egate, preferred_element_type=F32)
    g_rows = dot(dispatch, g_all).astype(BF16).reshape(rows_shape)
    expert_grad = (gate_rows[:, :, None] * g_rows.astype(F32)).astype(BF16)
    hidden_up = jnp.einsum("nmh,nhq->nmq", expert_in, w_eup, preferred_element_type=F32)
    expert_act = swiglu(hidden_gate, hidden_up).astype(BF16)
    grad_edown = jnp.einsum("kcf,kcd->kfd", expert_act, expert_grad, preferred_element_type=F32)
    grad_edown = grad_edown.astype(BF16)
    (g_rows,) = after([g_rows], [grad_edown, out_sgate, out_sup, out_sdown])

    d_act_plain = jnp.einsum("kcd,kfd->kcf", g_rows, w_edown, preferred_element_type=F32)
    d_act_plain = lax.optimization_barrier(d_act_plain)
    d_gate_rows = jnp.sum(expert_act.astype(F32) * d_act_plain, axis=-1)
    _, expert_pull = jax.vjp(swiglu, hidden_gate, hidden_up)
    d_hidden_gate, d_hidden_up = expert_pull(gate_rows[:, :, None] * d_act_plain)
    d_hidden_gate = d_hidden_gate.astype(BF16)
    d_hidden_up = d_hidden_up.astype(BF16)
    grad_egate = jnp.einsum("kcd,kcf->kdf", expert_in, d_hidden_gate, preferred_element_type=F32)
    grad_eup = jnp.einsum("kcd,kcf->kdf", expert_in, d_hidden_up, preferred_element_type=F32)
    grad_egate, grad_eup = grad_egate.astype(BF16), grad_eup.astype(BF16)
    shard_edown = lax.psum_scatter(grad_edown, "dp", scatter_dimension=2, tiled=True).astype(F32)
    shard_egate = lax.psum_scatter(grad_egate, "dp", scatter_dimension=1, tiled=True).astype(F32)
    shard_eup = lax.psum_scatter(grad_eup, "dp", scatter_dimension=1, tiled=True).astype(F32)
    d_hidden_gate, d_hidden_up = after([d_hidden_gate, d_hidden_up], [grad_egate, grad_eup])
    d_expert_in = (
        jnp.einsum("sta,sra->str", d_hidden_gate, w_egate, preferred_element_type=F32)
        + jnp.einsum("sta,sra->str", d_hidden_up, w_eup, preferred_element_type=F32)
    ).astype(BF16)
    d_ffn_partial = dot_t(d_side, w_sin) + t_dot(
        dispatch, d_expert_in.reshape(EXP_DEV * CAP, width)
    )
    d_gate_own = jnp.sum(jnp.where(placed, d_gate_rows[:, :, None], 0.0), axis=1)
    mine_hot = (my_experts[:, None] == expert_ids[None, :]).astype(F32)
    d_gate_wide = jnp.sum(d_gate_own[:, :, None] * mine_hot[:, None, :], axis=0)
    d_gate_high = d_gate_wide.astype(BF16)
    d_gate_low = (d_gate_wide - d_gate_high.astype(F32)).astype(BF16)
    d_gate_pack = jnp.concatenate(
        [d_gate_high, d_gate_low, jnp.zeros((group, 128 - 2 * experts), BF16)], axis=1
    )
    d_ffn, d_gate = communicate(
        6,
        [
            ScatterSeq(d_ffn_partial.astype(BF16).reshape(seq_count, tokens, width)),
            ScatterSeq(d_gate_pack.reshape(seq_count, tokens, 128)),
        ],
    )
    d_gate = d_gate[:, :experts] + d_gate[:, experts : 2 * experts]

    (expert_act,) = after([expert_act], [d_ffn])
    expert_out = jnp.einsum("kcf,kfd->kcd", expert_act, w_edown, preferred_element_type=F32)
    expert_out = expert_out.astype(BF16).astype(F32)
    moe_rows = (gate_rows[:, :, None] * expert_out).astype(BF16).reshape(EXP_DEV * CAP, width)
    ffn_out = (dot(side_act, w_sdown) + t_dot(dispatch, moe_rows)).astype(BF16)

    own_hot = own(route_hot)
    own_probs = own(router_probs)
    own_gates = own(gates)
    d_chosen = (d_gate - jnp.sum(d_gate * own_gates, axis=-1, keepdims=True)) / own(chosen_sum)
    d_probs = jnp.where(own_hot, d_chosen, 0.0)
    d_logits = own_probs * (d_probs - jnp.sum(own_probs * d_probs, axis=-1, keepdims=True))
    grad_router = jnp.einsum("td,te->de", ffn_in.astype(F32), d_logits, precision=HIGHEST)
    d_ffn = d_ffn + jnp.einsum("te,de->td", d_logits, w_router.astype(F32), precision=HIGHEST)

    grad_out = cotangent[0].astype(F32)
    d_resid_part, grad_ffn_gain = norm_backward(residual, g_ffn, d_ffn)
    d_residual = grad_out + d_resid_part
    d_attn = d_residual.astype(BF16)
    d_head = dot_t(d_attn, w_output).astype(BF16)
    d_head = jnp.swapaxes(d_head.reshape(tokens, seq_count, heads_dev * VDIM), 0, 1)
    (head_grad,) = communicate(7, [ExchangeSeq(d_head)])
    head_grad = head_grad.reshape(group, heads_dev, VDIM)

    d_values = jnp.einsum("hqk,qhd->khd", soft, head_grad, preferred_element_type=F32).astype(BF16)
    d_prob = jnp.einsum("qhd,khd->hqk", head_grad, values, preferred_element_type=F32)
    d_score = (
        soft_float * (d_prob - jnp.sum(soft_float * d_prob, axis=-1, keepdims=True))
    ).astype(BF16)
    d_query = jnp.einsum("hqk,khd->qhd", d_score, k_full, preferred_element_type=F32)
    d_query = (d_query * score_scale).astype(BF16).astype(F32)
    d_key = jnp.einsum("hqk,qhd->khd", d_score, q_full, preferred_element_type=F32)
    d_key = (d_key * score_scale).astype(BF16)
    d_q_raw = jnp.concatenate(
        [d_query[..., :NOPE], rotate(d_query[..., NOPE:], cosine[:, None, :], -sine[:, None, :])],
        axis=-1,
    )
    d_q_raw = d_q_raw.astype(BF16).reshape(group, hq)
    d_key_value = jnp.concatenate([d_key[..., :NOPE], d_values], axis=-1).reshape(group, hkv)
    dk_rope = jnp.sum(d_key[..., NOPE:].astype(F32), axis=1)
    latent_pad = -latent_width % 128
    d_latent_part = jnp.concatenate(
        [dot_t(d_key_value, w_expand), dk_rope, jnp.zeros((group, latent_pad), F32)], axis=-1
    ).astype(BF16)
    d_attn_part = dot_t(d_q_raw, w_query).astype(BF16)
    grad_expand = t_dot(latent_normed, d_key_value).astype(BF16)
    grad_query = t_dot(attn_in, d_q_raw).astype(BF16)

    def by_group(rows):
        return jnp.swapaxes(rows.reshape(tokens, dp_count, -1), 0, 1)

    left_out = background_exchange(by_group(flat_out))
    right_out = background_gather(d_attn)
    right_out, d_attn_part = after([right_out, d_attn_part], [left_out])
    left_latent = background_exchange(by_group(own(attn_in)))
    query_pieces = background_pieces(grad_query.reshape(dp_count, shard, hq))
    expand_pieces = background_pieces(grad_expand.reshape(dp_count, rank_shard, hkv))
    d_latent_sum, d_attn_in, moe = communicate(
        8,
        [
            ScatterSeq(d_latent_part.reshape(seq_count, tokens, latent_width + latent_pad)),
            ScatterSeq(d_attn_part.reshape(seq_count, tokens, width)),
            ScatterSeq(ffn_out.reshape(seq_count, tokens, width)),
        ],
        micros=90,
    )
    query_pieces[0], expand_pieces[0] = after([query_pieces[0], expand_pieces[0]], [d_attn_in])
    sum_query, sum_expand = sum_pieces(query_pieces), sum_pieces(expand_pieces)
    d_k_pe = rotate(d_latent_sum[:, KV_RANK:latent_width], own(cosine), -own(sine))
    d_latent, grad_latent_gain = norm_backward(
        own(latent), g_latent, d_latent_sum[:, :KV_RANK]
    )
    d_latent_raw = jnp.concatenate([d_latent, d_k_pe], axis=-1).astype(BF16)
    d_attn_in = d_attn_in + dot_t(d_latent_raw, w_latent)
    d_x_part, grad_attn_gain = norm_backward(x_float, g_attn, d_attn_in)
    grad_inputs = d_residual + d_x_part

    all_tokens = dp_count * tokens
    grad_output = t_dot(left_out.reshape(all_tokens, shard), right_out.reshape(all_tokens, width))
    grad_output = grad_output.astype(BF16).reshape(seq_count, shard // seq_count, width)
    latent_rows = jnp.pad(d_latent_raw, ((0, 0), (0, latent_pad)))

    gains = jnp.concatenate(
        [
            grad_attn_gain.reshape(dp_count, -1),
            grad_ffn_gain.reshape(dp_count, -1),
            grad_latent_gain.reshape(dp_count, -1),
            grad_router.reshape(dp_count, -1),
        ],
        axis=1,
    )
    gain_width = gains.shape[1]
    gain_rows = -(-gain_width // (16 * 128)) * 16
    gains = jnp.pad(gains, ((0, 0), (0, gain_rows * 128 - gain_width)))

    right_latent = background_gather(latent_rows)
    grad_latent = t_dot(
        left_latent.reshape(all_tokens, shard),
        right_latent.reshape(all_tokens, -1)[:, :latent_width],
    ).astype(BF16)
    latent_blocks = jnp.pad(
        grad_latent.reshape(seq_count, shard // seq_count, latent_width),
        ((0, 0), (0, 0), (0, latent_pad)),
    )
    out_output, all_query, all_expand, out_latent, all_gains = communicate(
        9,
        [
            SumSeq(grad_output),
            GatherSeq(sum_query),
            GatherSeq(sum_expand),
            SumSeq(latent_blocks),
            ReduceDpGatherSeq(gains.reshape(dp_count, gain_rows, 128)),
        ],
    )
    layer_out = (residual + moe).astype(BF16)
    out_query = jnp.swapaxes(all_query, 0, 1).reshape(shard, HEADS * QK).astype(F32)
    out_expand = (
        jnp.swapaxes(all_expand, 0, 1).reshape(rank_shard, HEADS * (NOPE + VDIM)).astype(F32)
    )
    out_output = out_output.reshape(shard, width).astype(F32)
    out_latent = out_latent.reshape(shard, -1)[:, :latent_width].astype(F32)

    sums = jnp.sum(all_gains, axis=0).reshape(-1)
    out_attn_gain = sums[:shard]
    out_ffn_gain = sums[shard : 2 * shard]
    out_latent_gain = sums[2 * shard : 2 * shard + rank_shard]
    out_router = sums[2 * shard + rank_shard : gain_width].reshape(shard, experts)

    return (
        layer_out[None],
        grad_inputs[None],
        out_attn_gain,
        out_query,
        out_latent,
        out_latent_gain,
        out_expand,
        out_output,
        out_ffn_gain,
        out_router,
        out_sgate,
        out_sup,
        out_sdown,
        shard_egate,
        shard_eup,
        shard_edown,
    )


def solution(mesh):
    placed = (
        P("dp", "seq", None),
        P("dp", None),
        P("dp", "seq", None),
        P("dp", "seq", None),
        P("dp"),
        P("dp", None),
        P("dp", None),
        P("dp"),
        P("dp", None),
        P("dp", None),
        P("dp"),
        P("dp", None),
        P("dp", None),
        P("dp", None),
        P("dp", None),
        P("seq", "dp", None),
        P("seq", "dp", None),
        P("seq", None, "dp"),
    )
    return jax.shard_map(
        local,
        mesh=mesh,
        in_specs=placed,
        out_specs=(
            P("dp", "seq", None),
            P("dp", "seq", None),
            P("dp"),
            P("dp", None),
            P("dp", None),
            P("dp"),
            P("dp", None),
            P("dp", None),
            P("dp"),
            P("dp", None),
            P("dp", None),
            P("dp", None),
            P("dp", None),
            P("seq", "dp", None),
            P("seq", "dp", None),
            P("seq", None, "dp"),
        ),
        check_vma=False,
    )
```

```python
import math

import jax
import jax.numpy as jnp
from jax import lax
from jax.experimental import pallas as pl
from jax.experimental.pallas import tpu as pltpu
from jax.sharding import PartitionSpec as P

HEADS = 16
NOPE = 128
ROPE = 64
VDIM = 128
KV_RANK = 512
TOP = 6
EXP_DEV = 2
CAP = 480

EPSILON = 1e-06
MASKED = -1e30
HIGHEST = lax.Precision.HIGHEST
F32 = jnp.float32
BF16 = jnp.bfloat16
QK = NOPE + ROPE


def normalized_rows(values, gain):
    return values * lax.rsqrt(jnp.mean(values * values, axis=-1, keepdims=True) + EPSILON) * gain


def norm_backward(values, gain, upstream):
    scale = lax.rsqrt(jnp.mean(values * values, axis=-1, keepdims=True) + EPSILON)
    normed = values * scale
    weighted = upstream * gain
    d_values = scale * (weighted - normed * jnp.mean(weighted * normed, axis=-1, keepdims=True))
    return d_values, jnp.sum(upstream * normed, axis=0)


def angles(positions, width):
    frequency = 10000.0 ** (-(2.0 * jnp.arange(width // 2, dtype=F32)) / width)
    turned = positions.astype(F32)[:, None] * frequency[None, :]
    return (jnp.cos(turned), jnp.sin(turned))


def rotate(values, cosine, sine):
    half_width = values.shape[-1] // 2
    lower_half = values[..., :half_width]
    upper_half = values[..., half_width:]
    return jnp.concatenate(
        [lower_half * cosine - upper_half * sine, upper_half * cosine + lower_half * sine], axis=-1
    )


def swiglu(gate_portion, up_part):
    return jax.nn.silu(gate_portion) * up_part


def dot(left, right):
    return jnp.dot(left, right, preferred_element_type=F32)


def dot_t(left, right):
    return lax.dot_general(left, right, (((1,), (1,)), ((), ())), preferred_element_type=F32)


def t_dot(left, right):
    return lax.dot_general(left, right, (((0,), (0,)), ((), ())), preferred_element_type=F32)


def flip_copy(src, dst, send_sem, recv_sem, target):
    copy = pltpu.make_async_remote_copy(
        src_ref=src,
        dst_ref=dst,
        send_sem=send_sem,
        recv_sem=recv_sem,
        device_id=target,
        device_id_type=pl.DeviceIdType.MESH,
    )
    copy.start()
    return copy


def waiting(block, send_sem, recv_sem, target):
    return pltpu.make_async_remote_copy(
        src_ref=block,
        dst_ref=block,
        send_sem=send_sem,
        recv_sem=recv_sem,
        device_id=target,
        device_id_type=pl.DeviceIdType.MESH,
    )


def spread_seq(block, out, sems, place, chips):
    sends, recvs, near_send, near_recv, own_sem = sems
    chip, core, group = place
    beside = {"seq": 2 * chip + 1 - core}
    local_copy = pltpu.make_async_copy(block, out.at[chip, core], own_sem.at[0])
    local_copy.start()
    more = [chip + 1 < chips, chip > 0]
    onward = [{"seq": 2 * (chip + 1) + core}, {"seq": 2 * (chip - 1) + core}]
    for way in range(2):

        @pl.when(more[way])
        def _(way=way):
            flip_copy(
                block, out.at[chip, core], sends.at[way, 0], recvs.at[way, 0], onward[way]
            )

    flip_copy(block, out.at[chip, core], near_send.at[0, 0], near_recv.at[0, 0], beside)
    yield
    for step in range(1, chips):
        for way in range(2):
            source = chip - step if way == 0 else chip + step
            there = source >= 0 if way == 0 else source < chips

            @pl.when(there)
            def _(way=way, step=step, source=source):
                arrived = out.at[source, core]
                waiting(
                    arrived, sends.at[way, step - 1], recvs.at[way, step - 1], beside
                ).wait_recv()
                if step < chips - 1:

                    @pl.when(more[way])
                    def _():
                        flip_copy(
                            arrived,
                            arrived,
                            sends.at[way, step],
                            recvs.at[way, step],
                            onward[way],
                        )

                flip_copy(
                    arrived, arrived, near_send.at[way, step], near_recv.at[way, step], beside
                )

        yield
    own = out.at[chip, core]
    waiting(own, near_send.at[0, 0], near_recv.at[0, 0], beside).wait()
    for step in range(chips):
        for way in range(2):
            source = chip - step if way == 0 else chip + step
            there = source >= 0 if way == 0 else source < chips
            if step:

                @pl.when(there)
                def _(way=way, step=step):
                    waiting(
                        own, near_send.at[way, step], near_recv.at[way, step], beside
                    ).wait()

            if step < chips - 1:

                @pl.when(there & more[way])
                def _(way=way, step=step):
                    waiting(
                        own, sends.at[way, step], recvs.at[way, step], onward[way]
                    ).wait_send()

    local_copy.wait()


def spread_sems(chips):
    return [pltpu.SemaphoreType.DMA((2, chips)) for _ in range(4)] + [
        pltpu.SemaphoreType.DMA((1,))
    ]


class Part:
    axes = ("near", "far")
    alias = False

    def __init__(self, value):
        self.value = value
        self.chips = lax.axis_size("seq") // 2
        self.groups = lax.axis_size("dp")


class GatherSeq(Part):
    def result(self):
        shape = (self.chips, 2) + self.value.shape
        return jax.ShapeDtypeStruct(shape, self.value.dtype), pl.ANY

    def scratch(self):
        return spread_sems(self.chips)

    def steps(self, block, out, scratch, place):
        chip, core, group = place
        yield from spread_seq(block, out, scratch, place, self.chips)

    def finish(self, out):
        return out.reshape((2 * self.chips,) + self.value.shape)


class ExchangeSeq(Part):
    axes = ("near", "all")

    def result(self):
        return jax.ShapeDtypeStruct(self.value.shape, self.value.dtype), pl.ANY

    def scratch(self):
        count = 2 * self.chips
        return [pltpu.SemaphoreType.DMA((count,)), pltpu.SemaphoreType.DMA((count,))]

    def steps(self, block, out, scratch, place):
        chip, core, group = place
        send, recv = scratch
        me = 2 * chip + core
        local_copy = pltpu.make_async_copy(block.at[me], out.at[me], send.at[0])
        local_copy.start()
        copies = [
            flip_copy(block.at[me ^ m], out.at[me], send.at[m], recv.at[m], {"seq": me ^ m})
            for m in range(1, 2 * self.chips)
        ]
        yield
        for copy in copies:
            copy.wait()
        local_copy.wait()

    def finish(self, out):
        return out


class GatherDp(Part):
    axes = ("dp",)
    cores = False

    def result(self):
        lead = (self.groups, 2) if self.cores else (self.groups,)
        return jax.ShapeDtypeStruct(lead + self.value.shape, self.value.dtype), pl.ANY

    def scratch(self):
        return [pltpu.SemaphoreType.DMA((2, self.groups + 1)) for _ in range(2)] + [
            pltpu.SemaphoreType.DMA((2, 1)) for _ in range(2)
        ]

    def steps(self, block, out, scratch, place):
        chip, core, group = place
        send, recv, relay_send, relay_recv = scratch
        count = self.groups
        beside = {"seq": 2 * chip + 1 - core}
        relayed = count == 4

        def at(rank):
            return out.at[rank, core] if self.cores else out.at[rank]

        def near(p):
            return flip_copy(
                at(group ^ p), at(group ^ p), send.at[1, p], recv.at[1, p], beside
            )

        local_copy = pltpu.make_async_copy(block, at(group), send.at[0, count])
        local_copy.start()
        copies = {
            p: flip_copy(block, at(group), send.at[0, p], recv.at[0, p], {"dp": group ^ p})
            for p in range(1, count)
            if not (relayed and p == 3)
        }
        cores = []
        if self.cores:
            cores.append(
                flip_copy(block, at(group), send.at[1, 0], recv.at[1, 0], beside)
            )
        yield
        relays = []
        for p, copy in copies.items():
            copy.wait_recv()
            if relayed:
                first = self.value.shape[0] // 32 * 16
                rows = pl.ds(0, first) if p == 1 else pl.ds(first, self.value.shape[0] - first)
                half = at(group ^ p).at[rows]
                relays.append(
                    flip_copy(
                        half,
                        half,
                        relay_send.at[p - 1, 0],
                        relay_recv.at[p - 1, 0],
                        {"dp": group ^ (3 - p)},
                    )
                )
            if self.cores:
                cores.append(near(p))
        yield
        for copy in relays:
            copy.wait()
        if self.cores and relayed:
            cores.append(near(3))
        for copy in copies.values():
            copy.wait_send()
        yield
        for copy in cores:
            copy.wait()
        local_copy.wait()

    def finish(self, out):
        return out


class GatherDpCores(GatherDp):
    axes = ("dp", "near")
    cores = True


class Pass(Part):
    axes = ()
    alias = True

    def result(self):
        return jax.ShapeDtypeStruct(self.value.shape, self.value.dtype), pl.ANY

    def scratch(self):
        return []

    def steps(self, block, out, scratch, place):
        yield

    def finish(self, out):
        return out


class ExchangeDp(Part):
    axes = ("dp",)

    def result(self):
        return jax.ShapeDtypeStruct(self.value.shape, self.value.dtype), pl.ANY

    def scratch(self):
        return [pltpu.SemaphoreType.DMA((self.groups,)) for _ in range(2)]

    def steps(self, block, out, scratch, place):
        chip, core, group = place
        send, recv = scratch
        local_copy = pltpu.make_async_copy(block.at[group], out.at[group], send.at[0])
        local_copy.start()
        copies = [
            flip_copy(block.at[group ^ p], out.at[group], send.at[p], recv.at[p], {"dp": group ^ p})
            for p in range(1, self.groups)
        ]
        yield
        for copy in copies:
            copy.wait()
        local_copy.wait()

    def finish(self, out):
        return out


def add_rows(target, sources):
    rows = target.shape[0]

    @pl.loop(0, rows // 16)
    def _(i):
        at = pl.ds(pl.multiple_of(i * 16, 16), 16)
        total = sources[0][at, :].astype(F32)
        for source in sources[1:]:
            total = total + source[at, :].astype(F32)
        target[at, :] = total.astype(target.dtype)


class ScatterSeq(Part):
    axes = ("near", "far")

    def result(self):
        return jax.ShapeDtypeStruct(self.value.shape[1:], F32), pltpu.VMEM

    def prepare(self):
        shape = self.value.shape
        return self.value.reshape((self.chips, 2) + shape[1:])

    def scratch(self):
        block = self.value.shape[1:]
        return [
            pltpu.VMEM((self.chips,) + block, BF16),
            pltpu.VMEM((self.chips,) + block, BF16),
            pltpu.VMEM((2, self.chips) + block, BF16),
            pltpu.SemaphoreType.DMA((2, self.chips)),
            pltpu.SemaphoreType.DMA((2, self.chips)),
            pltpu.SemaphoreType.DMA((2, self.chips)),
            pltpu.SemaphoreType.DMA((1,)),
        ]

    def reduce(self, partial, out, scratch, place):
        chip, core, group = place
        chips = self.chips
        mine, peer, arrived, send, recv, near, own_sem = scratch
        local_copy = pltpu.make_async_copy(partial.at[:, core], mine, own_sem.at[0])
        local_copy.start()
        order = [k for i in range(chips // 2) for k in (chips - 1 - i, i)]
        beside = {
            k: flip_copy(
                partial.at[k, 1 - core],
                peer.at[k],
                near.at[0, k],
                near.at[1, k],
                {"seq": 2 * chip + 1 - core},
            )
            for k in order
        }
        yield
        local_copy.wait()

        def pair(k):
            beside[k].wait()
            add_rows(mine.at[k], [mine.at[k], peer.at[k]])

        more = [chip + 1 < chips, chip > 0]
        onward = [{"seq": 2 * (chip + 1) + core}, {"seq": 2 * (chip - 1) + core}]
        for step in range(chips - 1):
            for way in range(2):
                to = chips - 1 - step if way == 0 else step
                ahead = chip < to if way == 0 else chip > to
                if 2 * step < chips:
                    pair(to)

                @pl.when(ahead)
                def _(way=way, to=to):
                    @pl.when(more[1 - way])
                    def _():
                        waiting(
                            arrived.at[way, to], send.at[way, to], recv.at[way, to], onward[way]
                        ).wait_recv()
                        add_rows(mine.at[to], [mine.at[to], arrived.at[way, to]])

                    flip_copy(
                        mine.at[to],
                        arrived.at[way, to],
                        send.at[way, to],
                        recv.at[way, to],
                        onward[way],
                    )

            yield
        for way in range(2):

            @pl.when(more[1 - way])
            def _(way=way):
                waiting(
                    arrived.at[way, chip], send.at[way, chip], recv.at[way, chip], onward[way]
                ).wait_recv()

        @pl.when(more[0] & more[1])
        def _():
            add_rows(out, [mine.at[chip], arrived.at[0, chip], arrived.at[1, chip]])

        for way in range(2):

            @pl.when(more[1 - way] & jnp.logical_not(more[way]))
            def _(way=way):
                add_rows(out, [mine.at[chip], arrived.at[way, chip]])

            for to in range(chips):
                ahead = chip < to if way == 0 else chip > to

                @pl.when(ahead)
                def _(way=way, to=to):
                    waiting(
                        mine.at[to], send.at[way, to], recv.at[way, to], onward[way]
                    ).wait_send()

    def steps(self, partial, out, scratch, place):
        yield from self.reduce(partial, out, scratch, place)

    def finish(self, out):
        return out


class SumSeq(ScatterSeq):
    def result(self):
        return jax.ShapeDtypeStruct((self.chips, 2) + self.value.shape[1:], BF16), pl.ANY

    def scratch(self):
        return (
            ScatterSeq.scratch(self)
            + [pltpu.VMEM(self.value.shape[1:], BF16)]
            + spread_sems(self.chips)
        )

    def steps(self, partial, out, scratch, place):
        chip, core, group = place
        total = scratch[7]
        yield from self.reduce(partial, total, scratch[:7], place)
        yield from spread_seq(total, out, scratch[8:], place, self.chips)

    def finish(self, out):
        return out.reshape(self.value.shape)


class ReduceDp(Part):
    axes = ("dp",)

    def result(self):
        return jax.ShapeDtypeStruct(self.value.shape[1:], self.value.dtype), pltpu.VMEM

    def scratch(self):
        return [
            pltpu.VMEM(self.value.shape, self.value.dtype),
            pltpu.SemaphoreType.DMA((self.groups,)),
            pltpu.SemaphoreType.DMA((self.groups,)),
        ]

    def reduce(self, value, out, scratch, place):
        chip, core, group = place
        arrived, send, recv = scratch
        local_copy = pltpu.make_async_copy(value.at[group], arrived.at[0], send.at[0])
        local_copy.start()
        copies = [
            flip_copy(value.at[group ^ p], arrived.at[p], send.at[p], recv.at[p], {"dp": group ^ p})
            for p in range(1, self.groups)
        ]
        yield
        local_copy.wait()
        for copy in copies:
            copy.wait()
        add_rows(out, [arrived.at[p] for p in range(self.groups)])

    def steps(self, value, out, scratch, place):
        yield from self.reduce(value, out, scratch, place)

    def finish(self, out):
        return out


class ReduceDpGatherSeq(ReduceDp):
    axes = ("dp", "near", "far")

    def result(self):
        shape = (self.chips, 2) + self.value.shape[1:]
        return jax.ShapeDtypeStruct(shape, self.value.dtype), pl.ANY

    def scratch(self):
        return (
            ReduceDp.scratch(self)
            + [pltpu.VMEM(self.value.shape[1:], self.value.dtype)]
            + spread_sems(self.chips)
        )

    def steps(self, value, out, scratch, place):
        chip, core, group = place
        total = scratch[3]
        yield from self.reduce(value, total, scratch[:3], place)
        yield from spread_seq(total, out, scratch[4:], place, self.chips)

    def finish(self, out):
        return out.reshape((2 * self.chips,) + self.value.shape[1:])


def communicate(number, parts, micros=50):
    values = [part.prepare() if isinstance(part, ScatterSeq) else part.value for part in parts]
    results = [part.result() for part in parts]
    scratches = [part.scratch() for part in parts]
    chips, groups = parts[0].chips, parts[0].groups
    axes = set()
    for part in parts:
        axes.update(part.axes)

    def kernel(*refs):
        ins, outs = refs[: len(parts)], refs[len(parts) : 2 * len(parts)]
        rest = list(refs[2 * len(parts) :])
        me, group = lax.axis_index("seq"), lax.axis_index("dp")
        chip, core = me // 2, lax.rem(me, 2)
        targets = []
        for m in range(1, 2 * chips):
            if "all" in axes or (m == 1 and "near" in axes) or (m % 2 == 0 and "far" in axes):
                targets.append({"seq": me ^ m})
        if "dp" in axes:
            targets += [{"dp": group ^ p} for p in range(1, groups)]
        barrier = pltpu.get_barrier_semaphore()
        for target in targets:
            pl.semaphore_signal(
                barrier, inc=1, device_id=target, device_id_type=pl.DeviceIdType.MESH
            )
        pl.semaphore_wait(barrier, len(targets))
        running = []
        for part, value, out, scratch in zip(parts, ins, outs, scratches):
            own, rest = rest[: len(scratch)], rest[len(scratch) :]
            running.append(part.steps(value, out, own, (chip, core, group)))
        while running:
            running = [steps for steps in running if next(steps, "end") != "end"]

    outs = pl.pallas_call(
        kernel,
        out_shape=[shape for shape, _ in results],
        in_specs=[pl.BlockSpec(memory_space=pl.ANY)] * len(parts),
        out_specs=[pl.BlockSpec(memory_space=space) for _, space in results],
        scratch_shapes=[item for scratch in scratches for item in scratch],
        input_output_aliases={i: i for i, part in enumerate(parts) if part.alias},
        cost_estimate=pl.CostEstimate(
            flops=0, bytes_accessed=micros * 3_000_000, transcendentals=0
        ),
        compiler_params=pltpu.CompilerParams(
            collective_id=number, has_side_effects=True, vmem_limit_bytes=48 * 1024 * 1024
        ),
    )(*values)
    return [part.finish(out) for part, out in zip(parts, outs)]


def swap_dp(value, mask):
    return lax.ppermute(value, "dp", [(i, i ^ mask) for i in range(lax.axis_size("dp"))])


def background_pieces(value):
    me = lax.axis_index("dp")
    groups = lax.axis_size("dp")
    pieces = [
        lax.dynamic_index_in_dim(value, me ^ p, 0, keepdims=False) for p in range(groups)
    ]
    return [pieces[0]] + [swap_dp(pieces[p], p) for p in range(1, groups)]


def sum_pieces(pieces):
    return sum([piece.astype(F32) for piece in pieces[1:]], pieces[0].astype(F32)).astype(BF16)


def background_gather(value):
    return jnp.stack([value] + [swap_dp(value, p) for p in range(1, lax.axis_size("dp"))])


def own_first(value):
    me = lax.axis_index("dp")
    return jnp.stack(
        [
            lax.dynamic_index_in_dim(value, me ^ p, 0, keepdims=False)
            for p in range(lax.axis_size("dp"))
        ]
    )


def after(values, others):
    def kernel(*refs):
        del refs

    count = len(values)
    return pl.pallas_call(
        kernel,
        out_shape=[jax.ShapeDtypeStruct(v.shape, v.dtype) for v in values],
        in_specs=[pl.BlockSpec(memory_space=pl.ANY)] * (count + len(others)),
        out_specs=[pl.BlockSpec(memory_space=pl.ANY)] * count,
        input_output_aliases={i: i for i in range(count)},
        compiler_params=pltpu.CompilerParams(has_side_effects=True),
    )(*values, *others)


def joined_columns(pieces, groups, unit):
    count, rows, columns = pieces.shape
    half = columns // 2
    block = 64

    def kernel(pieces_ref, *out_refs):
        parts = [pieces_ref[rank].astype(F32) for rank in range(count)]
        for side, out_ref in enumerate(out_refs):
            out_ref[...] = jnp.concatenate(
                [
                    parts[rank][:, side * half + p * unit : side * half + (p + 1) * unit]
                    for p in range(groups)
                    for rank in range(count)
                ],
                axis=1,
            )

    shape = jax.ShapeDtypeStruct((rows, count * half), F32)
    return pl.pallas_call(
        kernel,
        grid=(rows // block,),
        out_shape=[shape, shape],
        in_specs=[pl.BlockSpec((count, block, columns), lambda i: (0, i, 0))],
        out_specs=[pl.BlockSpec((block, count * half), lambda i: (i, 0))] * 2,
        compiler_params=pltpu.CompilerParams(vmem_limit_bytes=48 * 1024 * 1024),
    )(pieces)


def padded_rows(value):
    rows = value.shape[-2]
    more = -rows % 16
    return jnp.pad(value, [(0, 0)] * (value.ndim - 2) + [(0, more), (0, 0)])


def local(
    inputs,
    segments,
    routes,
    cotangent,
    attention_gain,
    query_weight,
    latent_weight,
    latent_gain,
    expand_weight,
    output_weight,
    feedforward_gain,
    router_weight,
    shared_gate,
    shared_up,
    shared_down,
    expert_gate,
    expert_up,
    expert_down,
):
    seq_count = lax.axis_size("seq")
    dp_count = lax.axis_size("dp")
    me = lax.axis_index("seq")
    d_rank = lax.axis_index("dp")
    tokens = inputs.shape[1]
    width = inputs.shape[2]
    group = tokens * seq_count
    experts = EXP_DEV * seq_count
    heads_dev = HEADS // seq_count
    score_scale = 1.0 / math.sqrt(QK)
    shard = width // dp_count

    hq = heads_dev * QK
    hkv = heads_dev * (NOPE + VDIM)
    rank_shard = latent_gain.shape[0]
    latent_width = latent_weight.shape[1]
    small = jnp.concatenate(
        [attention_gain, feedforward_gain, latent_gain, router_weight.reshape(-1)]
    )
    fold = shard // rank_shard
    expand_part = lax.dynamic_slice_in_dim(expand_weight, me * hkv, hkv, 1)
    expand_part = (
        expand_part.reshape(rank_shard, fold, hkv // fold).transpose(1, 0, 2).reshape(shard, -1)
    )
    pack = jnp.concatenate(
        [lax.dynamic_slice_in_dim(query_weight, me * hq, hq, 1), expand_part], axis=1
    )
    pack_width = pack.shape[1]
    small_rows = -(-small.shape[0] // (16 * pack_width)) * 16
    small_pack = jnp.pad(small, (0, small_rows * pack_width - small.shape[0]))
    pack = jnp.concatenate([pack, small_pack.reshape(small_rows, pack_width)], axis=0)
    routes_pad = jnp.pad(routes[0], ((0, 0), (0, 128 - TOP))).astype(BF16)

    core = lax.rem(me, 2)

    def half_of(weight):
        rows = weight.shape[0] // 2
        return lax.dynamic_slice_in_dim(weight, core * rows, rows, 0)

    hidden = shared_gate.shape[1]
    unit = hidden // (dp_count * seq_count)
    side = dp_count * unit

    def columns_of(weight):
        return [
            lax.dynamic_slice_in_dim(weight, (p * seq_count + me) * unit, unit, 1)
            for p in range(dp_count)
        ]

    x_all, routes_all, pack, w_latent, w_output, g_all = communicate(
        1,
        [
            GatherSeq(inputs[0]),
            GatherSeq(routes_pad),
            GatherDp(pack),
            GatherDpCores(half_of(latent_weight)),
            GatherDpCores(half_of(output_weight)),
            GatherSeq(cotangent[0]),
        ],
    )
    arrived = routes_all[0, 0, 0] >= 0
    expert_gate, expert_up, expert_down = (
        jnp.where(arrived, weight, jnp.zeros_like(weight))
        for weight in (expert_gate, expert_up, expert_down)
    )
    w_egate = lax.all_gather(expert_gate, "dp", axis=1, tiled=True)
    w_eup = lax.all_gather(expert_up, "dp", axis=1, tiled=True)
    w_edown = lax.all_gather(expert_down, "dp", axis=2, tiled=True)
    g_all = g_all.reshape(group, width)
    x_all = x_all.reshape(group, width)
    w_query = pack[:, :shard, :hq].reshape(width, hq)
    w_latent = w_latent.reshape(width, latent_width)
    w_expand = (
        pack[:, :shard, hq:]
        .reshape(dp_count, fold, rank_shard, hkv // fold)
        .transpose(0, 2, 1, 3)
        .reshape(KV_RANK, hkv)
    )
    small = pack[:, shard:].reshape(dp_count, small_rows * pack_width)
    g_attn = small[:, :shard].reshape(width).astype(F32)
    g_ffn = small[:, shard : 2 * shard].reshape(width).astype(F32)
    g_latent = small[:, 2 * shard : 2 * shard + rank_shard].reshape(KV_RANK).astype(F32)
    w_router = small[:, 2 * shard + rank_shard :][:, : shard * experts].reshape(width, experts)

    routes_all = routes_all.reshape(group, 128)[:, :TOP].astype(jnp.int32)
    positions = jnp.arange(group, dtype=jnp.int32)
    seg_all = segments[0]
    cosine, sine = angles(positions, ROPE)
    my_experts = me * EXP_DEV + jnp.arange(EXP_DEV, dtype=jnp.int32)
    expert_ids = jnp.arange(experts, dtype=jnp.int32)
    hit = jnp.any(routes_all[None] == my_experts[:, None, None], axis=-1).astype(jnp.int32)
    slot = jnp.where(hit == 1, jnp.cumsum(hit, axis=1) - hit, CAP)
    route_hot = jnp.any(routes_all[:, :, None] == expert_ids[None, None, :], axis=1)
    placed = slot[:, None, :] == jnp.arange(CAP, dtype=jnp.int32)[None, :, None]
    dispatch = placed.astype(BF16).reshape(EXP_DEV * CAP, group)

    def own(value):
        return lax.dynamic_slice_in_dim(value, me * tokens, tokens, 0)

    attn_in = normalized_rows(x_all.astype(F32), g_attn).astype(BF16)
    q_raw = dot(attn_in, w_query).reshape(group, heads_dev, QK)
    latent_raw = dot(attn_in, w_latent)
    latent = latent_raw[:, :KV_RANK]
    latent_normed = normalized_rows(latent, g_latent).astype(BF16)
    key_value = dot(latent_normed, w_expand).reshape(group, heads_dev, NOPE + VDIM)
    q_full = jnp.concatenate(
        [q_raw[..., :NOPE], rotate(q_raw[..., NOPE:], cosine[:, None, :], sine[:, None, :])],
        axis=-1,
    ).astype(BF16)
    k_rot = rotate(latent_raw[:, KV_RANK:], cosine, sine)
    k_full = jnp.concatenate(
        [key_value[..., :NOPE], jnp.broadcast_to(k_rot[:, None, :], (group, heads_dev, ROPE))],
        axis=-1,
    ).astype(BF16)
    values = key_value[..., NOPE:].astype(BF16)
    visible = (seg_all[:, None] == seg_all[None, :]) & (seg_all[:, None] >= 0) & (
        positions[None, :] <= positions[:, None]
    ) | (positions[None, :] == positions[:, None])
    scores = jnp.einsum("qhd,khd->hqk", q_full, k_full, preferred_element_type=F32) * score_scale
    scores = jnp.where(visible[None], scores, MASKED)
    row_peak = jnp.max(scores, axis=-1, keepdims=True)
    exponent = jnp.exp(scores - row_peak)
    soft_float = exponent / jnp.sum(exponent, axis=-1, keepdims=True)
    soft = soft_float.astype(BF16)
    head_out = jnp.einsum("hqk,khd->qhd", soft, values, preferred_element_type=F32)
    head_out = head_out.astype(BF16).reshape(seq_count, tokens, heads_dev * VDIM)

    (head_out,) = communicate(2, [ExchangeSeq(head_out)])
    w_output = w_output.reshape(width, width)
    flat_out = jnp.swapaxes(head_out, 0, 1).reshape(tokens, HEADS * VDIM)
    x_float = inputs[0].astype(F32)
    residual = x_float + dot(flat_out, w_output)
    ffn_in = normalized_rows(residual, g_ffn).astype(BF16)

    ffn_all, w_sin, w_sdown = communicate(
        3,
        [
            GatherSeq(ffn_in),
            GatherDp(jnp.concatenate(columns_of(shared_gate) + columns_of(shared_up), axis=1)),
            GatherDp(padded_rows(lax.dynamic_slice_in_dim(shared_down, me * unit, unit, 0))),
        ],
    )
    w_sin = w_sin.reshape(width, 2 * side)
    w_sdown = w_sdown[:, :unit].reshape(side, width)
    ffn_all = ffn_all.reshape(group, width)

    router_probs = jax.nn.softmax(dot(ffn_all, w_router), axis=-1)
    chosen = jnp.where(route_hot, router_probs, 0.0)
    chosen_sum = jnp.sum(chosen, axis=-1, keepdims=True)
    gates = chosen / chosen_sum
    my_gates = lax.dynamic_slice_in_dim(gates.T, me * EXP_DEV, EXP_DEV, 0)
    gate_rows = jnp.sum(jnp.where(placed, my_gates[:, None, :], 0.0), axis=-1)

    side_in = dot(ffn_all, w_sin)
    side_gate, side_up = side_in[:, :side], side_in[:, side:]
    side_act = swiglu(side_gate, side_up).astype(BF16)
    grad_sdown = t_dot(side_act, g_all)
    d_side_act = dot_t(g_all, w_sdown)
    _, side_pull = jax.vjp(swiglu, side_gate, side_up)
    d_side_gate, d_side_up = side_pull(d_side_act)
    d_side = jnp.concatenate([d_side_gate, d_side_up], axis=1).astype(BF16)
    grad_sin = t_dot(ffn_all, d_side)
    dispatch, all_sin, all_sdown = communicate(
        5,
        [
            Pass(dispatch),
            ReduceDpGatherSeq(grad_sin.astype(BF16).reshape(dp_count, shard, 2 * side)),
            ReduceDpGatherSeq(padded_rows(grad_sdown.astype(BF16).reshape(dp_count, unit, width))),
        ],
    )

    out_sgate, out_sup = joined_columns(all_sin, dp_count, unit)
    out_sdown = all_sdown[:, :unit].reshape(hidden // dp_count, width).astype(F32)

    rows_shape = (EXP_DEV, CAP, width)
    expert_in = dot(dispatch, ffn_all).astype(BF16).reshape(rows_shape)
    hidden_gate = jnp.einsum("nmh,nhq->nmq", expert_in, w_egate, preferred_element_type=F32)
    g_rows = dot(dispatch, g_all).astype(BF16).reshape(rows_shape)
    expert_grad = (gate_rows[:, :, None] * g_rows.astype(F32)).astype(BF16)
    hidden_up = jnp.einsum("nmh,nhq->nmq", expert_in, w_eup, preferred_element_type=F32)
    expert_act = swiglu(hidden_gate, hidden_up).astype(BF16)
    grad_edown = jnp.einsum("kcf,kcd->kfd", expert_act, expert_grad, preferred_element_type=F32)
    grad_edown = grad_edown.astype(BF16)
    (g_rows,) = after([g_rows], [grad_edown, out_sgate, out_sup, out_sdown])

    d_act_plain = jnp.einsum("kcd,kfd->kcf", g_rows, w_edown, preferred_element_type=F32)
    d_act_plain = lax.optimization_barrier(d_act_plain)
    d_gate_rows = jnp.sum(expert_act.astype(F32) * d_act_plain, axis=-1)
    _, expert_pull = jax.vjp(swiglu, hidden_gate, hidden_up)
    d_hidden_gate, d_hidden_up = expert_pull(gate_rows[:, :, None] * d_act_plain)
    d_hidden_gate = d_hidden_gate.astype(BF16)
    d_hidden_up = d_hidden_up.astype(BF16)
    grad_egate = jnp.einsum("kcd,kcf->kdf", expert_in, d_hidden_gate, preferred_element_type=F32)
    grad_eup = jnp.einsum("kcd,kcf->kdf", expert_in, d_hidden_up, preferred_element_type=F32)
    grad_egate, grad_eup = grad_egate.astype(BF16), grad_eup.astype(BF16)
    shard_edown = lax.psum_scatter(grad_edown, "dp", scatter_dimension=2, tiled=True).astype(F32)
    shard_egate = lax.psum_scatter(grad_egate, "dp", scatter_dimension=1, tiled=True).astype(F32)
    shard_eup = lax.psum_scatter(grad_eup, "dp", scatter_dimension=1, tiled=True).astype(F32)
    d_hidden_gate, d_hidden_up = after([d_hidden_gate, d_hidden_up], [grad_egate, grad_eup])
    d_expert_in = (
        jnp.einsum("sta,sra->str", d_hidden_gate, w_egate, preferred_element_type=F32)
        + jnp.einsum("sta,sra->str", d_hidden_up, w_eup, preferred_element_type=F32)
    ).astype(BF16)
    d_ffn_partial = dot_t(d_side, w_sin) + t_dot(
        dispatch, d_expert_in.reshape(EXP_DEV * CAP, width)
    )
    d_gate_own = jnp.sum(jnp.where(placed, d_gate_rows[:, :, None], 0.0), axis=1)
    mine_hot = (my_experts[:, None] == expert_ids[None, :]).astype(F32)
    d_gate_wide = jnp.sum(d_gate_own[:, :, None] * mine_hot[:, None, :], axis=0)
    d_gate_high = d_gate_wide.astype(BF16)
    d_gate_low = (d_gate_wide - d_gate_high.astype(F32)).astype(BF16)
    d_gate_pack = jnp.concatenate(
        [d_gate_high, d_gate_low, jnp.zeros((group, 128 - 2 * experts), BF16)], axis=1
    )
    def by_group(rows):
        return jnp.swapaxes(rows.reshape(tokens, dp_count, -1), 0, 1)

    d_ffn, d_gate, left_out, left_latent = communicate(
        6,
        [
            ScatterSeq(d_ffn_partial.astype(BF16).reshape(seq_count, tokens, width)),
            ScatterSeq(d_gate_pack.reshape(seq_count, tokens, 128)),
            ExchangeDp(by_group(flat_out)),
            ExchangeDp(by_group(own(attn_in))),
        ],
    )
    d_gate = d_gate[:, :experts] + d_gate[:, experts : 2 * experts]

    (expert_act,) = after([expert_act], [d_ffn])
    expert_out = jnp.einsum("kcf,kfd->kcd", expert_act, w_edown, preferred_element_type=F32)
    expert_out = expert_out.astype(BF16).astype(F32)
    moe_rows = (gate_rows[:, :, None] * expert_out).astype(BF16).reshape(EXP_DEV * CAP, width)
    ffn_out = (dot(side_act, w_sdown) + t_dot(dispatch, moe_rows)).astype(BF16)

    own_hot = own(route_hot)
    own_probs = own(router_probs)
    own_gates = own(gates)
    d_chosen = (d_gate - jnp.sum(d_gate * own_gates, axis=-1, keepdims=True)) / own(chosen_sum)
    d_probs = jnp.where(own_hot, d_chosen, 0.0)
    d_logits = own_probs * (d_probs - jnp.sum(own_probs * d_probs, axis=-1, keepdims=True))
    grad_router = jnp.einsum("td,te->de", ffn_in.astype(F32), d_logits, precision=HIGHEST)
    d_ffn = d_ffn + jnp.einsum("te,de->td", d_logits, w_router.astype(F32), precision=HIGHEST)

    grad_out = cotangent[0].astype(F32)
    d_resid_part, grad_ffn_gain = norm_backward(residual, g_ffn, d_ffn)
    d_residual = grad_out + d_resid_part
    d_attn = d_residual.astype(BF16)
    d_head = dot_t(d_attn, w_output).astype(BF16)
    d_head = jnp.swapaxes(d_head.reshape(tokens, seq_count, heads_dev * VDIM), 0, 1)
    (head_grad,) = communicate(7, [ExchangeSeq(d_head)])
    head_grad = head_grad.reshape(group, heads_dev, VDIM)

    d_values = jnp.einsum("hqk,qhd->khd", soft, head_grad, preferred_element_type=F32).astype(BF16)
    d_prob = jnp.einsum("qhd,khd->hqk", head_grad, values, preferred_element_type=F32)
    d_score = (
        soft_float * (d_prob - jnp.sum(soft_float * d_prob, axis=-1, keepdims=True))
    ).astype(BF16)
    d_query = jnp.einsum("hqk,khd->qhd", d_score, k_full, preferred_element_type=F32)
    d_query = (d_query * score_scale).astype(BF16).astype(F32)
    d_key = jnp.einsum("hqk,qhd->khd", d_score, q_full, preferred_element_type=F32)
    d_key = (d_key * score_scale).astype(BF16)
    d_q_raw = jnp.concatenate(
        [d_query[..., :NOPE], rotate(d_query[..., NOPE:], cosine[:, None, :], -sine[:, None, :])],
        axis=-1,
    )
    d_q_raw = d_q_raw.astype(BF16).reshape(group, hq)
    d_key_value = jnp.concatenate([d_key[..., :NOPE], d_values], axis=-1).reshape(group, hkv)
    dk_rope = jnp.sum(d_key[..., NOPE:].astype(F32), axis=1)
    latent_pad = -latent_width % 128
    d_latent_part = jnp.concatenate(
        [dot_t(d_key_value, w_expand), dk_rope, jnp.zeros((group, latent_pad), F32)], axis=-1
    ).astype(BF16)
    d_attn_part = dot_t(d_q_raw, w_query).astype(BF16)
    grad_expand = t_dot(latent_normed, d_key_value).astype(BF16)
    grad_query = t_dot(attn_in, d_q_raw).astype(BF16)

    left_out, left_latent = own_first(left_out), own_first(left_latent)
    right_out = background_gather(d_attn)
    right_out, d_attn_part = after([right_out, d_attn_part], [left_out])
    query_pieces = background_pieces(grad_query.reshape(dp_count, shard, hq))
    expand_pieces = background_pieces(grad_expand.reshape(dp_count, rank_shard, hkv))
    d_latent_sum, d_attn_in, moe = communicate(
        8,
        [
            ScatterSeq(d_latent_part.reshape(seq_count, tokens, latent_width + latent_pad)),
            ScatterSeq(d_attn_part.reshape(seq_count, tokens, width)),
            ScatterSeq(ffn_out.reshape(seq_count, tokens, width)),
        ],
        micros=90,
    )
    query_pieces[0], expand_pieces[0] = after([query_pieces[0], expand_pieces[0]], [d_attn_in])
    sum_query, sum_expand = sum_pieces(query_pieces), sum_pieces(expand_pieces)
    d_k_pe = rotate(d_latent_sum[:, KV_RANK:latent_width], own(cosine), -own(sine))
    d_latent, grad_latent_gain = norm_backward(
        own(latent), g_latent, d_latent_sum[:, :KV_RANK]
    )
    d_latent_raw = jnp.concatenate([d_latent, d_k_pe], axis=-1).astype(BF16)
    d_attn_in = d_attn_in + dot_t(d_latent_raw, w_latent)
    d_x_part, grad_attn_gain = norm_backward(x_float, g_attn, d_attn_in)
    grad_inputs = d_residual + d_x_part

    all_tokens = dp_count * tokens
    grad_output = t_dot(left_out.reshape(all_tokens, shard), right_out.reshape(all_tokens, width))
    grad_output = grad_output.astype(BF16).reshape(seq_count, shard // seq_count, width)
    latent_rows = jnp.pad(d_latent_raw, ((0, 0), (0, latent_pad)))

    gains = jnp.concatenate(
        [
            grad_attn_gain.reshape(dp_count, -1),
            grad_ffn_gain.reshape(dp_count, -1),
            grad_latent_gain.reshape(dp_count, -1),
            grad_router.reshape(dp_count, -1),
        ],
        axis=1,
    )
    gain_width = gains.shape[1]
    gain_rows = -(-gain_width // (16 * 128)) * 16
    gains = jnp.pad(gains, ((0, 0), (0, gain_rows * 128 - gain_width)))

    right_latent = background_gather(latent_rows)
    grad_latent = t_dot(
        left_latent.reshape(all_tokens, shard),
        right_latent.reshape(all_tokens, -1)[:, :latent_width],
    ).astype(BF16)
    latent_blocks = jnp.pad(
        grad_latent.reshape(seq_count, shard // seq_count, latent_width),
        ((0, 0), (0, 0), (0, latent_pad)),
    )
    out_output, all_query, all_expand, out_latent, all_gains = communicate(
        9,
        [
            SumSeq(grad_output),
            GatherSeq(sum_query),
            GatherSeq(sum_expand),
            SumSeq(latent_blocks),
            ReduceDpGatherSeq(gains.reshape(dp_count, gain_rows, 128)),
        ],
    )
    layer_out = (residual + moe).astype(BF16)
    out_query = jnp.swapaxes(all_query, 0, 1).reshape(shard, HEADS * QK).astype(F32)
    out_expand = (
        jnp.swapaxes(all_expand, 0, 1).reshape(rank_shard, HEADS * (NOPE + VDIM)).astype(F32)
    )
    out_output = out_output.reshape(shard, width).astype(F32)
    out_latent = out_latent.reshape(shard, -1)[:, :latent_width].astype(F32)

    sums = jnp.sum(all_gains, axis=0).reshape(-1)
    out_attn_gain = sums[:shard]
    out_ffn_gain = sums[shard : 2 * shard]
    out_latent_gain = sums[2 * shard : 2 * shard + rank_shard]
    out_router = sums[2 * shard + rank_shard : gain_width].reshape(shard, experts)

    return (
        layer_out[None],
        grad_inputs[None],
        out_attn_gain,
        out_query,
        out_latent,
        out_latent_gain,
        out_expand,
        out_output,
        out_ffn_gain,
        out_router,
        out_sgate,
        out_sup,
        out_sdown,
        shard_egate,
        shard_eup,
        shard_edown,
    )


def solution(mesh):
    placed = (
        P("dp", "seq", None),
        P("dp", None),
        P("dp", "seq", None),
        P("dp", "seq", None),
        P("dp"),
        P("dp", None),
        P("dp", None),
        P("dp"),
        P("dp", None),
        P("dp", None),
        P("dp"),
        P("dp", None),
        P("dp", None),
        P("dp", None),
        P("dp", None),
        P("seq", "dp", None),
        P("seq", "dp", None),
        P("seq", None, "dp"),
    )
    return jax.shard_map(
        local,
        mesh=mesh,
        in_specs=placed,
        out_specs=(
            P("dp", "seq", None),
            P("dp", "seq", None),
            P("dp"),
            P("dp", None),
            P("dp", None),
            P("dp"),
            P("dp", None),
            P("dp", None),
            P("dp"),
            P("dp", None),
            P("dp", None),
            P("dp", None),
            P("dp", None),
            P("seq", "dp", None),
            P("seq", "dp", None),
            P("seq", None, "dp"),
        ),
        check_vma=False,
    )
```

```python
import math

import jax
import jax.numpy as jnp
from jax import lax
from jax.experimental import pallas as pl
from jax.experimental.pallas import tpu as pltpu
from jax.sharding import PartitionSpec as P

HEADS = 16
NOPE = 128
ROPE = 64
VDIM = 128
KV_RANK = 512
TOP = 6
EXP_DEV = 2
CAP = 480

EPSILON = 1e-06
MASKED = -1e30
HIGHEST = lax.Precision.HIGHEST
F32 = jnp.float32
BF16 = jnp.bfloat16
QK = NOPE + ROPE


def normalized_rows(values, gain):
    return values * lax.rsqrt(jnp.mean(values * values, axis=-1, keepdims=True) + EPSILON) * gain


def norm_backward(values, gain, upstream):
    scale = lax.rsqrt(jnp.mean(values * values, axis=-1, keepdims=True) + EPSILON)
    normed = values * scale
    weighted = upstream * gain
    d_values = scale * (weighted - normed * jnp.mean(weighted * normed, axis=-1, keepdims=True))
    return d_values, jnp.sum(upstream * normed, axis=0)


def angles(positions, width):
    frequency = 10000.0 ** (-(2.0 * jnp.arange(width // 2, dtype=F32)) / width)
    turned = positions.astype(F32)[:, None] * frequency[None, :]
    return (jnp.cos(turned), jnp.sin(turned))


def rotate(values, cosine, sine):
    half_width = values.shape[-1] // 2
    lower_half = values[..., :half_width]
    upper_half = values[..., half_width:]
    return jnp.concatenate(
        [lower_half * cosine - upper_half * sine, upper_half * cosine + lower_half * sine], axis=-1
    )


def swiglu(gate_portion, up_part):
    return jax.nn.silu(gate_portion) * up_part


def dot(left, right):
    return jnp.dot(left, right, preferred_element_type=F32)


def dot_t(left, right):
    return lax.dot_general(left, right, (((1,), (1,)), ((), ())), preferred_element_type=F32)


def t_dot(left, right):
    return lax.dot_general(left, right, (((0,), (0,)), ((), ())), preferred_element_type=F32)


def flip_copy(src, dst, send_sem, recv_sem, target):
    copy = pltpu.make_async_remote_copy(
        src_ref=src,
        dst_ref=dst,
        send_sem=send_sem,
        recv_sem=recv_sem,
        device_id=target,
        device_id_type=pl.DeviceIdType.MESH,
    )
    copy.start()
    return copy


def waiting(block, send_sem, recv_sem, target):
    return pltpu.make_async_remote_copy(
        src_ref=block,
        dst_ref=block,
        send_sem=send_sem,
        recv_sem=recv_sem,
        device_id=target,
        device_id_type=pl.DeviceIdType.MESH,
    )


def spread_seq(block, out, sems, place, chips):
    sends, recvs, near_send, near_recv, own_sem = sems
    chip, core, group = place
    beside = {"seq": 2 * chip + 1 - core}
    local_copy = pltpu.make_async_copy(block, out.at[chip, core], own_sem.at[0])
    local_copy.start()
    more = [chip + 1 < chips, chip > 0]
    onward = [{"seq": 2 * (chip + 1) + core}, {"seq": 2 * (chip - 1) + core}]
    for way in range(2):

        @pl.when(more[way])
        def _(way=way):
            flip_copy(
                block, out.at[chip, core], sends.at[way, 0], recvs.at[way, 0], onward[way]
            )

    flip_copy(block, out.at[chip, core], near_send.at[0, 0], near_recv.at[0, 0], beside)
    yield
    for step in range(1, chips):
        for way in range(2):
            source = chip - step if way == 0 else chip + step
            there = source >= 0 if way == 0 else source < chips

            @pl.when(there)
            def _(way=way, step=step, source=source):
                arrived = out.at[source, core]
                waiting(
                    arrived, sends.at[way, step - 1], recvs.at[way, step - 1], beside
                ).wait_recv()
                if step < chips - 1:

                    @pl.when(more[way])
                    def _():
                        flip_copy(
                            arrived,
                            arrived,
                            sends.at[way, step],
                            recvs.at[way, step],
                            onward[way],
                        )

                flip_copy(
                    arrived, arrived, near_send.at[way, step], near_recv.at[way, step], beside
                )

        yield
    own = out.at[chip, core]
    waiting(own, near_send.at[0, 0], near_recv.at[0, 0], beside).wait()
    for step in range(chips):
        for way in range(2):
            source = chip - step if way == 0 else chip + step
            there = source >= 0 if way == 0 else source < chips
            if step:

                @pl.when(there)
                def _(way=way, step=step):
                    waiting(
                        own, near_send.at[way, step], near_recv.at[way, step], beside
                    ).wait()

            if step < chips - 1:

                @pl.when(there & more[way])
                def _(way=way, step=step):
                    waiting(
                        own, sends.at[way, step], recvs.at[way, step], onward[way]
                    ).wait_send()

    local_copy.wait()


def spread_sems(chips):
    return [pltpu.SemaphoreType.DMA((2, chips)) for _ in range(4)] + [
        pltpu.SemaphoreType.DMA((1,))
    ]


class Part:
    axes = ("near", "far")
    alias = False

    def __init__(self, value):
        self.value = value
        self.chips = lax.axis_size("seq") // 2
        self.groups = lax.axis_size("dp")


class GatherSeq(Part):
    def result(self):
        shape = (self.chips, 2) + self.value.shape
        return jax.ShapeDtypeStruct(shape, self.value.dtype), pl.ANY

    def scratch(self):
        return spread_sems(self.chips)

    def steps(self, block, out, scratch, place):
        chip, core, group = place
        yield from spread_seq(block, out, scratch, place, self.chips)

    def finish(self, out):
        return out.reshape((2 * self.chips,) + self.value.shape)


class ExchangeSeq(Part):
    axes = ("near", "all")

    def result(self):
        return jax.ShapeDtypeStruct(self.value.shape, self.value.dtype), pl.ANY

    def scratch(self):
        count = 2 * self.chips
        return [pltpu.SemaphoreType.DMA((count,)), pltpu.SemaphoreType.DMA((count,))]

    def steps(self, block, out, scratch, place):
        chip, core, group = place
        send, recv = scratch
        me = 2 * chip + core
        local_copy = pltpu.make_async_copy(block.at[me], out.at[me], send.at[0])
        local_copy.start()
        copies = [
            flip_copy(block.at[me ^ m], out.at[me], send.at[m], recv.at[m], {"seq": me ^ m})
            for m in range(1, 2 * self.chips)
        ]
        yield
        for copy in copies:
            copy.wait()
        local_copy.wait()

    def finish(self, out):
        return out


class GatherDp(Part):
    axes = ("dp",)
    cores = False
    relay = True
    late = 0

    def result(self):
        lead = (self.groups, 2) if self.cores else (self.groups,)
        return jax.ShapeDtypeStruct(lead + self.value.shape, self.value.dtype), pl.ANY

    def scratch(self):
        return [pltpu.SemaphoreType.DMA((2, self.groups + 1)) for _ in range(2)] + [
            pltpu.SemaphoreType.DMA((2, 1)) for _ in range(2)
        ]

    def steps(self, block, out, scratch, place):
        chip, core, group = place
        send, recv, relay_send, relay_recv = scratch
        count = self.groups
        beside = {"seq": 2 * chip + 1 - core}
        relayed = self.relay and count == 4

        def at(rank):
            return out.at[rank, core] if self.cores else out.at[rank]

        def near(p):
            return flip_copy(
                at(group ^ p), at(group ^ p), send.at[1, p], recv.at[1, p], beside
            )

        local_copy = pltpu.make_async_copy(block, at(group), send.at[0, count])
        local_copy.start()
        copies = {
            p: flip_copy(block, at(group), send.at[0, p], recv.at[0, p], {"dp": group ^ p})
            for p in range(1, count)
            if not (relayed and p == 3)
        }
        cores = []
        if self.cores:
            cores.append(
                flip_copy(block, at(group), send.at[1, 0], recv.at[1, 0], beside)
            )
        for _ in range(1 + self.late):
            yield
        relays = []
        for p, copy in copies.items():
            copy.wait_recv()
            if relayed:
                first = self.value.shape[0] // 32 * 16
                rows = pl.ds(0, first) if p == 1 else pl.ds(first, self.value.shape[0] - first)
                half = at(group ^ p).at[rows]
                relays.append(
                    flip_copy(
                        half,
                        half,
                        relay_send.at[p - 1, 0],
                        relay_recv.at[p - 1, 0],
                        {"dp": group ^ (3 - p)},
                    )
                )
            if self.cores:
                cores.append(near(p))
        yield
        for copy in relays:
            copy.wait()
        if self.cores and relayed:
            cores.append(near(3))
        for copy in copies.values():
            copy.wait_send()
        yield
        for copy in cores:
            copy.wait()
        local_copy.wait()

    def finish(self, out):
        return out


class GatherDpLate(GatherDp):
    relay = False
    late = 4


class GatherDpCores(GatherDp):
    axes = ("dp", "near")
    cores = True


class Pass(Part):
    axes = ()
    alias = True

    def result(self):
        return jax.ShapeDtypeStruct(self.value.shape, self.value.dtype), pl.ANY

    def scratch(self):
        return []

    def steps(self, block, out, scratch, place):
        yield

    def finish(self, out):
        return out


class ExchangeDp(Part):
    axes = ("dp",)

    def result(self):
        return jax.ShapeDtypeStruct(self.value.shape, self.value.dtype), pl.ANY

    def scratch(self):
        return [pltpu.SemaphoreType.DMA((self.groups,)) for _ in range(2)]

    def steps(self, block, out, scratch, place):
        chip, core, group = place
        send, recv = scratch
        local_copy = pltpu.make_async_copy(block.at[group], out.at[group], send.at[0])
        local_copy.start()
        copies = [
            flip_copy(block.at[group ^ p], out.at[group], send.at[p], recv.at[p], {"dp": group ^ p})
            for p in range(1, self.groups)
        ]
        yield
        for copy in copies:
            copy.wait()
        local_copy.wait()

    def finish(self, out):
        return out


def add_rows(target, sources):
    rows = target.shape[0]

    @pl.loop(0, rows // 16)
    def _(i):
        at = pl.ds(pl.multiple_of(i * 16, 16), 16)
        total = sources[0][at, :].astype(F32)
        for source in sources[1:]:
            total = total + source[at, :].astype(F32)
        target[at, :] = total.astype(target.dtype)


class ScatterSeq(Part):
    axes = ("near", "far")

    def result(self):
        return jax.ShapeDtypeStruct(self.value.shape[1:], F32), pltpu.VMEM

    def prepare(self):
        shape = self.value.shape
        return self.value.reshape((self.chips, 2) + shape[1:])

    def scratch(self):
        block = self.value.shape[1:]
        return [
            pltpu.VMEM((self.chips,) + block, BF16),
            pltpu.VMEM((self.chips,) + block, BF16),
            pltpu.VMEM((2, self.chips) + block, BF16),
            pltpu.SemaphoreType.DMA((2, self.chips)),
            pltpu.SemaphoreType.DMA((2, self.chips)),
            pltpu.SemaphoreType.DMA((2, self.chips)),
            pltpu.SemaphoreType.DMA((1,)),
        ]

    def reduce(self, partial, out, scratch, place):
        chip, core, group = place
        chips = self.chips
        mine, peer, arrived, send, recv, near, own_sem = scratch
        local_copy = pltpu.make_async_copy(partial.at[:, core], mine, own_sem.at[0])
        local_copy.start()
        order = [k for i in range(chips // 2) for k in (chips - 1 - i, i)]
        beside = {
            k: flip_copy(
                partial.at[k, 1 - core],
                peer.at[k],
                near.at[0, k],
                near.at[1, k],
                {"seq": 2 * chip + 1 - core},
            )
            for k in order
        }
        yield
        local_copy.wait()

        def pair(k):
            beside[k].wait()
            add_rows(mine.at[k], [mine.at[k], peer.at[k]])

        more = [chip + 1 < chips, chip > 0]
        onward = [{"seq": 2 * (chip + 1) + core}, {"seq": 2 * (chip - 1) + core}]
        for step in range(chips - 1):
            for way in range(2):
                to = chips - 1 - step if way == 0 else step
                ahead = chip < to if way == 0 else chip > to
                if 2 * step < chips:
                    pair(to)

                @pl.when(ahead)
                def _(way=way, to=to):
                    @pl.when(more[1 - way])
                    def _():
                        waiting(
                            arrived.at[way, to], send.at[way, to], recv.at[way, to], onward[way]
                        ).wait_recv()
                        add_rows(mine.at[to], [mine.at[to], arrived.at[way, to]])

                    flip_copy(
                        mine.at[to],
                        arrived.at[way, to],
                        send.at[way, to],
                        recv.at[way, to],
                        onward[way],
                    )

            yield
        for way in range(2):

            @pl.when(more[1 - way])
            def _(way=way):
                waiting(
                    arrived.at[way, chip], send.at[way, chip], recv.at[way, chip], onward[way]
                ).wait_recv()

        @pl.when(more[0] & more[1])
        def _():
            add_rows(out, [mine.at[chip], arrived.at[0, chip], arrived.at[1, chip]])

        for way in range(2):

            @pl.when(more[1 - way] & jnp.logical_not(more[way]))
            def _(way=way):
                add_rows(out, [mine.at[chip], arrived.at[way, chip]])

            for to in range(chips):
                ahead = chip < to if way == 0 else chip > to

                @pl.when(ahead)
                def _(way=way, to=to):
                    waiting(
                        mine.at[to], send.at[way, to], recv.at[way, to], onward[way]
                    ).wait_send()

    def steps(self, partial, out, scratch, place):
        yield from self.reduce(partial, out, scratch, place)

    def finish(self, out):
        return out


class SumSeq(ScatterSeq):
    def result(self):
        return jax.ShapeDtypeStruct((self.chips, 2) + self.value.shape[1:], BF16), pl.ANY

    def scratch(self):
        return (
            ScatterSeq.scratch(self)
            + [pltpu.VMEM(self.value.shape[1:], BF16)]
            + spread_sems(self.chips)
        )

    def steps(self, partial, out, scratch, place):
        chip, core, group = place
        total = scratch[7]
        yield from self.reduce(partial, total, scratch[:7], place)
        yield from spread_seq(total, out, scratch[8:], place, self.chips)

    def finish(self, out):
        return out.reshape(self.value.shape)


class ReduceDp(Part):
    axes = ("dp",)

    def result(self):
        return jax.ShapeDtypeStruct(self.value.shape[1:], self.value.dtype), pltpu.VMEM

    def scratch(self):
        return [
            pltpu.VMEM(self.value.shape, self.value.dtype),
            pltpu.SemaphoreType.DMA((self.groups,)),
            pltpu.SemaphoreType.DMA((self.groups,)),
        ]

    def reduce(self, value, out, scratch, place):
        chip, core, group = place
        arrived, send, recv = scratch
        local_copy = pltpu.make_async_copy(value.at[group], arrived.at[0], send.at[0])
        local_copy.start()
        copies = [
            flip_copy(value.at[group ^ p], arrived.at[p], send.at[p], recv.at[p], {"dp": group ^ p})
            for p in range(1, self.groups)
        ]
        yield
        local_copy.wait()
        for copy in copies:
            copy.wait()
        add_rows(out, [arrived.at[p] for p in range(self.groups)])

    def steps(self, value, out, scratch, place):
        yield from self.reduce(value, out, scratch, place)

    def finish(self, out):
        return out


class ReduceDpGatherSeq(ReduceDp):
    axes = ("dp", "near", "far")

    def result(self):
        shape = (self.chips, 2) + self.value.shape[1:]
        return jax.ShapeDtypeStruct(shape, self.value.dtype), pl.ANY

    def scratch(self):
        return (
            ReduceDp.scratch(self)
            + [pltpu.VMEM(self.value.shape[1:], self.value.dtype)]
            + spread_sems(self.chips)
        )

    def steps(self, value, out, scratch, place):
        chip, core, group = place
        total = scratch[3]
        yield from self.reduce(value, total, scratch[:3], place)
        yield from spread_seq(total, out, scratch[4:], place, self.chips)

    def finish(self, out):
        return out.reshape((2 * self.chips,) + self.value.shape[1:])


def communicate(number, parts, micros=50):
    values = [part.prepare() if isinstance(part, ScatterSeq) else part.value for part in parts]
    results = [part.result() for part in parts]
    scratches = [part.scratch() for part in parts]
    chips, groups = parts[0].chips, parts[0].groups
    axes = set()
    for part in parts:
        axes.update(part.axes)

    def kernel(*refs):
        ins, outs = refs[: len(parts)], refs[len(parts) : 2 * len(parts)]
        rest = list(refs[2 * len(parts) :])
        me, group = lax.axis_index("seq"), lax.axis_index("dp")
        chip, core = me // 2, lax.rem(me, 2)
        targets = []
        for m in range(1, 2 * chips):
            if "all" in axes or (m == 1 and "near" in axes) or (m % 2 == 0 and "far" in axes):
                targets.append({"seq": me ^ m})
        if "dp" in axes:
            targets += [{"dp": group ^ p} for p in range(1, groups)]
        barrier = pltpu.get_barrier_semaphore()
        for target in targets:
            pl.semaphore_signal(
                barrier, inc=1, device_id=target, device_id_type=pl.DeviceIdType.MESH
            )
        pl.semaphore_wait(barrier, len(targets))
        running = []
        for part, value, out, scratch in zip(parts, ins, outs, scratches):
            own, rest = rest[: len(scratch)], rest[len(scratch) :]
            running.append(part.steps(value, out, own, (chip, core, group)))
        while running:
            running = [steps for steps in running if next(steps, "end") != "end"]

    outs = pl.pallas_call(
        kernel,
        out_shape=[shape for shape, _ in results],
        in_specs=[pl.BlockSpec(memory_space=pl.ANY)] * len(parts),
        out_specs=[pl.BlockSpec(memory_space=space) for _, space in results],
        scratch_shapes=[item for scratch in scratches for item in scratch],
        input_output_aliases={i: i for i, part in enumerate(parts) if part.alias},
        cost_estimate=pl.CostEstimate(
            flops=0, bytes_accessed=micros * 3_000_000, transcendentals=0
        ),
        compiler_params=pltpu.CompilerParams(
            collective_id=number, has_side_effects=True, vmem_limit_bytes=48 * 1024 * 1024
        ),
    )(*values)
    return [part.finish(out) for part, out in zip(parts, outs)]


def swap_dp(value, mask):
    return lax.ppermute(value, "dp", [(i, i ^ mask) for i in range(lax.axis_size("dp"))])


def background_pieces(value):
    me = lax.axis_index("dp")
    groups = lax.axis_size("dp")
    pieces = [
        lax.dynamic_index_in_dim(value, me ^ p, 0, keepdims=False) for p in range(groups)
    ]
    return [pieces[0]] + [swap_dp(pieces[p], p) for p in range(1, groups)]


def sum_pieces(pieces):
    return sum([piece.astype(F32) for piece in pieces[1:]], pieces[0].astype(F32)).astype(BF16)


def background_gather(value):
    return jnp.stack([value] + [swap_dp(value, p) for p in range(1, lax.axis_size("dp"))])


def own_first(value):
    me = lax.axis_index("dp")
    return jnp.stack(
        [
            lax.dynamic_index_in_dim(value, me ^ p, 0, keepdims=False)
            for p in range(lax.axis_size("dp"))
        ]
    )


def after(values, others):
    def kernel(*refs):
        del refs

    count = len(values)
    return pl.pallas_call(
        kernel,
        out_shape=[jax.ShapeDtypeStruct(v.shape, v.dtype) for v in values],
        in_specs=[pl.BlockSpec(memory_space=pl.ANY)] * (count + len(others)),
        out_specs=[pl.BlockSpec(memory_space=pl.ANY)] * count,
        input_output_aliases={i: i for i in range(count)},
        compiler_params=pltpu.CompilerParams(has_side_effects=True),
    )(*values, *others)


def joined_columns(pieces, groups, unit):
    count, rows, columns = pieces.shape
    half = columns // 2
    block = 64

    def kernel(pieces_ref, *out_refs):
        parts = [pieces_ref[rank].astype(F32) for rank in range(count)]
        for side, out_ref in enumerate(out_refs):
            out_ref[...] = jnp.concatenate(
                [
                    parts[rank][:, side * half + p * unit : side * half + (p + 1) * unit]
                    for p in range(groups)
                    for rank in range(count)
                ],
                axis=1,
            )

    shape = jax.ShapeDtypeStruct((rows, count * half), F32)
    return pl.pallas_call(
        kernel,
        grid=(rows // block,),
        out_shape=[shape, shape],
        in_specs=[pl.BlockSpec((count, block, columns), lambda i: (0, i, 0))],
        out_specs=[pl.BlockSpec((block, count * half), lambda i: (i, 0))] * 2,
        compiler_params=pltpu.CompilerParams(vmem_limit_bytes=48 * 1024 * 1024),
    )(pieces)


def padded_rows(value):
    rows = value.shape[-2]
    more = -rows % 16
    return jnp.pad(value, [(0, 0)] * (value.ndim - 2) + [(0, more), (0, 0)])


def local(
    inputs,
    segments,
    routes,
    cotangent,
    attention_gain,
    query_weight,
    latent_weight,
    latent_gain,
    expand_weight,
    output_weight,
    feedforward_gain,
    router_weight,
    shared_gate,
    shared_up,
    shared_down,
    expert_gate,
    expert_up,
    expert_down,
):
    seq_count = lax.axis_size("seq")
    dp_count = lax.axis_size("dp")
    me = lax.axis_index("seq")
    d_rank = lax.axis_index("dp")
    tokens = inputs.shape[1]
    width = inputs.shape[2]
    group = tokens * seq_count
    experts = EXP_DEV * seq_count
    heads_dev = HEADS // seq_count
    score_scale = 1.0 / math.sqrt(QK)
    shard = width // dp_count

    hq = heads_dev * QK
    hkv = heads_dev * (NOPE + VDIM)
    rank_shard = latent_gain.shape[0]
    latent_width = latent_weight.shape[1]
    small = jnp.concatenate(
        [attention_gain, feedforward_gain, latent_gain, router_weight.reshape(-1)]
    )
    fold = shard // rank_shard
    expand_part = lax.dynamic_slice_in_dim(expand_weight, me * hkv, hkv, 1)
    expand_part = (
        expand_part.reshape(rank_shard, fold, hkv // fold).transpose(1, 0, 2).reshape(shard, -1)
    )
    pack = jnp.concatenate(
        [lax.dynamic_slice_in_dim(query_weight, me * hq, hq, 1), expand_part], axis=1
    )
    pack_width = pack.shape[1]
    small_rows = -(-small.shape[0] // (16 * pack_width)) * 16
    small_pack = jnp.pad(small, (0, small_rows * pack_width - small.shape[0]))
    pack = jnp.concatenate([pack, small_pack.reshape(small_rows, pack_width)], axis=0)
    routes_pad = jnp.pad(routes[0], ((0, 0), (0, 128 - TOP))).astype(BF16)

    core = lax.rem(me, 2)

    def half_of(weight):
        rows = weight.shape[0] // 2
        return lax.dynamic_slice_in_dim(weight, core * rows, rows, 0)

    hidden = shared_gate.shape[1]
    unit = hidden // (dp_count * seq_count)
    side = dp_count * unit

    def columns_of(weight):
        return [
            lax.dynamic_slice_in_dim(weight, (p * seq_count + me) * unit, unit, 1)
            for p in range(dp_count)
        ]

    x_all, routes_all, pack, w_latent, w_output, g_all = communicate(
        1,
        [
            GatherSeq(inputs[0]),
            GatherSeq(routes_pad),
            GatherDp(pack),
            GatherDpCores(half_of(latent_weight)),
            GatherDpCores(half_of(output_weight)),
            GatherSeq(cotangent[0]),
        ],
    )
    arrived = routes_all[0, 0, 0] >= 0
    expert_gate, expert_up, expert_down = (
        jnp.where(arrived, weight, jnp.zeros_like(weight))
        for weight in (expert_gate, expert_up, expert_down)
    )
    w_egate = lax.all_gather(expert_gate, "dp", axis=1, tiled=True)
    w_eup = lax.all_gather(expert_up, "dp", axis=1, tiled=True)
    w_edown = lax.all_gather(expert_down, "dp", axis=2, tiled=True)
    g_all = g_all.reshape(group, width)
    x_all = x_all.reshape(group, width)
    w_query = pack[:, :shard, :hq].reshape(width, hq)
    w_latent = w_latent.reshape(width, latent_width)
    w_expand = (
        pack[:, :shard, hq:]
        .reshape(dp_count, fold, rank_shard, hkv // fold)
        .transpose(0, 2, 1, 3)
        .reshape(KV_RANK, hkv)
    )
    small = pack[:, shard:].reshape(dp_count, small_rows * pack_width)
    g_attn = small[:, :shard].reshape(width).astype(F32)
    g_ffn = small[:, shard : 2 * shard].reshape(width).astype(F32)
    g_latent = small[:, 2 * shard : 2 * shard + rank_shard].reshape(KV_RANK).astype(F32)
    w_router = small[:, 2 * shard + rank_shard :][:, : shard * experts].reshape(width, experts)

    routes_all = routes_all.reshape(group, 128)[:, :TOP].astype(jnp.int32)
    positions = jnp.arange(group, dtype=jnp.int32)
    seg_all = segments[0]
    cosine, sine = angles(positions, ROPE)
    my_experts = me * EXP_DEV + jnp.arange(EXP_DEV, dtype=jnp.int32)
    expert_ids = jnp.arange(experts, dtype=jnp.int32)
    hit = jnp.any(routes_all[None] == my_experts[:, None, None], axis=-1).astype(jnp.int32)
    slot = jnp.where(hit == 1, jnp.cumsum(hit, axis=1) - hit, CAP)
    route_hot = jnp.any(routes_all[:, :, None] == expert_ids[None, None, :], axis=1)
    placed = slot[:, None, :] == jnp.arange(CAP, dtype=jnp.int32)[None, :, None]
    dispatch = placed.astype(BF16).reshape(EXP_DEV * CAP, group)

    def own(value):
        return lax.dynamic_slice_in_dim(value, me * tokens, tokens, 0)

    attn_in = normalized_rows(x_all.astype(F32), g_attn).astype(BF16)
    q_raw = dot(attn_in, w_query).reshape(group, heads_dev, QK)
    latent_raw = dot(attn_in, w_latent)
    latent = latent_raw[:, :KV_RANK]
    latent_normed = normalized_rows(latent, g_latent).astype(BF16)
    key_value = dot(latent_normed, w_expand).reshape(group, heads_dev, NOPE + VDIM)
    q_full = jnp.concatenate(
        [q_raw[..., :NOPE], rotate(q_raw[..., NOPE:], cosine[:, None, :], sine[:, None, :])],
        axis=-1,
    ).astype(BF16)
    k_rot = rotate(latent_raw[:, KV_RANK:], cosine, sine)
    k_full = jnp.concatenate(
        [key_value[..., :NOPE], jnp.broadcast_to(k_rot[:, None, :], (group, heads_dev, ROPE))],
        axis=-1,
    ).astype(BF16)
    values = key_value[..., NOPE:].astype(BF16)
    visible = (seg_all[:, None] == seg_all[None, :]) & (seg_all[:, None] >= 0) & (
        positions[None, :] <= positions[:, None]
    ) | (positions[None, :] == positions[:, None])
    scores = jnp.einsum("qhd,khd->hqk", q_full, k_full, preferred_element_type=F32) * score_scale
    scores = jnp.where(visible[None], scores, MASKED)
    row_peak = jnp.max(scores, axis=-1, keepdims=True)
    exponent = jnp.exp(scores - row_peak)
    soft_float = exponent / jnp.sum(exponent, axis=-1, keepdims=True)
    soft = soft_float.astype(BF16)
    head_out = jnp.einsum("hqk,khd->qhd", soft, values, preferred_element_type=F32)
    head_out = head_out.astype(BF16).reshape(seq_count, tokens, heads_dev * VDIM)

    (head_out,) = communicate(2, [ExchangeSeq(head_out)])
    w_output = w_output.reshape(width, width)
    flat_out = jnp.swapaxes(head_out, 0, 1).reshape(tokens, HEADS * VDIM)
    x_float = inputs[0].astype(F32)
    residual = x_float + dot(flat_out, w_output)
    ffn_in = normalized_rows(residual, g_ffn).astype(BF16)

    ffn_all, w_sin, w_sdown = communicate(
        3,
        [
            GatherSeq(ffn_in),
            GatherDp(jnp.concatenate(columns_of(shared_gate) + columns_of(shared_up), axis=1)),
            GatherDp(padded_rows(lax.dynamic_slice_in_dim(shared_down, me * unit, unit, 0))),
        ],
    )
    w_sin = w_sin.reshape(width, 2 * side)
    w_sdown = w_sdown[:, :unit].reshape(side, width)
    ffn_all = ffn_all.reshape(group, width)

    router_probs = jax.nn.softmax(dot(ffn_all, w_router), axis=-1)
    chosen = jnp.where(route_hot, router_probs, 0.0)
    chosen_sum = jnp.sum(chosen, axis=-1, keepdims=True)
    gates = chosen / chosen_sum
    my_gates = lax.dynamic_slice_in_dim(gates.T, me * EXP_DEV, EXP_DEV, 0)
    gate_rows = jnp.sum(jnp.where(placed, my_gates[:, None, :], 0.0), axis=-1)

    side_in = dot(ffn_all, w_sin)
    side_gate, side_up = side_in[:, :side], side_in[:, side:]
    side_act = swiglu(side_gate, side_up).astype(BF16)
    grad_sdown = t_dot(side_act, g_all)
    d_side_act = dot_t(g_all, w_sdown)
    _, side_pull = jax.vjp(swiglu, side_gate, side_up)
    d_side_gate, d_side_up = side_pull(d_side_act)
    d_side = jnp.concatenate([d_side_gate, d_side_up], axis=1).astype(BF16)
    grad_sin = t_dot(ffn_all, d_side)
    dispatch, all_sin, all_sdown = communicate(
        5,
        [
            Pass(dispatch),
            ReduceDpGatherSeq(grad_sin.astype(BF16).reshape(dp_count, shard, 2 * side)),
            ReduceDpGatherSeq(padded_rows(grad_sdown.astype(BF16).reshape(dp_count, unit, width))),
        ],
    )

    out_sgate, out_sup = joined_columns(all_sin, dp_count, unit)
    out_sdown = all_sdown[:, :unit].reshape(hidden // dp_count, width).astype(F32)

    rows_shape = (EXP_DEV, CAP, width)
    expert_in = dot(dispatch, ffn_all).astype(BF16).reshape(rows_shape)
    hidden_gate = jnp.einsum("nmh,nhq->nmq", expert_in, w_egate, preferred_element_type=F32)
    g_rows = dot(dispatch, g_all).astype(BF16).reshape(rows_shape)
    expert_grad = (gate_rows[:, :, None] * g_rows.astype(F32)).astype(BF16)
    hidden_up = jnp.einsum("nmh,nhq->nmq", expert_in, w_eup, preferred_element_type=F32)
    expert_act = swiglu(hidden_gate, hidden_up).astype(BF16)
    grad_edown = jnp.einsum("kcf,kcd->kfd", expert_act, expert_grad, preferred_element_type=F32)
    grad_edown = grad_edown.astype(BF16)
    (g_rows,) = after([g_rows], [grad_edown, out_sgate, out_sup, out_sdown])

    d_act_plain = jnp.einsum("kcd,kfd->kcf", g_rows, w_edown, preferred_element_type=F32)
    d_act_plain = lax.optimization_barrier(d_act_plain)
    d_gate_rows = jnp.sum(expert_act.astype(F32) * d_act_plain, axis=-1)
    _, expert_pull = jax.vjp(swiglu, hidden_gate, hidden_up)
    d_hidden_gate, d_hidden_up = expert_pull(gate_rows[:, :, None] * d_act_plain)
    d_hidden_gate = d_hidden_gate.astype(BF16)
    d_hidden_up = d_hidden_up.astype(BF16)
    grad_egate = jnp.einsum("kcd,kcf->kdf", expert_in, d_hidden_gate, preferred_element_type=F32)
    grad_eup = jnp.einsum("kcd,kcf->kdf", expert_in, d_hidden_up, preferred_element_type=F32)
    grad_egate, grad_eup = grad_egate.astype(BF16), grad_eup.astype(BF16)
    shard_edown = lax.psum_scatter(grad_edown, "dp", scatter_dimension=2, tiled=True).astype(F32)
    shard_egate = lax.psum_scatter(grad_egate, "dp", scatter_dimension=1, tiled=True).astype(F32)
    shard_eup = lax.psum_scatter(grad_eup, "dp", scatter_dimension=1, tiled=True).astype(F32)
    d_hidden_gate, d_hidden_up = after([d_hidden_gate, d_hidden_up], [grad_egate, grad_eup])
    d_expert_in = (
        jnp.einsum("sta,sra->str", d_hidden_gate, w_egate, preferred_element_type=F32)
        + jnp.einsum("sta,sra->str", d_hidden_up, w_eup, preferred_element_type=F32)
    ).astype(BF16)
    d_ffn_partial = dot_t(d_side, w_sin) + t_dot(
        dispatch, d_expert_in.reshape(EXP_DEV * CAP, width)
    )
    d_gate_own = jnp.sum(jnp.where(placed, d_gate_rows[:, :, None], 0.0), axis=1)
    mine_hot = (my_experts[:, None] == expert_ids[None, :]).astype(F32)
    d_gate_wide = jnp.sum(d_gate_own[:, :, None] * mine_hot[:, None, :], axis=0)
    d_gate_high = d_gate_wide.astype(BF16)
    d_gate_low = (d_gate_wide - d_gate_high.astype(F32)).astype(BF16)
    d_gate_pack = jnp.concatenate(
        [d_gate_high, d_gate_low, jnp.zeros((group, 128 - 2 * experts), BF16)], axis=1
    )
    def by_group(rows):
        return jnp.swapaxes(rows.reshape(tokens, dp_count, -1), 0, 1)

    d_ffn, d_gate, left_out, left_latent = communicate(
        6,
        [
            ScatterSeq(d_ffn_partial.astype(BF16).reshape(seq_count, tokens, width)),
            ScatterSeq(d_gate_pack.reshape(seq_count, tokens, 128)),
            ExchangeDp(by_group(flat_out)),
            ExchangeDp(by_group(own(attn_in))),
        ],
    )
    d_gate = d_gate[:, :experts] + d_gate[:, experts : 2 * experts]

    (expert_act,) = after([expert_act], [d_ffn])
    expert_out = jnp.einsum("kcf,kfd->kcd", expert_act, w_edown, preferred_element_type=F32)
    expert_out = expert_out.astype(BF16).astype(F32)
    moe_rows = (gate_rows[:, :, None] * expert_out).astype(BF16).reshape(EXP_DEV * CAP, width)
    ffn_out = (dot(side_act, w_sdown) + t_dot(dispatch, moe_rows)).astype(BF16)

    own_hot = own(route_hot)
    own_probs = own(router_probs)
    own_gates = own(gates)
    d_chosen = (d_gate - jnp.sum(d_gate * own_gates, axis=-1, keepdims=True)) / own(chosen_sum)
    d_probs = jnp.where(own_hot, d_chosen, 0.0)
    d_logits = own_probs * (d_probs - jnp.sum(own_probs * d_probs, axis=-1, keepdims=True))
    grad_router = jnp.einsum("td,te->de", ffn_in.astype(F32), d_logits, precision=HIGHEST)
    d_ffn = d_ffn + jnp.einsum("te,de->td", d_logits, w_router.astype(F32), precision=HIGHEST)

    grad_out = cotangent[0].astype(F32)
    d_resid_part, grad_ffn_gain = norm_backward(residual, g_ffn, d_ffn)
    d_residual = grad_out + d_resid_part
    d_attn = d_residual.astype(BF16)
    d_head = dot_t(d_attn, w_output).astype(BF16)
    d_head = jnp.swapaxes(d_head.reshape(tokens, seq_count, heads_dev * VDIM), 0, 1)
    (head_grad,) = communicate(7, [ExchangeSeq(d_head)])
    head_grad = head_grad.reshape(group, heads_dev, VDIM)

    d_values = jnp.einsum("hqk,qhd->khd", soft, head_grad, preferred_element_type=F32).astype(BF16)
    d_prob = jnp.einsum("qhd,khd->hqk", head_grad, values, preferred_element_type=F32)
    d_score = (
        soft_float * (d_prob - jnp.sum(soft_float * d_prob, axis=-1, keepdims=True))
    ).astype(BF16)
    d_query = jnp.einsum("hqk,khd->qhd", d_score, k_full, preferred_element_type=F32)
    d_query = (d_query * score_scale).astype(BF16).astype(F32)
    d_key = jnp.einsum("hqk,qhd->khd", d_score, q_full, preferred_element_type=F32)
    d_key = (d_key * score_scale).astype(BF16)
    d_q_raw = jnp.concatenate(
        [d_query[..., :NOPE], rotate(d_query[..., NOPE:], cosine[:, None, :], -sine[:, None, :])],
        axis=-1,
    )
    d_q_raw = d_q_raw.astype(BF16).reshape(group, hq)
    d_key_value = jnp.concatenate([d_key[..., :NOPE], d_values], axis=-1).reshape(group, hkv)
    dk_rope = jnp.sum(d_key[..., NOPE:].astype(F32), axis=1)
    latent_pad = -latent_width % 128
    d_latent_part = jnp.concatenate(
        [dot_t(d_key_value, w_expand), dk_rope, jnp.zeros((group, latent_pad), F32)], axis=-1
    ).astype(BF16)
    d_attn_part = dot_t(d_q_raw, w_query).astype(BF16)
    grad_expand = t_dot(latent_normed, d_key_value).astype(BF16)
    grad_query = t_dot(attn_in, d_q_raw).astype(BF16)

    left_latent = own_first(left_latent)
    query_pieces = background_pieces(grad_query.reshape(dp_count, shard, hq))
    expand_pieces = background_pieces(grad_expand.reshape(dp_count, rank_shard, hkv))
    d_latent_sum, d_attn_in, moe, right_out = communicate(
        8,
        [
            ScatterSeq(d_latent_part.reshape(seq_count, tokens, latent_width + latent_pad)),
            ScatterSeq(d_attn_part.reshape(seq_count, tokens, width)),
            ScatterSeq(ffn_out.reshape(seq_count, tokens, width)),
            GatherDpLate(d_attn),
        ],
        micros=90,
    )
    query_pieces[0], expand_pieces[0] = after([query_pieces[0], expand_pieces[0]], [d_attn_in])
    sum_query, sum_expand = sum_pieces(query_pieces), sum_pieces(expand_pieces)
    d_k_pe = rotate(d_latent_sum[:, KV_RANK:latent_width], own(cosine), -own(sine))
    d_latent, grad_latent_gain = norm_backward(
        own(latent), g_latent, d_latent_sum[:, :KV_RANK]
    )
    d_latent_raw = jnp.concatenate([d_latent, d_k_pe], axis=-1).astype(BF16)
    d_attn_in = d_attn_in + dot_t(d_latent_raw, w_latent)
    d_x_part, grad_attn_gain = norm_backward(x_float, g_attn, d_attn_in)
    grad_inputs = d_residual + d_x_part

    all_tokens = dp_count * tokens
    grad_output = t_dot(left_out.reshape(all_tokens, shard), right_out.reshape(all_tokens, width))
    grad_output = grad_output.astype(BF16).reshape(seq_count, shard // seq_count, width)
    latent_rows = jnp.pad(d_latent_raw, ((0, 0), (0, latent_pad)))

    gains = jnp.concatenate(
        [
            grad_attn_gain.reshape(dp_count, -1),
            grad_ffn_gain.reshape(dp_count, -1),
            grad_latent_gain.reshape(dp_count, -1),
            grad_router.reshape(dp_count, -1),
        ],
        axis=1,
    )
    gain_width = gains.shape[1]
    gain_rows = -(-gain_width // (16 * 128)) * 16
    gains = jnp.pad(gains, ((0, 0), (0, gain_rows * 128 - gain_width)))

    right_latent = background_gather(latent_rows)
    grad_latent = t_dot(
        left_latent.reshape(all_tokens, shard),
        right_latent.reshape(all_tokens, -1)[:, :latent_width],
    ).astype(BF16)
    latent_blocks = jnp.pad(
        grad_latent.reshape(seq_count, shard // seq_count, latent_width),
        ((0, 0), (0, 0), (0, latent_pad)),
    )
    out_output, all_query, all_expand, out_latent, all_gains = communicate(
        9,
        [
            SumSeq(grad_output),
            GatherSeq(sum_query),
            GatherSeq(sum_expand),
            SumSeq(latent_blocks),
            ReduceDpGatherSeq(gains.reshape(dp_count, gain_rows, 128)),
        ],
    )
    layer_out = (residual + moe).astype(BF16)
    out_query = jnp.swapaxes(all_query, 0, 1).reshape(shard, HEADS * QK).astype(F32)
    out_expand = (
        jnp.swapaxes(all_expand, 0, 1).reshape(rank_shard, HEADS * (NOPE + VDIM)).astype(F32)
    )
    out_output = out_output.reshape(shard, width).astype(F32)
    out_latent = out_latent.reshape(shard, -1)[:, :latent_width].astype(F32)

    sums = jnp.sum(all_gains, axis=0).reshape(-1)
    out_attn_gain = sums[:shard]
    out_ffn_gain = sums[shard : 2 * shard]
    out_latent_gain = sums[2 * shard : 2 * shard + rank_shard]
    out_router = sums[2 * shard + rank_shard : gain_width].reshape(shard, experts)

    return (
        layer_out[None],
        grad_inputs[None],
        out_attn_gain,
        out_query,
        out_latent,
        out_latent_gain,
        out_expand,
        out_output,
        out_ffn_gain,
        out_router,
        out_sgate,
        out_sup,
        out_sdown,
        shard_egate,
        shard_eup,
        shard_edown,
    )


def solution(mesh):
    placed = (
        P("dp", "seq", None),
        P("dp", None),
        P("dp", "seq", None),
        P("dp", "seq", None),
        P("dp"),
        P("dp", None),
        P("dp", None),
        P("dp"),
        P("dp", None),
        P("dp", None),
        P("dp"),
        P("dp", None),
        P("dp", None),
        P("dp", None),
        P("dp", None),
        P("seq", "dp", None),
        P("seq", "dp", None),
        P("seq", None, "dp"),
    )
    return jax.shard_map(
        local,
        mesh=mesh,
        in_specs=placed,
        out_specs=(
            P("dp", "seq", None),
            P("dp", "seq", None),
            P("dp"),
            P("dp", None),
            P("dp", None),
            P("dp"),
            P("dp", None),
            P("dp", None),
            P("dp"),
            P("dp", None),
            P("dp", None),
            P("dp", None),
            P("dp", None),
            P("seq", "dp", None),
            P("seq", "dp", None),
            P("seq", None, "dp"),
        ),
        check_vma=False,
    )
```

```python
import math

import jax
import jax.numpy as jnp
from jax import lax
from jax.experimental import pallas as pl
from jax.experimental.pallas import tpu as pltpu
from jax.sharding import PartitionSpec as P

HEADS = 16
NOPE = 128
ROPE = 64
VDIM = 128
KV_RANK = 512
TOP = 6
EXP_DEV = 2
CAP = 480

EPSILON = 1e-06
MASKED = -1e30
HIGHEST = lax.Precision.HIGHEST
F32 = jnp.float32
BF16 = jnp.bfloat16
QK = NOPE + ROPE


def normalized_rows(values, gain):
    return values * lax.rsqrt(jnp.mean(values * values, axis=-1, keepdims=True) + EPSILON) * gain


def norm_backward(values, gain, upstream):
    scale = lax.rsqrt(jnp.mean(values * values, axis=-1, keepdims=True) + EPSILON)
    normed = values * scale
    weighted = upstream * gain
    d_values = scale * (weighted - normed * jnp.mean(weighted * normed, axis=-1, keepdims=True))
    return d_values, jnp.sum(upstream * normed, axis=0)


def angles(positions, width):
    frequency = 10000.0 ** (-(2.0 * jnp.arange(width // 2, dtype=F32)) / width)
    turned = positions.astype(F32)[:, None] * frequency[None, :]
    return (jnp.cos(turned), jnp.sin(turned))


def rotate(values, cosine, sine):
    half_width = values.shape[-1] // 2
    lower_half = values[..., :half_width]
    upper_half = values[..., half_width:]
    return jnp.concatenate(
        [lower_half * cosine - upper_half * sine, upper_half * cosine + lower_half * sine], axis=-1
    )


def swiglu(gate_portion, up_part):
    return jax.nn.silu(gate_portion) * up_part


def dot(left, right):
    return jnp.dot(left, right, preferred_element_type=F32)


def dot_t(left, right):
    return lax.dot_general(left, right, (((1,), (1,)), ((), ())), preferred_element_type=F32)


def t_dot(left, right):
    return lax.dot_general(left, right, (((0,), (0,)), ((), ())), preferred_element_type=F32)


def flip_copy(src, dst, send_sem, recv_sem, target):
    copy = pltpu.make_async_remote_copy(
        src_ref=src,
        dst_ref=dst,
        send_sem=send_sem,
        recv_sem=recv_sem,
        device_id=target,
        device_id_type=pl.DeviceIdType.MESH,
    )
    copy.start()
    return copy


def waiting(block, send_sem, recv_sem, target):
    return pltpu.make_async_remote_copy(
        src_ref=block,
        dst_ref=block,
        send_sem=send_sem,
        recv_sem=recv_sem,
        device_id=target,
        device_id_type=pl.DeviceIdType.MESH,
    )


def spread_seq(block, out, sems, place, chips):
    sends, recvs, near_send, near_recv, own_sem = sems
    chip, core, group = place
    beside = {"seq": 2 * chip + 1 - core}
    local_copy = pltpu.make_async_copy(block, out.at[chip, core], own_sem.at[0])
    local_copy.start()
    more = [chip + 1 < chips, chip > 0]
    onward = [{"seq": 2 * (chip + 1) + core}, {"seq": 2 * (chip - 1) + core}]
    for way in range(2):

        @pl.when(more[way])
        def _(way=way):
            flip_copy(
                block, out.at[chip, core], sends.at[way, 0], recvs.at[way, 0], onward[way]
            )

    flip_copy(block, out.at[chip, core], near_send.at[0, 0], near_recv.at[0, 0], beside)
    yield
    for step in range(1, chips):
        for way in range(2):
            source = chip - step if way == 0 else chip + step
            there = source >= 0 if way == 0 else source < chips

            @pl.when(there)
            def _(way=way, step=step, source=source):
                arrived = out.at[source, core]
                waiting(
                    arrived, sends.at[way, step - 1], recvs.at[way, step - 1], beside
                ).wait_recv()
                if step < chips - 1:

                    @pl.when(more[way])
                    def _():
                        flip_copy(
                            arrived,
                            arrived,
                            sends.at[way, step],
                            recvs.at[way, step],
                            onward[way],
                        )

                flip_copy(
                    arrived, arrived, near_send.at[way, step], near_recv.at[way, step], beside
                )

        yield
    own = out.at[chip, core]
    waiting(own, near_send.at[0, 0], near_recv.at[0, 0], beside).wait()
    for step in range(chips):
        for way in range(2):
            source = chip - step if way == 0 else chip + step
            there = source >= 0 if way == 0 else source < chips
            if step:

                @pl.when(there)
                def _(way=way, step=step):
                    waiting(
                        own, near_send.at[way, step], near_recv.at[way, step], beside
                    ).wait()

            if step < chips - 1:

                @pl.when(there & more[way])
                def _(way=way, step=step):
                    waiting(
                        own, sends.at[way, step], recvs.at[way, step], onward[way]
                    ).wait_send()

    local_copy.wait()


def spread_sems(chips):
    return [pltpu.SemaphoreType.DMA((2, chips)) for _ in range(4)] + [
        pltpu.SemaphoreType.DMA((1,))
    ]


class Part:
    axes = ("near", "far")
    alias = False

    def __init__(self, value):
        self.value = value
        self.chips = lax.axis_size("seq") // 2
        self.groups = lax.axis_size("dp")


class GatherSeq(Part):
    def result(self):
        shape = (self.chips, 2) + self.value.shape
        return jax.ShapeDtypeStruct(shape, self.value.dtype), pl.ANY

    def scratch(self):
        return spread_sems(self.chips)

    def steps(self, block, out, scratch, place):
        chip, core, group = place
        yield from spread_seq(block, out, scratch, place, self.chips)

    def finish(self, out):
        return out.reshape((2 * self.chips,) + self.value.shape)


class ExchangeSeq(Part):
    axes = ("near", "all")

    def result(self):
        return jax.ShapeDtypeStruct(self.value.shape, self.value.dtype), pl.ANY

    def scratch(self):
        count = 2 * self.chips
        return [pltpu.SemaphoreType.DMA((count,)), pltpu.SemaphoreType.DMA((count,))]

    def steps(self, block, out, scratch, place):
        chip, core, group = place
        send, recv = scratch
        me = 2 * chip + core
        local_copy = pltpu.make_async_copy(block.at[me], out.at[me], send.at[0])
        local_copy.start()
        copies = [
            flip_copy(block.at[me ^ m], out.at[me], send.at[m], recv.at[m], {"seq": me ^ m})
            for m in range(1, 2 * self.chips)
        ]
        yield
        for copy in copies:
            copy.wait()
        local_copy.wait()

    def finish(self, out):
        return out


class GatherDp(Part):
    axes = ("dp",)
    cores = False

    def result(self):
        lead = (self.groups, 2) if self.cores else (self.groups,)
        return jax.ShapeDtypeStruct(lead + self.value.shape, self.value.dtype), pl.ANY

    def scratch(self):
        return [pltpu.SemaphoreType.DMA((2, self.groups + 1)) for _ in range(2)] + [
            pltpu.SemaphoreType.DMA((2, 1)) for _ in range(2)
        ]

    def steps(self, block, out, scratch, place):
        chip, core, group = place
        send, recv, relay_send, relay_recv = scratch
        count = self.groups
        beside = {"seq": 2 * chip + 1 - core}
        relayed = count == 4

        def at(rank):
            return out.at[rank, core] if self.cores else out.at[rank]

        def near(p):
            return flip_copy(
                at(group ^ p), at(group ^ p), send.at[1, p], recv.at[1, p], beside
            )

        local_copy = pltpu.make_async_copy(block, at(group), send.at[0, count])
        local_copy.start()
        copies = {
            p: flip_copy(block, at(group), send.at[0, p], recv.at[0, p], {"dp": group ^ p})
            for p in range(1, count)
            if not (relayed and p == 3)
        }
        cores = []
        if self.cores:
            cores.append(
                flip_copy(block, at(group), send.at[1, 0], recv.at[1, 0], beside)
            )
        yield
        relays = []
        for p, copy in copies.items():
            copy.wait_recv()
            if relayed:
                first = self.value.shape[0] // 32 * 16
                rows = pl.ds(0, first) if p == 1 else pl.ds(first, self.value.shape[0] - first)
                half = at(group ^ p).at[rows]
                relays.append(
                    flip_copy(
                        half,
                        half,
                        relay_send.at[p - 1, 0],
                        relay_recv.at[p - 1, 0],
                        {"dp": group ^ (3 - p)},
                    )
                )
            if self.cores:
                cores.append(near(p))
        yield
        for copy in relays:
            copy.wait()
        if self.cores and relayed:
            cores.append(near(3))
        for copy in copies.values():
            copy.wait_send()
        yield
        for copy in cores:
            copy.wait()
        local_copy.wait()

    def finish(self, out):
        return out


class GatherDpCores(GatherDp):
    axes = ("dp", "near")
    cores = True


class Pass(Part):
    axes = ()
    alias = True

    def result(self):
        return jax.ShapeDtypeStruct(self.value.shape, self.value.dtype), pl.ANY

    def scratch(self):
        return []

    def steps(self, block, out, scratch, place):
        yield

    def finish(self, out):
        return out


class ExchangeDp(Part):
    axes = ("dp",)

    def result(self):
        return jax.ShapeDtypeStruct(self.value.shape, self.value.dtype), pl.ANY

    def scratch(self):
        return [pltpu.SemaphoreType.DMA((self.groups,)) for _ in range(2)]

    def steps(self, block, out, scratch, place):
        chip, core, group = place
        send, recv = scratch
        local_copy = pltpu.make_async_copy(block.at[group], out.at[group], send.at[0])
        local_copy.start()
        copies = [
            flip_copy(block.at[group ^ p], out.at[group], send.at[p], recv.at[p], {"dp": group ^ p})
            for p in range(1, self.groups)
        ]
        yield
        for copy in copies:
            copy.wait()
        local_copy.wait()

    def finish(self, out):
        return out


def add_rows(target, sources):
    rows = target.shape[0]

    @pl.loop(0, rows // 16)
    def _(i):
        at = pl.ds(pl.multiple_of(i * 16, 16), 16)
        total = sources[0][at, :].astype(F32)
        for source in sources[1:]:
            total = total + source[at, :].astype(F32)
        target[at, :] = total.astype(target.dtype)


class ScatterSeq(Part):
    axes = ("near", "far")

    def result(self):
        return jax.ShapeDtypeStruct(self.value.shape[1:], F32), pltpu.VMEM

    def prepare(self):
        shape = self.value.shape
        return self.value.reshape((self.chips, 2) + shape[1:])

    def scratch(self):
        block = self.value.shape[1:]
        return [
            pltpu.VMEM((self.chips,) + block, BF16),
            pltpu.VMEM((self.chips,) + block, BF16),
            pltpu.VMEM((2, self.chips) + block, BF16),
            pltpu.SemaphoreType.DMA((2, self.chips)),
            pltpu.SemaphoreType.DMA((2, self.chips)),
            pltpu.SemaphoreType.DMA((2, self.chips)),
            pltpu.SemaphoreType.DMA((1,)),
        ]

    def reduce(self, partial, out, scratch, place):
        chip, core, group = place
        chips = self.chips
        mine, peer, arrived, send, recv, near, own_sem = scratch
        local_copy = pltpu.make_async_copy(partial.at[:, core], mine, own_sem.at[0])
        local_copy.start()
        order = [k for i in range(chips // 2) for k in (chips - 1 - i, i)]
        beside = {
            k: flip_copy(
                partial.at[k, 1 - core],
                peer.at[k],
                near.at[0, k],
                near.at[1, k],
                {"seq": 2 * chip + 1 - core},
            )
            for k in order
        }
        yield
        local_copy.wait()

        def pair(k):
            beside[k].wait()
            add_rows(mine.at[k], [mine.at[k], peer.at[k]])

        more = [chip + 1 < chips, chip > 0]
        onward = [{"seq": 2 * (chip + 1) + core}, {"seq": 2 * (chip - 1) + core}]
        for step in range(chips - 1):
            for way in range(2):
                to = chips - 1 - step if way == 0 else step
                ahead = chip < to if way == 0 else chip > to
                if 2 * step < chips:
                    pair(to)

                @pl.when(ahead)
                def _(way=way, to=to):
                    @pl.when(more[1 - way])
                    def _():
                        waiting(
                            arrived.at[way, to], send.at[way, to], recv.at[way, to], onward[way]
                        ).wait_recv()
                        add_rows(mine.at[to], [mine.at[to], arrived.at[way, to]])

                    flip_copy(
                        mine.at[to],
                        arrived.at[way, to],
                        send.at[way, to],
                        recv.at[way, to],
                        onward[way],
                    )

            yield
        for way in range(2):

            @pl.when(more[1 - way])
            def _(way=way):
                waiting(
                    arrived.at[way, chip], send.at[way, chip], recv.at[way, chip], onward[way]
                ).wait_recv()

        @pl.when(more[0] & more[1])
        def _():
            add_rows(out, [mine.at[chip], arrived.at[0, chip], arrived.at[1, chip]])

        for way in range(2):

            @pl.when(more[1 - way] & jnp.logical_not(more[way]))
            def _(way=way):
                add_rows(out, [mine.at[chip], arrived.at[way, chip]])

            for to in range(chips):
                ahead = chip < to if way == 0 else chip > to

                @pl.when(ahead)
                def _(way=way, to=to):
                    waiting(
                        mine.at[to], send.at[way, to], recv.at[way, to], onward[way]
                    ).wait_send()

    def steps(self, partial, out, scratch, place):
        yield from self.reduce(partial, out, scratch, place)

    def finish(self, out):
        return out


class SumSeq(ScatterSeq):
    def result(self):
        return jax.ShapeDtypeStruct((self.chips, 2) + self.value.shape[1:], BF16), pl.ANY

    def scratch(self):
        return (
            ScatterSeq.scratch(self)
            + [pltpu.VMEM(self.value.shape[1:], BF16)]
            + spread_sems(self.chips)
        )

    def steps(self, partial, out, scratch, place):
        chip, core, group = place
        total = scratch[7]
        yield from self.reduce(partial, total, scratch[:7], place)
        yield from spread_seq(total, out, scratch[8:], place, self.chips)

    def finish(self, out):
        return out.reshape(self.value.shape)


class ReduceDp(Part):
    axes = ("dp",)

    def result(self):
        return jax.ShapeDtypeStruct(self.value.shape[1:], self.value.dtype), pltpu.VMEM

    def scratch(self):
        return [
            pltpu.VMEM(self.value.shape, self.value.dtype),
            pltpu.SemaphoreType.DMA((self.groups,)),
            pltpu.SemaphoreType.DMA((self.groups,)),
        ]

    def reduce(self, value, out, scratch, place):
        chip, core, group = place
        arrived, send, recv = scratch
        local_copy = pltpu.make_async_copy(value.at[group], arrived.at[0], send.at[0])
        local_copy.start()
        copies = [
            flip_copy(value.at[group ^ p], arrived.at[p], send.at[p], recv.at[p], {"dp": group ^ p})
            for p in range(1, self.groups)
        ]
        yield
        local_copy.wait()
        for copy in copies:
            copy.wait()
        add_rows(out, [arrived.at[p] for p in range(self.groups)])

    def steps(self, value, out, scratch, place):
        yield from self.reduce(value, out, scratch, place)

    def finish(self, out):
        return out


class ReduceDpGatherSeq(ReduceDp):
    axes = ("dp", "near", "far")

    def result(self):
        shape = (self.chips, 2) + self.value.shape[1:]
        return jax.ShapeDtypeStruct(shape, self.value.dtype), pl.ANY

    def scratch(self):
        return (
            ReduceDp.scratch(self)
            + [pltpu.VMEM(self.value.shape[1:], self.value.dtype)]
            + spread_sems(self.chips)
        )

    def steps(self, value, out, scratch, place):
        chip, core, group = place
        total = scratch[3]
        yield from self.reduce(value, total, scratch[:3], place)
        yield from spread_seq(total, out, scratch[4:], place, self.chips)

    def finish(self, out):
        return out.reshape((2 * self.chips,) + self.value.shape[1:])


def communicate(number, parts, micros=50):
    values = [part.prepare() if isinstance(part, ScatterSeq) else part.value for part in parts]
    results = [part.result() for part in parts]
    scratches = [part.scratch() for part in parts]
    chips, groups = parts[0].chips, parts[0].groups
    axes = set()
    for part in parts:
        axes.update(part.axes)

    def kernel(*refs):
        ins, outs = refs[: len(parts)], refs[len(parts) : 2 * len(parts)]
        rest = list(refs[2 * len(parts) :])
        me, group = lax.axis_index("seq"), lax.axis_index("dp")
        chip, core = me // 2, lax.rem(me, 2)
        targets = []
        for m in range(1, 2 * chips):
            if "all" in axes or (m == 1 and "near" in axes) or (m % 2 == 0 and "far" in axes):
                targets.append({"seq": me ^ m})
        if "dp" in axes:
            targets += [{"dp": group ^ p} for p in range(1, groups)]
        barrier = pltpu.get_barrier_semaphore()
        for target in targets:
            pl.semaphore_signal(
                barrier, inc=1, device_id=target, device_id_type=pl.DeviceIdType.MESH
            )
        pl.semaphore_wait(barrier, len(targets))
        running = []
        for part, value, out, scratch in zip(parts, ins, outs, scratches):
            own, rest = rest[: len(scratch)], rest[len(scratch) :]
            running.append(part.steps(value, out, own, (chip, core, group)))
        while running:
            running = [steps for steps in running if next(steps, "end") != "end"]

    outs = pl.pallas_call(
        kernel,
        out_shape=[shape for shape, _ in results],
        in_specs=[pl.BlockSpec(memory_space=pl.ANY)] * len(parts),
        out_specs=[pl.BlockSpec(memory_space=space) for _, space in results],
        scratch_shapes=[item for scratch in scratches for item in scratch],
        input_output_aliases={i: i for i, part in enumerate(parts) if part.alias},
        cost_estimate=pl.CostEstimate(
            flops=0, bytes_accessed=micros * 3_000_000, transcendentals=0
        ),
        compiler_params=pltpu.CompilerParams(
            collective_id=number, has_side_effects=True, vmem_limit_bytes=48 * 1024 * 1024
        ),
    )(*values)
    return [part.finish(out) for part, out in zip(parts, outs)]


def swap_dp(value, mask):
    return lax.ppermute(value, "dp", [(i, i ^ mask) for i in range(lax.axis_size("dp"))])


def background_pieces(value):
    me = lax.axis_index("dp")
    groups = lax.axis_size("dp")
    pieces = [
        lax.dynamic_index_in_dim(value, me ^ p, 0, keepdims=False) for p in range(groups)
    ]
    return [pieces[0]] + [swap_dp(pieces[p], p) for p in range(1, groups)]


def sum_pieces(pieces):
    return sum([piece.astype(F32) for piece in pieces[1:]], pieces[0].astype(F32)).astype(BF16)


def background_gather(value):
    return jnp.stack([value] + [swap_dp(value, p) for p in range(1, lax.axis_size("dp"))])


def own_first(value):
    me = lax.axis_index("dp")
    return jnp.stack(
        [
            lax.dynamic_index_in_dim(value, me ^ p, 0, keepdims=False)
            for p in range(lax.axis_size("dp"))
        ]
    )


def after(values, others):
    def kernel(*refs):
        del refs

    count = len(values)
    return pl.pallas_call(
        kernel,
        out_shape=[jax.ShapeDtypeStruct(v.shape, v.dtype) for v in values],
        in_specs=[pl.BlockSpec(memory_space=pl.ANY)] * (count + len(others)),
        out_specs=[pl.BlockSpec(memory_space=pl.ANY)] * count,
        input_output_aliases={i: i for i in range(count)},
        compiler_params=pltpu.CompilerParams(has_side_effects=True),
    )(*values, *others)


def joined_columns(pieces, groups, unit):
    count, rows, columns = pieces.shape
    half = columns // 2
    block = 64

    def kernel(pieces_ref, *out_refs):
        parts = [pieces_ref[rank].astype(F32) for rank in range(count)]
        for side, out_ref in enumerate(out_refs):
            out_ref[...] = jnp.concatenate(
                [
                    parts[rank][:, side * half + p * unit : side * half + (p + 1) * unit]
                    for p in range(groups)
                    for rank in range(count)
                ],
                axis=1,
            )

    shape = jax.ShapeDtypeStruct((rows, count * half), F32)
    return pl.pallas_call(
        kernel,
        grid=(rows // block,),
        out_shape=[shape, shape],
        in_specs=[pl.BlockSpec((count, block, columns), lambda i: (0, i, 0))],
        out_specs=[pl.BlockSpec((block, count * half), lambda i: (i, 0))] * 2,
        compiler_params=pltpu.CompilerParams(vmem_limit_bytes=48 * 1024 * 1024),
    )(pieces)


def padded_rows(value):
    rows = value.shape[-2]
    more = -rows % 16
    return jnp.pad(value, [(0, 0)] * (value.ndim - 2) + [(0, more), (0, 0)])


def local(
    inputs,
    segments,
    routes,
    cotangent,
    attention_gain,
    query_weight,
    latent_weight,
    latent_gain,
    expand_weight,
    output_weight,
    feedforward_gain,
    router_weight,
    shared_gate,
    shared_up,
    shared_down,
    expert_gate,
    expert_up,
    expert_down,
):
    seq_count = lax.axis_size("seq")
    dp_count = lax.axis_size("dp")
    me = lax.axis_index("seq")
    d_rank = lax.axis_index("dp")
    tokens = inputs.shape[1]
    width = inputs.shape[2]
    group = tokens * seq_count
    experts = EXP_DEV * seq_count
    heads_dev = HEADS // seq_count
    score_scale = 1.0 / math.sqrt(QK)
    shard = width // dp_count

    hq = heads_dev * QK
    hkv = heads_dev * (NOPE + VDIM)
    rank_shard = latent_gain.shape[0]
    latent_width = latent_weight.shape[1]
    small = jnp.concatenate(
        [attention_gain, feedforward_gain, latent_gain, router_weight.reshape(-1)]
    )
    fold = shard // rank_shard
    expand_part = lax.dynamic_slice_in_dim(expand_weight, me * hkv, hkv, 1)
    expand_part = (
        expand_part.reshape(rank_shard, fold, hkv // fold).transpose(1, 0, 2).reshape(shard, -1)
    )
    pack = jnp.concatenate(
        [lax.dynamic_slice_in_dim(query_weight, me * hq, hq, 1), expand_part], axis=1
    )
    pack_width = pack.shape[1]
    small_rows = -(-small.shape[0] // (16 * pack_width)) * 16
    small_pack = jnp.pad(small, (0, small_rows * pack_width - small.shape[0]))
    pack = jnp.concatenate([pack, small_pack.reshape(small_rows, pack_width)], axis=0)
    routes_pad = jnp.pad(routes[0], ((0, 0), (0, 128 - TOP))).astype(BF16)

    core = lax.rem(me, 2)

    def half_of(weight):
        rows = weight.shape[0] // 2
        return lax.dynamic_slice_in_dim(weight, core * rows, rows, 0)

    hidden = shared_gate.shape[1]
    unit = hidden // (dp_count * seq_count)
    side = dp_count * unit

    def columns_of(weight):
        return [
            lax.dynamic_slice_in_dim(weight, (p * seq_count + me) * unit, unit, 1)
            for p in range(dp_count)
        ]

    x_all, routes_all, pack, w_latent, w_output, g_all = communicate(
        1,
        [
            GatherSeq(inputs[0]),
            GatherSeq(routes_pad),
            GatherDp(pack),
            GatherDpCores(half_of(latent_weight)),
            GatherDpCores(half_of(output_weight)),
            GatherSeq(cotangent[0]),
        ],
    )
    arrived = routes_all[0, 0, 0] >= 0
    expert_gate, expert_up, expert_down = (
        jnp.where(arrived, weight, jnp.zeros_like(weight))
        for weight in (expert_gate, expert_up, expert_down)
    )
    w_egate = lax.all_gather(expert_gate, "dp", axis=1, tiled=True)
    w_eup = lax.all_gather(expert_up, "dp", axis=1, tiled=True)
    w_edown = lax.all_gather(expert_down, "dp", axis=2, tiled=True)
    g_all = g_all.reshape(group, width)
    x_all = x_all.reshape(group, width)
    w_query = pack[:, :shard, :hq].reshape(width, hq)
    w_latent = w_latent.reshape(width, latent_width)
    w_expand = (
        pack[:, :shard, hq:]
        .reshape(dp_count, fold, rank_shard, hkv // fold)
        .transpose(0, 2, 1, 3)
        .reshape(KV_RANK, hkv)
    )
    small = pack[:, shard:].reshape(dp_count, small_rows * pack_width)
    g_attn = small[:, :shard].reshape(width).astype(F32)
    g_ffn = small[:, shard : 2 * shard].reshape(width).astype(F32)
    g_latent = small[:, 2 * shard : 2 * shard + rank_shard].reshape(KV_RANK).astype(F32)
    w_router = small[:, 2 * shard + rank_shard :][:, : shard * experts].reshape(width, experts)

    routes_all = routes_all.reshape(group, 128)[:, :TOP].astype(jnp.int32)
    positions = jnp.arange(group, dtype=jnp.int32)
    seg_all = segments[0]
    cosine, sine = angles(positions, ROPE)
    my_experts = me * EXP_DEV + jnp.arange(EXP_DEV, dtype=jnp.int32)
    expert_ids = jnp.arange(experts, dtype=jnp.int32)
    hit = jnp.any(routes_all[None] == my_experts[:, None, None], axis=-1).astype(jnp.int32)
    slot = jnp.where(hit == 1, jnp.cumsum(hit, axis=1) - hit, CAP)
    route_hot = jnp.any(routes_all[:, :, None] == expert_ids[None, None, :], axis=1)
    placed = slot[:, None, :] == jnp.arange(CAP, dtype=jnp.int32)[None, :, None]
    dispatch = placed.astype(BF16).reshape(EXP_DEV * CAP, group)

    def own(value):
        return lax.dynamic_slice_in_dim(value, me * tokens, tokens, 0)

    attn_in = normalized_rows(x_all.astype(F32), g_attn).astype(BF16)
    q_raw = dot(attn_in, w_query).reshape(group, heads_dev, QK)
    latent_raw = dot(attn_in, w_latent)
    latent = latent_raw[:, :KV_RANK]
    latent_normed = normalized_rows(latent, g_latent).astype(BF16)
    key_value = dot(latent_normed, w_expand).reshape(group, heads_dev, NOPE + VDIM)
    q_full = jnp.concatenate(
        [q_raw[..., :NOPE], rotate(q_raw[..., NOPE:], cosine[:, None, :], sine[:, None, :])],
        axis=-1,
    ).astype(BF16)
    k_rot = rotate(latent_raw[:, KV_RANK:], cosine, sine)
    k_full = jnp.concatenate(
        [key_value[..., :NOPE], jnp.broadcast_to(k_rot[:, None, :], (group, heads_dev, ROPE))],
        axis=-1,
    ).astype(BF16)
    values = key_value[..., NOPE:].astype(BF16)
    visible = (seg_all[:, None] == seg_all[None, :]) & (seg_all[:, None] >= 0) & (
        positions[None, :] <= positions[:, None]
    ) | (positions[None, :] == positions[:, None])
    scores = jnp.einsum("qhd,khd->hqk", q_full, k_full, preferred_element_type=F32) * score_scale
    scores = jnp.where(visible[None], scores, MASKED)
    row_peak = jnp.max(scores, axis=-1, keepdims=True)
    exponent = jnp.exp(scores - row_peak)
    soft_float = exponent / jnp.sum(exponent, axis=-1, keepdims=True)
    soft = soft_float.astype(BF16)
    head_out = jnp.einsum("hqk,khd->qhd", soft, values, preferred_element_type=F32)
    head_out = head_out.astype(BF16).reshape(seq_count, tokens, heads_dev * VDIM)

    (head_out,) = communicate(2, [ExchangeSeq(head_out)])
    w_output = w_output.reshape(width, width)
    flat_out = jnp.swapaxes(head_out, 0, 1).reshape(tokens, HEADS * VDIM)
    x_float = inputs[0].astype(F32)
    residual = x_float + dot(flat_out, w_output)
    ffn_in = normalized_rows(residual, g_ffn).astype(BF16)

    ffn_all, w_sin, w_sdown = communicate(
        3,
        [
            GatherSeq(ffn_in),
            GatherDp(jnp.concatenate(columns_of(shared_gate) + columns_of(shared_up), axis=1)),
            GatherDp(padded_rows(lax.dynamic_slice_in_dim(shared_down, me * unit, unit, 0))),
        ],
    )
    w_sin = w_sin.reshape(width, 2 * side)
    w_sdown = w_sdown[:, :unit].reshape(side, width)
    ffn_all = ffn_all.reshape(group, width)

    router_probs = jax.nn.softmax(dot(ffn_all, w_router), axis=-1)
    chosen = jnp.where(route_hot, router_probs, 0.0)
    chosen_sum = jnp.sum(chosen, axis=-1, keepdims=True)
    gates = chosen / chosen_sum
    my_gates = lax.dynamic_slice_in_dim(gates.T, me * EXP_DEV, EXP_DEV, 0)
    gate_rows = jnp.sum(jnp.where(placed, my_gates[:, None, :], 0.0), axis=-1)

    side_in = dot(ffn_all, w_sin)
    side_gate, side_up = side_in[:, :side], side_in[:, side:]
    side_act = swiglu(side_gate, side_up).astype(BF16)
    grad_sdown = t_dot(side_act, g_all)
    d_side_act = dot_t(g_all, w_sdown)
    _, side_pull = jax.vjp(swiglu, side_gate, side_up)
    d_side_gate, d_side_up = side_pull(d_side_act)
    d_side = jnp.concatenate([d_side_gate, d_side_up], axis=1).astype(BF16)
    grad_sin = t_dot(ffn_all, d_side)
    dispatch, all_sdown, all_sin = communicate(
        5,
        [
            Pass(dispatch),
            ReduceDpGatherSeq(padded_rows(grad_sdown.astype(BF16).reshape(dp_count, unit, width))),
            ReduceDpGatherSeq(grad_sin.astype(BF16).reshape(dp_count, shard, 2 * side)),
        ],
    )

    out_sgate, out_sup = joined_columns(all_sin, dp_count, unit)
    out_sdown = all_sdown[:, :unit].reshape(hidden // dp_count, width).astype(F32)

    rows_shape = (EXP_DEV, CAP, width)
    expert_in = dot(dispatch, ffn_all).astype(BF16).reshape(rows_shape)
    hidden_gate = jnp.einsum("nmh,nhq->nmq", expert_in, w_egate, preferred_element_type=F32)
    g_rows = dot(dispatch, g_all).astype(BF16).reshape(rows_shape)
    expert_grad = (gate_rows[:, :, None] * g_rows.astype(F32)).astype(BF16)
    hidden_up = jnp.einsum("nmh,nhq->nmq", expert_in, w_eup, preferred_element_type=F32)
    expert_act = swiglu(hidden_gate, hidden_up).astype(BF16)
    grad_edown = jnp.einsum("kcf,kcd->kfd", expert_act, expert_grad, preferred_element_type=F32)
    grad_edown = grad_edown.astype(BF16)
    (g_rows,) = after([g_rows], [grad_edown, out_sgate, out_sup, out_sdown])

    d_act_plain = jnp.einsum("kcd,kfd->kcf", g_rows, w_edown, preferred_element_type=F32)
    d_act_plain = lax.optimization_barrier(d_act_plain)
    d_gate_rows = jnp.sum(expert_act.astype(F32) * d_act_plain, axis=-1)
    _, expert_pull = jax.vjp(swiglu, hidden_gate, hidden_up)
    d_hidden_gate, d_hidden_up = expert_pull(gate_rows[:, :, None] * d_act_plain)
    d_hidden_gate = d_hidden_gate.astype(BF16)
    d_hidden_up = d_hidden_up.astype(BF16)
    grad_egate = jnp.einsum("kcd,kcf->kdf", expert_in, d_hidden_gate, preferred_element_type=F32)
    grad_eup = jnp.einsum("kcd,kcf->kdf", expert_in, d_hidden_up, preferred_element_type=F32)
    grad_egate, grad_eup = grad_egate.astype(BF16), grad_eup.astype(BF16)
    shard_edown = lax.psum_scatter(grad_edown, "dp", scatter_dimension=2, tiled=True).astype(F32)
    shard_egate = lax.psum_scatter(grad_egate, "dp", scatter_dimension=1, tiled=True).astype(F32)
    shard_eup = lax.psum_scatter(grad_eup, "dp", scatter_dimension=1, tiled=True).astype(F32)
    d_hidden_gate, d_hidden_up = after([d_hidden_gate, d_hidden_up], [grad_egate, grad_eup])
    d_expert_in = (
        jnp.einsum("sta,sra->str", d_hidden_gate, w_egate, preferred_element_type=F32)
        + jnp.einsum("sta,sra->str", d_hidden_up, w_eup, preferred_element_type=F32)
    ).astype(BF16)
    d_ffn_partial = dot_t(d_side, w_sin) + t_dot(
        dispatch, d_expert_in.reshape(EXP_DEV * CAP, width)
    )
    d_gate_own = jnp.sum(jnp.where(placed, d_gate_rows[:, :, None], 0.0), axis=1)
    mine_hot = (my_experts[:, None] == expert_ids[None, :]).astype(F32)
    d_gate_wide = jnp.sum(d_gate_own[:, :, None] * mine_hot[:, None, :], axis=0)
    d_gate_high = d_gate_wide.astype(BF16)
    d_gate_low = (d_gate_wide - d_gate_high.astype(F32)).astype(BF16)
    d_gate_pack = jnp.concatenate(
        [d_gate_high, d_gate_low, jnp.zeros((group, 128 - 2 * experts), BF16)], axis=1
    )
    def by_group(rows):
        return jnp.swapaxes(rows.reshape(tokens, dp_count, -1), 0, 1)

    d_ffn, d_gate, left_out, left_latent = communicate(
        6,
        [
            ScatterSeq(d_ffn_partial.astype(BF16).reshape(seq_count, tokens, width)),
            ScatterSeq(d_gate_pack.reshape(seq_count, tokens, 128)),
            ExchangeDp(by_group(flat_out)),
            ExchangeDp(by_group(own(attn_in))),
        ],
    )
    d_gate = d_gate[:, :experts] + d_gate[:, experts : 2 * experts]

    (expert_act,) = after([expert_act], [d_ffn])
    expert_out = jnp.einsum("kcf,kfd->kcd", expert_act, w_edown, preferred_element_type=F32)
    expert_out = expert_out.astype(BF16).astype(F32)
    moe_rows = (gate_rows[:, :, None] * expert_out).astype(BF16).reshape(EXP_DEV * CAP, width)
    ffn_out = (dot(side_act, w_sdown) + t_dot(dispatch, moe_rows)).astype(BF16)

    own_hot = own(route_hot)
    own_probs = own(router_probs)
    own_gates = own(gates)
    d_chosen = (d_gate - jnp.sum(d_gate * own_gates, axis=-1, keepdims=True)) / own(chosen_sum)
    d_probs = jnp.where(own_hot, d_chosen, 0.0)
    d_logits = own_probs * (d_probs - jnp.sum(own_probs * d_probs, axis=-1, keepdims=True))
    grad_router = jnp.einsum("td,te->de", ffn_in.astype(F32), d_logits, precision=HIGHEST)
    d_ffn = d_ffn + jnp.einsum("te,de->td", d_logits, w_router.astype(F32), precision=HIGHEST)

    grad_out = cotangent[0].astype(F32)
    d_resid_part, grad_ffn_gain = norm_backward(residual, g_ffn, d_ffn)
    d_residual = grad_out + d_resid_part
    d_attn = d_residual.astype(BF16)
    d_head = dot_t(d_attn, w_output).astype(BF16)
    d_head = jnp.swapaxes(d_head.reshape(tokens, seq_count, heads_dev * VDIM), 0, 1)
    (head_grad,) = communicate(7, [ExchangeSeq(d_head)])
    head_grad = head_grad.reshape(group, heads_dev, VDIM)

    d_values = jnp.einsum("hqk,qhd->khd", soft, head_grad, preferred_element_type=F32).astype(BF16)
    d_prob = jnp.einsum("qhd,khd->hqk", head_grad, values, preferred_element_type=F32)
    d_score = (
        soft_float * (d_prob - jnp.sum(soft_float * d_prob, axis=-1, keepdims=True))
    ).astype(BF16)
    d_query = jnp.einsum("hqk,khd->qhd", d_score, k_full, preferred_element_type=F32)
    d_query = (d_query * score_scale).astype(BF16).astype(F32)
    d_key = jnp.einsum("hqk,qhd->khd", d_score, q_full, preferred_element_type=F32)
    d_key = (d_key * score_scale).astype(BF16)
    d_q_raw = jnp.concatenate(
        [d_query[..., :NOPE], rotate(d_query[..., NOPE:], cosine[:, None, :], -sine[:, None, :])],
        axis=-1,
    )
    d_q_raw = d_q_raw.astype(BF16).reshape(group, hq)
    d_key_value = jnp.concatenate([d_key[..., :NOPE], d_values], axis=-1).reshape(group, hkv)
    dk_rope = jnp.sum(d_key[..., NOPE:].astype(F32), axis=1)
    latent_pad = -latent_width % 128
    d_latent_part = jnp.concatenate(
        [dot_t(d_key_value, w_expand), dk_rope, jnp.zeros((group, latent_pad), F32)], axis=-1
    ).astype(BF16)
    d_attn_part = dot_t(d_q_raw, w_query).astype(BF16)
    grad_expand = t_dot(latent_normed, d_key_value).astype(BF16)
    grad_query = t_dot(attn_in, d_q_raw).astype(BF16)

    left_out, left_latent = own_first(left_out), own_first(left_latent)
    right_out = background_gather(d_attn)
    right_out, d_attn_part = after([right_out, d_attn_part], [left_out])
    query_pieces = background_pieces(grad_query.reshape(dp_count, shard, hq))
    expand_pieces = background_pieces(grad_expand.reshape(dp_count, rank_shard, hkv))
    d_latent_sum, d_attn_in, moe = communicate(
        8,
        [
            ScatterSeq(d_latent_part.reshape(seq_count, tokens, latent_width + latent_pad)),
            ScatterSeq(d_attn_part.reshape(seq_count, tokens, width)),
            ScatterSeq(ffn_out.reshape(seq_count, tokens, width)),
        ],
        micros=90,
    )
    query_pieces[0], expand_pieces[0] = after([query_pieces[0], expand_pieces[0]], [d_attn_in])
    sum_query, sum_expand = sum_pieces(query_pieces), sum_pieces(expand_pieces)
    d_k_pe = rotate(d_latent_sum[:, KV_RANK:latent_width], own(cosine), -own(sine))
    d_latent, grad_latent_gain = norm_backward(
        own(latent), g_latent, d_latent_sum[:, :KV_RANK]
    )
    d_latent_raw = jnp.concatenate([d_latent, d_k_pe], axis=-1).astype(BF16)
    d_attn_in = d_attn_in + dot_t(d_latent_raw, w_latent)
    d_x_part, grad_attn_gain = norm_backward(x_float, g_attn, d_attn_in)
    grad_inputs = d_residual + d_x_part

    all_tokens = dp_count * tokens
    grad_output = t_dot(left_out.reshape(all_tokens, shard), right_out.reshape(all_tokens, width))
    grad_output = grad_output.astype(BF16).reshape(seq_count, shard // seq_count, width)
    latent_rows = jnp.pad(d_latent_raw, ((0, 0), (0, latent_pad)))

    gains = jnp.concatenate(
        [
            grad_attn_gain.reshape(dp_count, -1),
            grad_ffn_gain.reshape(dp_count, -1),
            grad_latent_gain.reshape(dp_count, -1),
            grad_router.reshape(dp_count, -1),
        ],
        axis=1,
    )
    gain_width = gains.shape[1]
    gain_rows = -(-gain_width // (16 * 128)) * 16
    gains = jnp.pad(gains, ((0, 0), (0, gain_rows * 128 - gain_width)))

    right_latent = background_gather(latent_rows)
    grad_latent = t_dot(
        left_latent.reshape(all_tokens, shard),
        right_latent.reshape(all_tokens, -1)[:, :latent_width],
    ).astype(BF16)
    latent_blocks = jnp.pad(
        grad_latent.reshape(seq_count, shard // seq_count, latent_width),
        ((0, 0), (0, 0), (0, latent_pad)),
    )
    out_output, all_query, all_expand, out_latent, all_gains = communicate(
        9,
        [
            SumSeq(grad_output),
            GatherSeq(sum_query),
            GatherSeq(sum_expand),
            SumSeq(latent_blocks),
            ReduceDpGatherSeq(gains.reshape(dp_count, gain_rows, 128)),
        ],
    )
    layer_out = (residual + moe).astype(BF16)
    out_query = jnp.swapaxes(all_query, 0, 1).reshape(shard, HEADS * QK).astype(F32)
    out_expand = (
        jnp.swapaxes(all_expand, 0, 1).reshape(rank_shard, HEADS * (NOPE + VDIM)).astype(F32)
    )
    out_output = out_output.reshape(shard, width).astype(F32)
    out_latent = out_latent.reshape(shard, -1)[:, :latent_width].astype(F32)

    sums = jnp.sum(all_gains, axis=0).reshape(-1)
    out_attn_gain = sums[:shard]
    out_ffn_gain = sums[shard : 2 * shard]
    out_latent_gain = sums[2 * shard : 2 * shard + rank_shard]
    out_router = sums[2 * shard + rank_shard : gain_width].reshape(shard, experts)

    return (
        layer_out[None],
        grad_inputs[None],
        out_attn_gain,
        out_query,
        out_latent,
        out_latent_gain,
        out_expand,
        out_output,
        out_ffn_gain,
        out_router,
        out_sgate,
        out_sup,
        out_sdown,
        shard_egate,
        shard_eup,
        shard_edown,
    )


def solution(mesh):
    placed = (
        P("dp", "seq", None),
        P("dp", None),
        P("dp", "seq", None),
        P("dp", "seq", None),
        P("dp"),
        P("dp", None),
        P("dp", None),
        P("dp"),
        P("dp", None),
        P("dp", None),
        P("dp"),
        P("dp", None),
        P("dp", None),
        P("dp", None),
        P("dp", None),
        P("seq", "dp", None),
        P("seq", "dp", None),
        P("seq", None, "dp"),
    )
    return jax.shard_map(
        local,
        mesh=mesh,
        in_specs=placed,
        out_specs=(
            P("dp", "seq", None),
            P("dp", "seq", None),
            P("dp"),
            P("dp", None),
            P("dp", None),
            P("dp"),
            P("dp", None),
            P("dp", None),
            P("dp"),
            P("dp", None),
            P("dp", None),
            P("dp", None),
            P("dp", None),
            P("seq", "dp", None),
            P("seq", "dp", None),
            P("seq", None, "dp"),
        ),
        check_vma=False,
    )
```
